256 devices in a mesh: scen: 8 (over y, core), tile: 32 (over z, x).
Axes of the slice: x: 4, y: 4, z: 8, core: 2. Of those that a mesh axis runs over, the one named last changes fastest.
Arguments:
- cotangent: float32 [32, 2, 8, 128, 512], P('scen', None, None, 'tile'), may hold values from -120 to 120
- scenario_ids: int32 [32], P('scen'), may hold values from 0 to 63
- weather: float32 [64, 8], replicated, may hold values from 0 to 2000, as said below
- landuse: int32 [128, 512], P('tile'), may hold values from 0 to 16
- class_diff: float32 [2, 17], replicated, may hold values from 0.5 to 4
- level_scale: float32 [8], replicated, may hold values from 0.6 to 1.6
- emit_profile: float32 [8], replicated, may hold values from 0.1 to 1
- building_cells: int32 [4096, 16], P('tile'), may hold values from 0 to 65535, as said below
Outputs:
- adjoint_state: float32 [32, 2, 8, 128, 512], P('scen', None, None, 'tile')
- control_grad: float32 [2, 4096], P(None, 'tile')
The draws below stay inside these ranges and needn't reach their ends.
Inputs may be any that keep to these rules, and one draw needn't show every extreme that they name: `building_cells`: each building's cells form a 4 by 4 block of surface cells whose x rows lie in [k * 4, (k + 1) * 4) with k = b // 128; building 0 starts at cell 0 and the last building ends at the last cell. `weather`: rates along x and y lie in 100 to 2000, along z in 0.5 to 5, winds in 0 to 10, emission factors in 0.005 to 0.02.
All inputs are finite; a program needn't handle non-finite values.
Results may differ from the reference program's by a relative error of at most 0.0003.
Values sent between devices are 32-bit elements; how exact they have to be, the bound alone decides.
No kernel may reach another device: no remote copies, remote signals or barrier semaphores. Data moves between devices by JAX's collectives and lax.ppermute only.
A program may use at most 128 MiB of HBM per device.

```python
import math
import jax
import jax.numpy as jnp
from jax import lax

CX = 4
NZ = 8
CLASSES = 17
WEATHERS = 64
B_DEV = 128
FOOT = 16
NX = 128
NY = 512
SCEN = 32
BUILD = 4096


def draw_weather(key, part):
    key = jax.random.fold_in(key, 11)
    unit = jax.random.uniform(key, (WEATHERS, 8), jnp.float32)
    lows = jnp.array([100.0, 100.0, 0.5, 0.0, 0.0, 0.0, 0.005, 0.005], jnp.float32)
    highs = jnp.array([2000.0, 2000.0, 5.0, 10.0, 10.0, 10.0, 0.02, 0.02], jnp.float32)
    logged = jnp.exp(jnp.log(jnp.maximum(lows, 0.001)) + unit * (jnp.log(highs) - jnp.log(jnp.maximum(lows, 0.001))))
    linear = lows + unit * (highs - lows)
    column = jnp.arange(8)[None, :]
    is_wind = (column >= 3) & (column <= 5)
    return jnp.where(is_wind, linear, logged).astype(jnp.float32)


def draw_building_cells(key, part):
    key = jax.random.fold_in(key, 23)
    first_key, second_key = jax.random.split(key)
    slab = jnp.arange(BUILD, dtype=jnp.int32) // B_DEV
    x_start = slab * CX + jax.random.randint(first_key, (BUILD,), 0, CX - 3, dtype=jnp.int32)
    y_start = jax.random.randint(second_key, (BUILD,), 0, NY - 3, dtype=jnp.int32)
    x_start = x_start.at[0].set(0).at[BUILD - 1].set(NX - 4)
    y_start = y_start.at[0].set(0).at[BUILD - 1].set(NY - 4)
    offsets = jnp.arange(16, dtype=jnp.int32)
    cells = (x_start[:, None] + offsets[None, :] // 4) * NY + y_start[:, None] + offsets[None, :] % 4
    return cells.astype(jnp.int32)


def with_ends(values, rng, low, largest):
    spot = [jax.random.randint(jax.random.fold_in(rng, axis), (), 0, length) for axis, length in enumerate(values.shape)]
    longest = values.shape.index(max(values.shape))
    neighbour = spot[:longest] + [(spot[longest] + 1) % values.shape[longest]] + spot[longest + 1:]
    return values.at[tuple(spot)].set(low).at[tuple(neighbour)].set(largest)


def block_levels(rng, extent, pieces, low, largest):
    gain = 1.0
    for axis_at, parts in pieces:
        heights = jax.random.uniform(jax.random.fold_in(jax.random.fold_in(rng, 6), axis_at), (parts,), jnp.float32, low / len(pieces), largest / len(pieces))
        gain = gain * jnp.repeat(jnp.exp(heights), extent[axis_at] // parts).reshape((-1,) + (1,) * (len(extent) - 1 - axis_at))
    return gain


def centred(own_key, shape, spread, limit, shards=(), kind=jnp.bfloat16):
    values = spread * jax.random.normal(own_key, shape, jnp.float32)
    if shards:
        values = values * block_levels(own_key, shape, shards, -0.22, 0.18)
    return jnp.clip(values, -limit, limit).astype(kind)


def setup_inputs(seed: int = 0) -> dict:
    streams_of = jax.random.split(jax.random.key(seed), 9)
    return {
        "cotangent": centred(streams_of[0], (SCEN, 2, NZ, NX, NY), 20.0, 120.0, ((0, 8), (3, 32)), jnp.float32),
        "scenario_ids": with_ends(jax.random.randint(streams_of[1], (SCEN,), 0, WEATHERS), jax.random.fold_in(streams_of[1], 1), 0, WEATHERS - 1).astype(jnp.int32),
        "weather": draw_weather(jax.random.fold_in(streams_of[8], 71), 0),
        "landuse": with_ends(jax.random.randint(streams_of[3], (NX, NY), 0, CLASSES), jax.random.fold_in(streams_of[3], 1), 0, CLASSES - 1).astype(jnp.int32),
        "class_diff": jnp.clip(jnp.exp(jax.random.uniform(streams_of[4], (2, CLASSES), jnp.float32, math.log(0.5), math.log(4.0))), 0.5, 4.0),
        "level_scale": jnp.clip(jnp.exp(jax.random.uniform(streams_of[5], (NZ,), jnp.float32, math.log(0.6), math.log(1.6))), 0.6, 1.6),
        "emit_profile": jnp.clip(jnp.exp(jax.random.uniform(streams_of[6], (NZ,), jnp.float32, math.log(0.1), math.log(1.0))), 0.1, 1.0),
        "building_cells": draw_building_cells(jax.random.fold_in(streams_of[8], 71), 0),
    }


def adjoint_lines(cell_diff, rate, wind, axis):
    count = cell_diff.shape[axis]
    widths = [(0, 0)] * cell_diff.ndim
    widths[axis] = (1, 1)
    padded = jnp.pad(cell_diff, widths)
    left = (lax.slice_in_dim(padded, 0, count, axis=axis) + cell_diff) / 2.0
    right = (cell_diff + lax.slice_in_dim(padded, 2, count + 2, axis=axis)) / 2.0
    place = lax.broadcasted_iota(jnp.int32, cell_diff.shape, axis)
    lower = jnp.where(place > 0, -rate * left, 0.0 * left)
    upper = jnp.where(place < count - 1, -(rate * right + wind), 0.0 * right)
    middle = 1.0 + rate * (left + right) + wind
    return (lower, middle, upper)

def solve_along(lower, middle, upper, right_side, axis):
    shape = right_side.shape
    lower = jnp.moveaxis(jnp.broadcast_to(lower, shape), axis, -1)
    middle = jnp.moveaxis(jnp.broadcast_to(middle, shape), axis, -1)
    upper = jnp.moveaxis(jnp.broadcast_to(upper, shape), axis, -1)
    moved = jnp.moveaxis(right_side, axis, -1)[..., None]
    solved = lax.linalg.tridiagonal_solve(lower, middle, upper, moved)[..., 0]
    return jnp.moveaxis(solved, -1, axis)

def reference(cotangent, scenario_ids, weather, landuse, class_diff, level_scale, emit_profile, building_cells):
    table = weather[scenario_ids]
    marks = (landuse[None] == jnp.arange(CLASSES, dtype=jnp.int32)[:, None, None]).astype(jnp.float32)
    surface = jnp.sum(class_diff[:, :, None, None] * marks[None], axis=1)
    cell_diff = surface[:, None] * level_scale[None, :, None, None]

    def one_scenario(pair):
        field, row = pair
        lower, middle, upper = adjoint_lines(cell_diff, row[2], row[5], 1)
        field = solve_along(lower, middle, upper, field, 1)
        lower, middle, upper = adjoint_lines(cell_diff, row[1], row[4], 3)
        field = solve_along(lower, middle, upper, field, 3)
        lower, middle, upper = adjoint_lines(cell_diff, row[0], row[3], 2)
        return solve_along(lower, middle, upper, field, 2)
    adjoint_state = lax.map(one_scenario, (cotangent, table))
    column = jnp.sum(adjoint_state * emit_profile[None, None, :, None, None], axis=2)
    column = column.reshape(column.shape[0], 2, NX * NY)
    picked = jnp.take(column, building_cells.reshape(-1), axis=2)
    per_building = jnp.sum(picked.reshape(column.shape[0], 2, BUILD, FOOT), axis=3)
    control_grad = jnp.sum(per_building * table[:, 6:8, None], axis=0)
    return (adjoint_state, control_grad)
```

```python
import jax
import jax.numpy as jnp
from jax import lax
from jax.experimental import pallas as pl
from jax.experimental.pallas import tpu as pltpu
from jax.sharding import PartitionSpec as P

F32 = jnp.float32
SEND = 24


def inverse(value):
    guess = pl.reciprocal(value, approx=True)
    guess = guess * (2.0 - value * guess)
    return guess * (2.0 - value * guess)


def sublane():
    return lax.broadcasted_iota(jnp.int32, (8, 128), 0)


def lane():
    return lax.broadcasted_iota(jnp.int32, (8, 128), 1)


def choose(index, values):
    out = jnp.full((8, 128), values[-1], F32)
    for at in range(len(values) - 2, -1, -1):
        out = jnp.where(index == at, values[at], out)
    return out


def surface(classes, class_diff, field):
    out = jnp.zeros((8, 128), F32)
    for mark in range(class_diff.shape[1]):
        out = jnp.where(classes == mark, class_diff[field, mark], out)
    return out


def swap_halves(value):
    return pltpu.roll(value, 4, axis=0)


def pair_halves(first, second, low):
    return (
        jnp.where(low, first, swap_halves(second)),
        jnp.where(low, swap_halves(first), second),
    )


def solve_levels(cot, surf, scale, table, out, hold_a, hold_c, low):
    half = [(scale[z] + scale[z + 1]) * 0.5 for z in range(7)]
    for pair in range(2):
        chains = [(s, f, h) for s in (2 * pair, 2 * pair + 1) for f in range(2) for h in range(2)]
        rated = [surf[f][h] * table(s, 2) for s, f, h in chains]
        winds = [table(s, 5) for s, f, h in chains]
        values = [None] * 8
        slacks = [None] * 8
        faces = [None] * 8
        for z in range(8):
            for n, (s, f, h) in enumerate(chains):
                rhs = cot[pl.ds(s * 256 + f * 128 + z * 16 + h * 8, 8), :]
                if z == 0:
                    slack = 1.0 + rated[n] * (scale[0] * 0.5)
                else:
                    slack = 1.0 + faces[n] * slacks[n]
                    rhs = rhs + faces[n] * values[n]
                if z < 7:
                    face = rated[n] * half[z]
                    above = face + winds[n]
                    inv = inverse(above + slack)
                    values[n] = rhs * inv
                    slacks[n] = slack * inv
                    faces[n] = face
                    hold_a[pl.ds((z * 8 + n) * 8, 8), :] = values[n]
                    hold_c[pl.ds((z * 8 + n) * 8, 8), :] = above * inv
                else:
                    slack = slack + (rated[n] * (scale[7] * 0.5) + winds[n])
                    values[n] = rhs * inverse(slack)
        for z in range(7, -1, -1):
            if z < 7:
                for n in range(8):
                    at = pl.ds((z * 8 + n) * 8, 8)
                    values[n] = hold_a[at, :] + hold_c[at, :] * values[n]
            for f in range(2):
                for h in range(2):
                    n = f * 2 + h
                    even, odd = pair_halves(values[n], values[n + 4], low)
                    for yb, item in ((2 * h, even), (2 * h + 1, odd)):
                        out[pl.ds((f * 4 + yb) * 128 + z * 16 + pair * 8, 8), :] = item


def from_before(items, rows, distance):
    turned = [pltpu.roll(item, distance, axis=0) for item in items]
    return [
        turned[v] if v % 4 == 0 else jnp.where(rows < distance, turned[v - 1], turned[v])
        for v in range(8)
    ]


def from_after(items, rows, distance):
    turned = [pltpu.roll(item, 8 - distance, axis=0) for item in items]
    return [
        turned[v] if v % 4 == 3 else jnp.where(rows >= 8 - distance, turned[v + 1], turned[v])
        for v in range(8)
    ]


def solve_chunks(below, above, slack, rhs, rows):
    everyone = range(8)
    for distance in (1, 2, 4, 8, 16):
        inv = [inverse(below[v] + above[v] + slack[v]) for v in everyone]
        nb = [below[v] * inv[v] for v in everyone]
        na = [above[v] * inv[v] for v in everyone]
        ns = [slack[v] * inv[v] for v in everyone]
        nr = [rhs[v] * inv[v] for v in everyone]
        new_slack = list(slack)
        new_rhs = list(rhs)
        if distance < 8:
            pb, ps, pr = (from_before(item, rows, distance) for item in (nb, ns, nr))
            qa, qs, qr = (from_after(item, rows, distance) for item in (na, ns, nr))
            has_before = has_after = [True] * 8
        else:
            jump = distance // 8
            has_before = [v % 4 >= jump for v in everyone]
            has_after = [v % 4 < 4 - jump for v in everyone]
            pb, ps, pr = (
                [item[v - jump] if has_before[v] else None for v in everyone]
                for item in (nb, ns, nr)
            )
            qa, qs, qr = (
                [item[v + jump] if has_after[v] else None for v in everyone]
                for item in (na, ns, nr)
            )
        zero = jnp.zeros((8, 128), F32)
        new_below = [zero] * 8
        new_above = [zero] * 8
        for v in everyone:
            if has_before[v]:
                new_slack[v] = new_slack[v] + below[v] * ps[v]
                new_rhs[v] = new_rhs[v] + below[v] * pr[v]
                new_below[v] = below[v] * pb[v]
            if has_after[v]:
                new_slack[v] = new_slack[v] + above[v] * qs[v]
                new_rhs[v] = new_rhs[v] + above[v] * qr[v]
                new_above[v] = above[v] * qa[v]
        below, above, slack, rhs = new_below, new_above, new_slack, new_rhs
    return [rhs[v] * inverse(slack[v]) for v in everyone]


def solve_rows(turned, faces, leak, rate, wind, hold_a, hold_b, hold_c, rows):
    everyone = range(8)
    depth = 16

    def at(v, i):
        return pl.ds(v * 128 + i, 8, stride=depth)

    def keep(i, v):
        return pl.ds((i * 8 + v) * 8, 8)

    ends = [faces[at(v, depth - 1), :] * rate for v in everyone]
    before = from_before(ends, rows, 1)
    last = ends
    value = [None] * 8
    fill = [None] * 8
    slack = [None] * 8
    for i in range(depth):
        for v in everyone:
            rhs = turned[at(v, i), :]
            face = last[v] if i == depth - 1 else faces[at(v, i), :] * rate
            next_coef = face + wind
            if i == 0:
                link = before[v]
                own = jnp.ones((8, 128), F32)
                if v % 4 == 0:
                    own = jnp.where(rows == 0, 1.0 + leak[v // 4], own)
                    link = jnp.where(rows == 0, 0.0, link)
            else:
                link = before[v] * fill[v]
                own = 1.0 + before[v] * slack[v]
                rhs = rhs + before[v] * value[v]
            if i == depth - 1:
                if v % 4 == 3:
                    own = jnp.where(rows == 7, own + next_coef, own)
                    next_coef = jnp.where(rows == 7, 0.0, next_coef)
                value[v], fill[v], slack[v] = rhs, link, own
                before[v] = next_coef
                continue
            inv = inverse(next_coef + link + own)
            value[v] = rhs * inv
            fill[v] = link * inv
            slack[v] = own * inv
            upper = next_coef * inv
            hold_a[keep(i, v), :] = value[v]
            hold_b[keep(i, v), :] = fill[v]
            hold_c[keep(i, v), :] = upper
            before[v] = face
            if i == 0:
                if v == 0:
                    first_value, first_fill, first_slack, first_next = ([None] * 8 for _ in range(4))
                first_value[v], first_fill[v], first_slack[v], first_next[v] = (
                    value[v],
                    fill[v],
                    slack[v],
                    upper,
                )
            else:
                carry = first_next[v]
                first_value[v] = first_value[v] + carry * value[v]
                first_slack[v] = first_slack[v] + carry * slack[v]
                first_next[v] = carry * upper
    next_value = from_after(first_value, rows, 1)
    next_slack = from_after(first_slack, rows, 1)
    next_next = from_after(first_next, rows, 1)
    above = [before[v] * next_next[v] for v in everyone]
    slack = [slack[v] + before[v] * next_slack[v] for v in everyone]
    rhs = [value[v] + before[v] * next_value[v] for v in everyone]
    current = solve_chunks(fill, above, slack, rhs, rows)
    previous = from_before(current, rows, 1)
    for v in everyone:
        turned[at(v, depth - 1), :] = current[v]
    for i in range(depth - 2, -1, -1):
        for v in everyone:
            item = hold_a[keep(i, v), :] + hold_b[keep(i, v), :] * previous[v]
            current[v] = item + hold_c[keep(i, v), :] * current[v]
            turned[at(v, i), :] = current[v]


def inner_coefs(low_face, mid_face, high_face, wind):
    one_next = mid_face + wind
    one_inv = inverse(low_face + one_next + 1.0)
    one_fill = low_face * one_inv
    one_upper = one_next * one_inv
    two_next = high_face + wind
    two_fill = mid_face * one_fill
    two_slack = 1.0 + mid_face * one_inv
    two_inv = inverse(two_next + two_fill + two_slack)
    return one_inv, one_fill, one_upper, two_inv, two_fill, two_slack, two_next


def first_kernel(
    ids, weather, class_diff, scale, cot, landuse, sent, kept,
    levels, turned, faces, hold_a, hold_b, hold_c, surf_rows,
):
    rows = sublane()
    lanes = lane()
    low = rows < 4

    def table(s, column):
        return weather[ids[s], column]

    classes = [landuse[pl.ds(0, 8), :], landuse[pl.ds(8, 8), :]]
    surf = [[surface(item, class_diff, f) for item in classes] for f in range(2)]
    rate_y = choose((lanes // 4) % 4, [table(s, 1) for s in range(4)])
    wind_y = choose((lanes // 4) % 4, [table(s, 4) for s in range(4)])
    rate_y = rate_y * choose(lanes // 16, [scale[z] for z in range(8)])
    leak = []
    for f in range(2):
        upper, lower = surf[f]
        surf_rows[pl.ds(f * 16, 8), :] = upper
        surf_rows[pl.ds(f * 16 + 8, 8), :] = lower
        shifted = [pltpu.roll(item, 127, axis=1) for item in (upper, lower)]
        swapped = [swap_halves(item) for item in shifted]
        onward = [
            jnp.where(low, swapped[0], swapped[1]),
            jnp.where(low, swapped[1], 0.0),
        ]
        for h in range(2):
            right = jnp.where(lanes == 127, onward[h], shifted[h])
            face = (surf[f][h] + right) * 0.5
            other = swap_halves(face)
            for yb, item in (
                (2 * h, jnp.where(low, face, other)),
                (2 * h + 1, jnp.where(low, other, face)),
            ):
                tile = jnp.concatenate([item] * 16, axis=0)
                faces[pl.ds((f * 4 + yb) * 128, 128), :] = tile.T
        start = jnp.broadcast_to(upper[:, 0:1], (8, 128))
        start = jnp.where(rows == lanes % 4, start, 0.0)
        start = jnp.broadcast_to(jnp.sum(start, axis=0, keepdims=True), (8, 128))
        leak.append(start * 0.5 * rate_y)

    solve_levels(cot, surf, scale, table, levels, hold_a, hold_c, low)
    for v in range(8):
        block = pl.ds(v * 128, 128)
        turned[block, :] = levels[block, :].T
    solve_rows(turned, faces, leak, rate_y, wind_y, hold_a, hold_b, hold_c, rows)
    for v in range(8):
        block = pl.ds(v * 128, 128)
        levels[block, :] = turned[block, :].T

    rate_x = choose(rows % 4, [table(s, 0) for s in range(4)])
    wind_x = choose(rows % 4, [table(s, 3) for s in range(4)])
    for v in range(8):
        line = [surf_rows[pl.ds(v * 4 + x, 1), :] for x in range(4)]
        steps = [(line[x] + line[x + 1]) * 0.5 for x in range(3)]
        four = surf_rows[pl.ds((v // 2) * 8, 8), :]
        for zp in range(4):
            j = v * 4 + zp
            rate = rate_x * choose(rows // 4, [scale[2 * zp], scale[2 * zp + 1]])
            e01, e12, e23 = (rate * step for step in steps)
            rhs = [levels[pl.ds(v * 128 + zp * 32 + x, 8, stride=4), :] for x in range(4)]
            one_inv, one_fill, one_upper, two_inv, two_fill, two_slack, two_next = inner_coefs(
                e01, e12, e23, wind_x
            )
            one = rhs[1] * one_inv
            two = (rhs[2] + e12 * one) * two_inv
            sent[j, pl.ds(0, 8), :] = rhs[0] + (e01 + wind_x) * (one + one_upper * two)
            sent[j, pl.ds(8, 8), :] = rhs[3] + e23 * two
            sent[j, pl.ds(16, 8), :] = four if v % 2 == 0 else swap_halves(four)
            for n, item in enumerate(
                (one, one_fill, one_upper, two, two_fill * two_inv, two_next * two_inv)
            ):
                kept[j, pl.ds(n * 8, 8), :] = item


def middle_kernel(place, ids, weather, scale, got, ends):
    rows = sublane()

    def table(s, column):
        return weather[ids[s], column]

    rate = choose(rows % 4, [table(s, 0) for s in range(4)])
    wind = choose(rows % 4, [table(s, 3) for s in range(4)])
    zp = place[0] % 4
    rate = rate * choose(rows // 4, [scale[2 * zp], scale[2 * zp + 1]])
    slabs = got.shape[0]
    below, above, slack, rhs = [], [], [], []
    line = None
    outer = None
    for k in range(slabs):
        line = [got[k, pl.ds(16 + x, 1), :] for x in range(4)]
        if k == 0:
            outer = rate * (line[0] * 0.5)
        e01, e12, e23 = (rate * ((line[x] + line[x + 1]) * 0.5) for x in range(3))
        one_inv, one_fill, one_upper, two_inv, two_fill, two_slack, two_next = inner_coefs(
            e01, e12, e23, wind
        )
        two_slack = two_slack * two_inv
        q0 = e01 + wind
        own = 1.0 + q0 * (one_inv + one_upper * two_slack)
        if k == 0:
            own = own + outer
            below.append(None)
        else:
            below.append(outer)
        above.append(q0 * (one_upper * (two_next * two_inv)))
        slack.append(own)
        rhs.append(got[k, pl.ds(0, 8), :])
        if k < slabs - 1:
            outer = rate * ((line[3] + got[k + 1, pl.ds(16, 1), :]) * 0.5)
        else:
            outer = rate * (line[3] * 0.5)
        own = 1.0 + e23 * two_slack
        below.append(e23 * (two_fill * two_inv))
        if k < slabs - 1:
            above.append(outer + wind)
        else:
            own = own + (outer + wind)
            above.append(None)
        slack.append(own)
        rhs.append(got[k, pl.ds(8, 8), :])

    def total(i):
        out = slack[i]
        if below[i] is not None:
            out = out + below[i]
        if above[i] is not None:
            out = out + above[i]
        return out

    count = 2 * slabs
    alive = list(range(count))
    removed = []
    while len(alive) > 1:
        gone = alive[1::2]
        stay = alive[0::2]
        normal = {}
        for i in gone:
            inv = inverse(total(i))
            normal[i] = (
                below[i] * inv,
                None if above[i] is None else above[i] * inv,
                slack[i] * inv,
                rhs[i] * inv,
            )
        for n, i in enumerate(stay):
            new_below = new_above = None
            new_slack, new_rhs = slack[i], rhs[i]
            if n > 0:
                nb, na, ns, nr = normal[gone[n - 1]]
                new_slack = new_slack + below[i] * ns
                new_rhs = new_rhs + below[i] * nr
                new_below = below[i] * nb
            if n < len(gone):
                nb, na, ns, nr = normal[gone[n]]
                new_slack = new_slack + above[i] * ns
                new_rhs = new_rhs + above[i] * nr
                new_above = None if na is None else above[i] * na
            below[i], above[i], slack[i], rhs[i] = new_below, new_above, new_slack, new_rhs
        removed.append((alive, normal))
        alive = stay
    solved = {0: rhs[0] * inverse(slack[0])}
    for order, normal in reversed(removed):
        for n in range(1, len(order), 2):
            nb, na, ns, nr = normal[order[n]]
            item = nr + nb * solved[order[n - 1]]
            if na is not None:
                item = item + na * solved[order[n + 1]]
            solved[order[n]] = item
    for k in range(slabs):
        ends[k, pl.ds(0, 8), :] = solved[2 * k]
        ends[k, pl.ds(8, 8), :] = solved[2 * k + 1]


def last_kernel(ids, weather, scale_emit, ends, kept, cells, state, grad, lines):
    rows = sublane()
    low = rows < 4

    def table(s, column):
        return weather[ids[s], column]

    parts = []
    for f in range(2):
        factor = choose(rows % 4, [table(s, 6 + f) for s in range(4)])
        for yb in range(4):
            v = f * 4 + yb
            total = None
            for zp in range(4):
                j = v * 4 + zp
                weight = factor * choose(rows // 4, [scale_emit[2 * zp], scale_emit[2 * zp + 1]])
                first = ends[j, pl.ds(0, 8), :]
                last = ends[j, pl.ds(8, 8), :]
                a1, b1, c1, a2, b2, c2 = (kept[j, pl.ds(n * 8, 8), :] for n in range(6))
                two = a2 + b2 * first + c2 * last
                one = a1 + b1 * first + c1 * two
                for x, item in enumerate((first, one, two, last)):
                    lines[pl.ds(v * 128 + zp * 32 + x, 8, stride=4), :] = item
                item = weight * ((first + one) + (two + last))
                total = item if total is None else total + item
            parts.append(jnp.sum(total, axis=0, keepdims=True))
        for z in range(8):
            for sp in range(2):
                for h in range(2):
                    base = (f * 4 + 2 * h) * 128 + z * 16 + sp * 8
                    even, odd = pair_halves(
                        lines[pl.ds(base, 8), :], lines[pl.ds(base + 128, 8), :], low
                    )
                    for s, item in ((2 * sp, even), (2 * sp + 1, odd)):
                        state[pl.ds(s * 256 + f * 128 + z * 16 + h * 8, 8), :] = item
    width = 512
    start = jnp.min(cells[...] % width, axis=1, keepdims=True)
    place = lax.broadcasted_iota(jnp.int32, (128, width), 1)
    window = jnp.where((place >= start) & (place < start + 4), 1.0, 0.0).astype(jnp.bfloat16)
    sums = [jnp.concatenate(parts[f * 4 : f * 4 + 4], axis=1) for f in range(2)]
    sums = jnp.concatenate(sums + [jnp.zeros((6, width), F32)], axis=0)
    picked = jnp.zeros((8, 128), F32)
    for _ in range(3):
        piece = sums.astype(jnp.bfloat16)
        sums = sums - piece.astype(F32)
        picked = picked + lax.dot_general(
            piece, window, (((1,), (1,)), ((), ())), preferred_element_type=F32
        )
    grad[...] = picked[0:2, :]


def rows_of(block):
    s, f, z, x, y = block.shape
    return block.reshape(s, f, z, x, y // 128, 128).transpose(0, 1, 2, 4, 3, 5).reshape(-1, 128)


def on_device(
    cotangent, scenario_ids, weather, landuse, class_diff, level_scale, emit_profile, building_cells
):
    smem = pl.BlockSpec(memory_space=pltpu.SMEM)
    vmem = pl.BlockSpec(memory_space=pltpu.VMEM)
    params = pltpu.CompilerParams(vmem_limit_bytes=32 * 1024 * 1024)
    slabs = lax.axis_size("tile")
    cot = rows_of(cotangent)
    classes = landuse.reshape(4, 4, 128).transpose(1, 0, 2).reshape(16, 128)
    sent, kept = pl.pallas_call(
        first_kernel,
        out_shape=(
            jax.ShapeDtypeStruct((slabs, SEND, 128), F32),
            jax.ShapeDtypeStruct((slabs, 48, 128), F32),
        ),
        in_specs=[smem] * 4 + [vmem] * 2,
        out_specs=(vmem, vmem),
        scratch_shapes=[pltpu.VMEM((1024, 128), F32)] * 6 + [pltpu.VMEM((32, 128), F32)],
        compiler_params=params,
    )(scenario_ids, weather, class_diff, level_scale, cot, classes)
    got = lax.all_to_all(sent, "tile", 0, 0)
    place = lax.axis_index("tile").astype(jnp.int32).reshape(1)
    ends = pl.pallas_call(
        middle_kernel,
        out_shape=jax.ShapeDtypeStruct((slabs, 16, 128), F32),
        in_specs=[smem] * 4 + [vmem],
        out_specs=vmem,
        compiler_params=params,
    )(place, scenario_ids, weather, level_scale, got)
    ends = lax.all_to_all(ends, "tile", 0, 0)
    state, grad = pl.pallas_call(
        last_kernel,
        out_shape=(
            jax.ShapeDtypeStruct((1024, 128), F32),
            jax.ShapeDtypeStruct((2, 128), F32),
        ),
        in_specs=[smem] * 3 + [vmem] * 3,
        out_specs=(vmem, vmem),
        scratch_shapes=[pltpu.VMEM((1024, 128), F32)],
        compiler_params=params,
    )(scenario_ids, weather, emit_profile, ends, kept, building_cells)
    state = state.reshape(4, 2, 8, 4, 4, 128).transpose(0, 1, 2, 4, 3, 5).reshape(cotangent.shape)
    grad = grad + lax.ppermute(grad, "scen", [(i, i ^ 1) for i in range(8)])
    grad = grad + sum(
        lax.ppermute(grad, "scen", [(i, (i + step) % 8) for i in range(8)]) for step in (2, 4, 6)
    )
    return (state, grad)


def solution(mesh):
    placed = (
        P("scen", None, None, "tile", None),
        P("scen"),
        P(),
        P("tile", None),
        P(),
        P(),
        P(),
        P("tile", None),
    )
    return jax.shard_map(
        on_device,
        mesh=mesh,
        in_specs=placed,
        out_specs=(P("scen", None, None, "tile", None), P(None, "tile")),
        check_vma=False,
    )
```

```python
import jax
import jax.numpy as jnp
from jax import lax
from jax.experimental import pallas as pl
from jax.experimental.pallas import tpu as pltpu
from jax.sharding import PartitionSpec as P

F32 = jnp.float32
SEND = 24


def inverse(value):
    guess = pl.reciprocal(value, approx=True)
    guess = guess * (2.0 - value * guess)
    return guess * (2.0 - value * guess)


def sublane():
    return lax.broadcasted_iota(jnp.int32, (8, 128), 0)


def lane():
    return lax.broadcasted_iota(jnp.int32, (8, 128), 1)


def choose(index, values):
    out = jnp.full((8, 128), values[-1], F32)
    for at in range(len(values) - 2, -1, -1):
        out = jnp.where(index == at, values[at], out)
    return out


def surface(classes, class_diff, field):
    out = jnp.zeros((8, 128), F32)
    for mark in range(class_diff.shape[1]):
        out = jnp.where(classes == mark, class_diff[field, mark], out)
    return out


def swap_halves(value):
    return pltpu.roll(value, 4, axis=0)


def pair_halves(first, second, low):
    return (
        jnp.where(low, first, swap_halves(second)),
        jnp.where(low, swap_halves(first), second),
    )


def solve_levels(cot, surf, scale, table, out, hold_a, hold_c, low, arrivals):
    half = [(scale[z] + scale[z + 1]) * 0.5 for z in range(7)]
    for pair in range(2):
        arrivals[pair].wait()
        chains = [(s, f, h) for s in (2 * pair, 2 * pair + 1) for f in range(2) for h in range(2)]
        rated = [surf[f][h] * table(s, 2) for s, f, h in chains]
        winds = [table(s, 5) for s, f, h in chains]
        values = [None] * 8
        slacks = [None] * 8
        faces = [None] * 8
        for z in range(8):
            for n, (s, f, h) in enumerate(chains):
                rhs = cot[pl.ds(s * 256 + f * 128 + z * 16 + h * 8, 8), :]
                if z == 0:
                    slack = 1.0 + rated[n] * (scale[0] * 0.5)
                else:
                    slack = 1.0 + faces[n] * slacks[n]
                    rhs = rhs + faces[n] * values[n]
                if z < 7:
                    face = rated[n] * half[z]
                    above = face + winds[n]
                    inv = inverse(above + slack)
                    values[n] = rhs * inv
                    slacks[n] = slack * inv
                    faces[n] = face
                    hold_a[pl.ds((z * 8 + n) * 8, 8), :] = values[n]
                    hold_c[pl.ds((z * 8 + n) * 8, 8), :] = above * inv
                else:
                    slack = slack + (rated[n] * (scale[7] * 0.5) + winds[n])
                    values[n] = rhs * inverse(slack)
        for z in range(7, -1, -1):
            if z < 7:
                for n in range(8):
                    at = pl.ds((z * 8 + n) * 8, 8)
                    values[n] = hold_a[at, :] + hold_c[at, :] * values[n]
            for f in range(2):
                for h in range(2):
                    n = f * 2 + h
                    even, odd = pair_halves(values[n], values[n + 4], low)
                    for yb, item in ((2 * h, even), (2 * h + 1, odd)):
                        out[pl.ds((f * 4 + yb) * 128 + z * 16 + pair * 8, 8), :] = item


def from_before(items, rows, distance):
    turned = [pltpu.roll(item, distance, axis=0) for item in items]
    return [
        turned[v] if v % 4 == 0 else jnp.where(rows < distance, turned[v - 1], turned[v])
        for v in range(8)
    ]


def from_after(items, rows, distance):
    turned = [pltpu.roll(item, 8 - distance, axis=0) for item in items]
    return [
        turned[v] if v % 4 == 3 else jnp.where(rows >= 8 - distance, turned[v + 1], turned[v])
        for v in range(8)
    ]


def solve_chunks(below, above, slack, rhs, rows):
    everyone = range(8)
    for distance in (1, 2, 4, 8, 16):
        inv = [inverse(below[v] + above[v] + slack[v]) for v in everyone]
        nb = [below[v] * inv[v] for v in everyone]
        na = [above[v] * inv[v] for v in everyone]
        ns = [slack[v] * inv[v] for v in everyone]
        nr = [rhs[v] * inv[v] for v in everyone]
        new_slack = list(slack)
        new_rhs = list(rhs)
        if distance < 8:
            pb, ps, pr = (from_before(item, rows, distance) for item in (nb, ns, nr))
            qa, qs, qr = (from_after(item, rows, distance) for item in (na, ns, nr))
            has_before = has_after = [True] * 8
        else:
            jump = distance // 8
            has_before = [v % 4 >= jump for v in everyone]
            has_after = [v % 4 < 4 - jump for v in everyone]
            pb, ps, pr = (
                [item[v - jump] if has_before[v] else None for v in everyone]
                for item in (nb, ns, nr)
            )
            qa, qs, qr = (
                [item[v + jump] if has_after[v] else None for v in everyone]
                for item in (na, ns, nr)
            )
        zero = jnp.zeros((8, 128), F32)
        new_below = [zero] * 8
        new_above = [zero] * 8
        for v in everyone:
            if has_before[v]:
                new_slack[v] = new_slack[v] + below[v] * ps[v]
                new_rhs[v] = new_rhs[v] + below[v] * pr[v]
                new_below[v] = below[v] * pb[v]
            if has_after[v]:
                new_slack[v] = new_slack[v] + above[v] * qs[v]
                new_rhs[v] = new_rhs[v] + above[v] * qr[v]
                new_above[v] = above[v] * qa[v]
        below, above, slack, rhs = new_below, new_above, new_slack, new_rhs
    return [rhs[v] * inverse(slack[v]) for v in everyone]


def solve_rows(turned, faces, leak, rate, wind, hold_a, hold_b, hold_c, rows):
    everyone = range(8)
    depth = 16

    def at(v, i):
        return pl.ds(v * 128 + i, 8, stride=depth)

    def keep(i, v):
        return pl.ds((i * 8 + v) * 8, 8)

    ends = [faces[at(v, depth - 1), :] * rate for v in everyone]
    before = from_before(ends, rows, 1)
    last = ends
    value = [None] * 8
    fill = [None] * 8
    slack = [None] * 8
    for i in range(depth):
        for v in everyone:
            rhs = turned[at(v, i), :]
            face = last[v] if i == depth - 1 else faces[at(v, i), :] * rate
            next_coef = face + wind
            if i == 0:
                link = before[v]
                own = jnp.ones((8, 128), F32)
                if v % 4 == 0:
                    own = jnp.where(rows == 0, 1.0 + leak[v // 4], own)
                    link = jnp.where(rows == 0, 0.0, link)
            else:
                link = before[v] * fill[v]
                own = 1.0 + before[v] * slack[v]
                rhs = rhs + before[v] * value[v]
            if i == depth - 1:
                if v % 4 == 3:
                    own = jnp.where(rows == 7, own + next_coef, own)
                    next_coef = jnp.where(rows == 7, 0.0, next_coef)
                value[v], fill[v], slack[v] = rhs, link, own
                before[v] = next_coef
                continue
            inv = inverse(next_coef + link + own)
            value[v] = rhs * inv
            fill[v] = link * inv
            slack[v] = own * inv
            upper = next_coef * inv
            hold_a[keep(i, v), :] = value[v]
            hold_b[keep(i, v), :] = fill[v]
            hold_c[keep(i, v), :] = upper
            before[v] = face
            if i == 0:
                if v == 0:
                    first_value, first_fill, first_slack, first_next = ([None] * 8 for _ in range(4))
                first_value[v], first_fill[v], first_slack[v], first_next[v] = (
                    value[v],
                    fill[v],
                    slack[v],
                    upper,
                )
            else:
                carry = first_next[v]
                first_value[v] = first_value[v] + carry * value[v]
                first_slack[v] = first_slack[v] + carry * slack[v]
                first_next[v] = carry * upper
    next_value = from_after(first_value, rows, 1)
    next_slack = from_after(first_slack, rows, 1)
    next_next = from_after(first_next, rows, 1)
    above = [before[v] * next_next[v] for v in everyone]
    slack = [slack[v] + before[v] * next_slack[v] for v in everyone]
    rhs = [value[v] + before[v] * next_value[v] for v in everyone]
    current = solve_chunks(fill, above, slack, rhs, rows)
    previous = from_before(current, rows, 1)
    for v in everyone:
        turned[at(v, depth - 1), :] = current[v]
    for i in range(depth - 2, -1, -1):
        for v in everyone:
            item = hold_a[keep(i, v), :] + hold_b[keep(i, v), :] * previous[v]
            current[v] = item + hold_c[keep(i, v), :] * current[v]
            turned[at(v, i), :] = current[v]


def inner_coefs(low_face, mid_face, high_face, wind):
    one_next = mid_face + wind
    one_inv = inverse(low_face + one_next + 1.0)
    one_fill = low_face * one_inv
    one_upper = one_next * one_inv
    two_next = high_face + wind
    two_fill = mid_face * one_fill
    two_slack = 1.0 + mid_face * one_inv
    two_inv = inverse(two_next + two_fill + two_slack)
    return one_inv, one_fill, one_upper, two_inv, two_fill, two_slack, two_next


def first_kernel(
    ids_in, weather_in, class_diff_in, scale_in, emit_in, landuse_in, cells_in, cot_in,
    sent, kept, vectors, window,
    ids, weather, class_diff, scale, emit, landuse, cells, cot,
    levels, turned, faces, hold_a, hold_b, hold_c, surf_rows, done,
):
    small = [
        pltpu.make_async_copy(source, target, done.at[n])
        for n, (source, target) in enumerate(
            (
                (ids_in, ids),
                (weather_in, weather),
                (class_diff_in, class_diff),
                (scale_in, scale),
                (emit_in, emit),
                (landuse_in, landuse),
                (cells_in, cells),
            )
        )
    ]
    halves = [
        pltpu.make_async_copy(
            cot_in.at[pl.ds(n * 512, 512), :], cot.at[pl.ds(n * 512, 512), :], done.at[7 + n]
        )
        for n in range(2)
    ]
    for copy in small + halves:
        copy.start()
    for copy in small:
        copy.wait()
    rows = sublane()
    lanes = lane()
    low = rows < 4

    def table(s, column):
        return weather[column, ids[s]]

    classes = [landuse[pl.ds(0, 8), :], landuse[pl.ds(8, 8), :]]
    surf = [[surface(item, class_diff, f) for item in classes] for f in range(2)]
    rate_y = choose((lanes // 4) % 4, [table(s, 1) for s in range(4)])
    wind_y = choose((lanes // 4) % 4, [table(s, 4) for s in range(4)])
    rate_y = rate_y * choose(lanes // 16, [scale[z] for z in range(8)])
    leak = []
    for f in range(2):
        upper, lower = surf[f]
        surf_rows[pl.ds(f * 16, 8), :] = upper
        surf_rows[pl.ds(f * 16 + 8, 8), :] = lower
        shifted = [pltpu.roll(item, 127, axis=1) for item in (upper, lower)]
        swapped = [swap_halves(item) for item in shifted]
        onward = [
            jnp.where(low, swapped[0], swapped[1]),
            jnp.where(low, swapped[1], 0.0),
        ]
        for h in range(2):
            right = jnp.where(lanes == 127, onward[h], shifted[h])
            face = (surf[f][h] + right) * 0.5
            other = swap_halves(face)
            for yb, item in (
                (2 * h, jnp.where(low, face, other)),
                (2 * h + 1, jnp.where(low, other, face)),
            ):
                tile = jnp.concatenate([item] * 16, axis=0)
                faces[pl.ds((f * 4 + yb) * 128, 128), :] = tile.T
        start = jnp.broadcast_to(upper[:, 0:1], (8, 128))
        start = jnp.where(rows == lanes % 4, start, 0.0)
        start = jnp.broadcast_to(jnp.sum(start, axis=0, keepdims=True), (8, 128))
        leak.append(start * 0.5 * rate_y)

    rate_x = choose(rows % 4, [table(s, 0) for s in range(4)])
    wind_x = choose(rows % 4, [table(s, 3) for s in range(4)])
    vectors[0] = rate_x
    vectors[1] = wind_x
    for f in range(2):
        factor = choose(rows % 4, [table(s, 6 + f) for s in range(4)])
        for zp in range(4):
            vectors[2 + f * 4 + zp] = factor * choose(rows // 4, [emit[2 * zp], emit[2 * zp + 1]])
    scales = [choose(rows // 4, [scale[2 * zp], scale[2 * zp + 1]]) for zp in range(4)]
    for v in range(8):
        line = [surf_rows[pl.ds(v * 4 + x, 1), :] for x in range(4)]
        steps = [(line[x] + line[x + 1]) * 0.5 for x in range(3)]
        four = surf_rows[pl.ds((v // 2) * 8, 8), :]
        four = four if v % 2 == 0 else swap_halves(four)
        for zp in range(4):
            j = v * 4 + zp
            rate = rate_x * scales[zp]
            one_inv, one_fill, one_upper, two_inv, two_fill, two_slack, two_next = inner_coefs(
                *(rate * step for step in steps), wind_x
            )
            for n, item in enumerate(
                (one_inv, one_fill, one_upper, two_inv, two_fill * two_inv, two_next * two_inv)
            ):
                kept[j, pl.ds(n * 8, 8), :] = item
            tail = jnp.where(rows == 4, scale[2 * zp], scale[2 * zp + 1])
            sent[j, pl.ds(16, 8), :] = jnp.where(low, four, tail)
    width = window.shape[0]
    start = jnp.min(cells[...] % width, axis=0, keepdims=True)
    place = lax.broadcasted_iota(jnp.int32, (width, 128), 0)
    window[...] = jnp.where((place >= start) & (place < start + 4), 1.0, 0.0).astype(jnp.bfloat16)

    solve_levels(cot, surf, scale, table, levels, hold_a, hold_c, low, halves)
    for v in range(8):
        block = pl.ds(v * 128, 128)
        turned[block, :] = levels[block, :].T
    solve_rows(turned, faces, leak, rate_y, wind_y, hold_a, hold_b, hold_c, rows)
    for v in range(8):
        block = pl.ds(v * 128, 128)
        levels[block, :] = turned[block, :].T

    for v in range(8):
        line = [surf_rows[pl.ds(v * 4 + x, 1), :] for x in range(4)]
        steps = [(line[x] + line[x + 1]) * 0.5 for x in range(3)]
        for zp in range(4):
            j = v * 4 + zp
            rate = rate_x * scales[zp]
            e01, e12, e23 = (rate * step for step in steps)
            rhs = [levels[pl.ds(v * 128 + zp * 32 + x, 8, stride=4), :] for x in range(4)]
            one = rhs[1] * kept[j, pl.ds(0, 8), :]
            two = (rhs[2] + e12 * one) * kept[j, pl.ds(24, 8), :]
            one_upper = kept[j, pl.ds(16, 8), :]
            sent[j, pl.ds(0, 8), :] = rhs[0] + (e01 + wind_x) * (one + one_upper * two)
            sent[j, pl.ds(8, 8), :] = rhs[3] + e23 * two
            kept[j, pl.ds(0, 8), :] = one
            kept[j, pl.ds(24, 8), :] = two


def middle_kernel(vectors, got, ends):
    rows = sublane()
    scale = jnp.where(rows < 4, got[0, pl.ds(20, 1), :], got[0, pl.ds(21, 1), :])
    rate = vectors[0] * scale
    wind = vectors[1]
    slabs = got.shape[0]
    below, above, slack, rhs = [], [], [], []
    line = None
    outer = None
    for k in range(slabs):
        line = [got[k, pl.ds(16 + x, 1), :] for x in range(4)]
        if k == 0:
            outer = rate * (line[0] * 0.5)
        e01, e12, e23 = (rate * ((line[x] + line[x + 1]) * 0.5) for x in range(3))
        one_inv, one_fill, one_upper, two_inv, two_fill, two_slack, two_next = inner_coefs(
            e01, e12, e23, wind
        )
        two_slack = two_slack * two_inv
        q0 = e01 + wind
        own = 1.0 + q0 * (one_inv + one_upper * two_slack)
        if k == 0:
            own = own + outer
            below.append(None)
        else:
            below.append(outer)
        above.append(q0 * (one_upper * (two_next * two_inv)))
        slack.append(own)
        rhs.append(got[k, pl.ds(0, 8), :])
        if k < slabs - 1:
            outer = rate * ((line[3] + got[k + 1, pl.ds(16, 1), :]) * 0.5)
        else:
            outer = rate * (line[3] * 0.5)
        own = 1.0 + e23 * two_slack
        below.append(e23 * (two_fill * two_inv))
        if k < slabs - 1:
            above.append(outer + wind)
        else:
            own = own + (outer + wind)
            above.append(None)
        slack.append(own)
        rhs.append(got[k, pl.ds(8, 8), :])

    def total(i):
        out = slack[i]
        if below[i] is not None:
            out = out + below[i]
        if above[i] is not None:
            out = out + above[i]
        return out

    count = 2 * slabs
    alive = list(range(count))
    removed = []
    while len(alive) > 1:
        gone = alive[1::2]
        stay = alive[0::2]
        normal = {}
        for i in gone:
            inv = inverse(total(i))
            normal[i] = (
                below[i] * inv,
                None if above[i] is None else above[i] * inv,
                slack[i] * inv,
                rhs[i] * inv,
            )
        for n, i in enumerate(stay):
            new_below = new_above = None
            new_slack, new_rhs = slack[i], rhs[i]
            if n > 0:
                nb, na, ns, nr = normal[gone[n - 1]]
                new_slack = new_slack + below[i] * ns
                new_rhs = new_rhs + below[i] * nr
                new_below = below[i] * nb
            if n < len(gone):
                nb, na, ns, nr = normal[gone[n]]
                new_slack = new_slack + above[i] * ns
                new_rhs = new_rhs + above[i] * nr
                new_above = None if na is None else above[i] * na
            below[i], above[i], slack[i], rhs[i] = new_below, new_above, new_slack, new_rhs
        removed.append((alive, normal))
        alive = stay
    solved = {0: rhs[0] * inverse(slack[0])}
    for order, normal in reversed(removed):
        for n in range(1, len(order), 2):
            nb, na, ns, nr = normal[order[n]]
            item = nr + nb * solved[order[n - 1]]
            if na is not None:
                item = item + na * solved[order[n + 1]]
            solved[order[n]] = item
    for k in range(slabs):
        ends[k, pl.ds(0, 8), :] = solved[2 * k]
        ends[k, pl.ds(8, 8), :] = solved[2 * k + 1]


def inner_rows(ends, kept, j):
    first = ends[j, pl.ds(0, 8), :]
    last = ends[j, pl.ds(8, 8), :]
    a1, b1, c1, a2, b2, c2 = (kept[j, pl.ds(n * 8, 8), :] for n in range(6))
    two = a2 + b2 * first + c2 * last
    one = a1 + b1 * first + c1 * two
    return first, one, two, last


def sums_kernel(vectors, window, ends, kept, grad):
    parts = []
    for v in range(8):
        total = None
        for zp in range(4):
            first, one, two, last = inner_rows(ends, kept, v * 4 + zp)
            item = vectors[2 + (v // 4) * 4 + zp] * ((first + one) + (two + last))
            total = item if total is None else total + item
        parts.append(jnp.sum(total, axis=0, keepdims=True))
    sums = [jnp.concatenate(parts[f * 4 : f * 4 + 4], axis=1) for f in range(2)]
    pieces = []
    for _ in range(3):
        piece = [item.astype(jnp.bfloat16).astype(F32) for item in sums]
        sums = [item - cut for item, cut in zip(sums, piece)]
        pieces += piece
    pieces = jnp.concatenate(pieces + [jnp.zeros((2, sums[0].shape[1]), F32)], axis=0)
    picked = jnp.dot(pieces.astype(jnp.bfloat16), window[...], preferred_element_type=F32)
    grad[...] = (picked[0:2, :] + picked[2:4, :]) + picked[4:6, :]


def state_kernel(ends, kept, state, lines):
    low = sublane() < 4
    for f in range(2):
        for yb in range(4):
            v = f * 4 + yb
            for zp in range(4):
                for x, item in enumerate(inner_rows(ends, kept, v * 4 + zp)):
                    lines[pl.ds(v * 128 + zp * 32 + x, 8, stride=4), :] = item
        for z in range(8):
            for sp in range(2):
                for h in range(2):
                    base = (f * 4 + 2 * h) * 128 + z * 16 + sp * 8
                    even, odd = pair_halves(
                        lines[pl.ds(base, 8), :], lines[pl.ds(base + 128, 8), :], low
                    )
                    for s, item in ((2 * sp, even), (2 * sp + 1, odd)):
                        state[pl.ds(s * 256 + f * 128 + z * 16 + h * 8, 8), :] = item


def rows_of(block):
    s, f, z, x, y = block.shape
    return block.reshape(s, f, z, x, y // 128, 128).transpose(0, 1, 2, 4, 3, 5).reshape(-1, 128)


def on_device(
    cotangent, scenario_ids, weather, landuse, class_diff, level_scale, emit_profile, building_cells
):
    hbm = pl.BlockSpec(memory_space=pltpu.HBM)
    vmem = pl.BlockSpec(memory_space=pltpu.VMEM)
    params = pltpu.CompilerParams(vmem_limit_bytes=32 * 1024 * 1024)
    slabs = lax.axis_size("tile")
    groups = lax.axis_size("scen")
    width = cotangent.shape[4]
    cells = building_cells.T
    classes = landuse.reshape(4, 4, 128).transpose(1, 0, 2).reshape(16, 128)
    small = (scenario_ids, weather.T, class_diff, level_scale, emit_profile)
    operands = (*small, classes, cells, rows_of(cotangent))
    sent, kept, vectors, window = pl.pallas_call(
        first_kernel,
        out_shape=(
            jax.ShapeDtypeStruct((slabs, SEND, 128), F32),
            jax.ShapeDtypeStruct((slabs, 48, 128), F32),
            jax.ShapeDtypeStruct((10, 8, 128), F32),
            jax.ShapeDtypeStruct((width, cells.shape[1]), jnp.bfloat16),
        ),
        in_specs=[hbm] * 8,
        out_specs=(vmem,) * 4,
        scratch_shapes=[pltpu.SMEM(item.shape, item.dtype) for item in small]
        + [pltpu.VMEM(item.shape, item.dtype) for item in (classes, cells)]
        + [pltpu.VMEM((1024, 128), F32)] * 7
        + [pltpu.VMEM((32, 128), F32), pltpu.SemaphoreType.DMA((9,))],
        compiler_params=params,
    )(*(pltpu.with_memory_space_constraint(item, pltpu.HBM) for item in operands))
    got = lax.all_to_all(sent, "tile", 0, 0)
    ends = pl.pallas_call(
        middle_kernel,
        out_shape=jax.ShapeDtypeStruct((slabs, 16, 128), F32),
        in_specs=[vmem] * 2,
        out_specs=vmem,
        compiler_params=params,
    )(vectors, got)
    ends = lax.all_to_all(ends, "tile", 0, 0)
    grad = pl.pallas_call(
        sums_kernel,
        out_shape=jax.ShapeDtypeStruct((2, cells.shape[1]), F32),
        in_specs=[vmem] * 4,
        out_specs=vmem,
        compiler_params=params,
    )(vectors, window, ends, kept)
    state = pl.pallas_call(
        state_kernel,
        out_shape=jax.ShapeDtypeStruct((1024, 128), F32),
        in_specs=[vmem] * 2,
        out_specs=vmem,
        scratch_shapes=[pltpu.VMEM((1024, 128), F32)],
        compiler_params=params,
    )(ends, kept)
    grad = grad + lax.ppermute(grad, "scen", [(i, i ^ 1) for i in range(groups)])
    grad = grad + sum(
        lax.ppermute(grad, "scen", [(i, (i + step) % groups) for i in range(groups)])
        for step in (2, 6, 4)
    )
    state = state.reshape(4, 2, 8, 4, 4, 128).transpose(0, 1, 2, 4, 3, 5).reshape(cotangent.shape)
    return (state, grad)


def solution(mesh):
    placed = (
        P("scen", None, None, "tile", None),
        P("scen"),
        P(),
        P("tile", None),
        P(),
        P(),
        P(),
        P("tile", None),
    )
    return jax.shard_map(
        on_device,
        mesh=mesh,
        in_specs=placed,
        out_specs=(P("scen", None, None, "tile", None), P(None, "tile")),
        check_vma=False,
    )
```

```python
import jax
import jax.numpy as jnp
from jax import lax
from jax.experimental import pallas as pl
from jax.experimental.pallas import tpu as pltpu
from jax.sharding import PartitionSpec as P

F32 = jnp.float32
SEND = 17


def inverse(value):
    guess = pl.reciprocal(value, approx=True)
    guess = guess * (2.0 - value * guess)
    return guess * (2.0 - value * guess)


def sublane():
    return lax.broadcasted_iota(jnp.int32, (8, 128), 0)


def lane():
    return lax.broadcasted_iota(jnp.int32, (8, 128), 1)


def choose(index, values):
    out = jnp.full((8, 128), values[-1], F32)
    for at in range(len(values) - 2, -1, -1):
        out = jnp.where(index == at, values[at], out)
    return out


def surface(classes, class_diff, field):
    out = jnp.zeros((8, 128), F32)
    for mark in range(class_diff.shape[1]):
        out = jnp.where(classes == mark, class_diff[field, mark], out)
    return out


def swap_halves(value):
    return pltpu.roll(value, 4, axis=0)


def pair_halves(first, second, low):
    return (
        jnp.where(low, first, swap_halves(second)),
        jnp.where(low, swap_halves(first), second),
    )


def exchange(items, lanes):
    for bit in range(3):
        step = 1 << bit
        clear = (lanes // 16) // step % 2 == 0
        out = list(items)
        for n in range(8):
            if n & step == 0:
                first, second = items[n], items[n + step]
                out[n] = jnp.where(clear, first, pltpu.roll(second, 16 * step, axis=1))
                out[n + step] = jnp.where(clear, pltpu.roll(first, 128 - 16 * step, axis=1), second)
        items = out
    return items


def solve_levels(cot, surf, scale, table, out, hold_a, hold_c, low, arrivals):
    half = [(scale[z] + scale[z + 1]) * 0.5 for z in range(7)]
    for pair in range(2):
        arrivals[pair].wait()
        chains = [(s, f, h) for s in (2 * pair, 2 * pair + 1) for f in range(2) for h in range(2)]
        rated = [surf[f][h] * table(s, 2) for s, f, h in chains]
        winds = [table(s, 5) for s, f, h in chains]
        values = [None] * 8
        slacks = [None] * 8
        faces = [None] * 8
        for z in range(8):
            for n, (s, f, h) in enumerate(chains):
                rhs = cot[pl.ds(s * 256 + f * 128 + z * 16 + h * 8, 8), :]
                if z == 0:
                    slack = 1.0 + rated[n] * (scale[0] * 0.5)
                else:
                    slack = 1.0 + faces[n] * slacks[n]
                    rhs = rhs + faces[n] * values[n]
                if z < 7:
                    face = rated[n] * half[z]
                    above = face + winds[n]
                    inv = inverse(above + slack)
                    values[n] = rhs * inv
                    slacks[n] = slack * inv
                    faces[n] = face
                    hold_a[pl.ds((z * 8 + n) * 8, 8), :] = values[n]
                    hold_c[pl.ds((z * 8 + n) * 8, 8), :] = above * inv
                else:
                    slack = slack + (rated[n] * (scale[7] * 0.5) + winds[n])
                    values[n] = rhs * inverse(slack)
        for z in range(7, -1, -1):
            if z < 7:
                for n in range(8):
                    at = pl.ds((z * 8 + n) * 8, 8)
                    values[n] = hold_a[at, :] + hold_c[at, :] * values[n]
            for f in range(2):
                for h in range(2):
                    n = f * 2 + h
                    even, odd = pair_halves(values[n], values[n + 4], low)
                    for yb, item in ((2 * h, even), (2 * h + 1, odd)):
                        out[pl.ds((f * 4 + yb) * 128 + z * 16 + pair * 8, 8), :] = item


def from_before(items, rows, distance):
    turned = [pltpu.roll(item, distance, axis=0) for item in items]
    return [
        turned[v] if v % 4 == 0 else jnp.where(rows < distance, turned[v - 1], turned[v])
        for v in range(8)
    ]


def from_after(items, rows, distance):
    turned = [pltpu.roll(item, 8 - distance, axis=0) for item in items]
    return [
        turned[v] if v % 4 == 3 else jnp.where(rows >= 8 - distance, turned[v + 1], turned[v])
        for v in range(8)
    ]


def solve_chunks(below, above, slack, rhs, rows):
    everyone = range(8)
    for distance in (1, 2, 4, 8, 16):
        inv = [inverse(below[v] + above[v] + slack[v]) for v in everyone]
        nb = [below[v] * inv[v] for v in everyone]
        na = [above[v] * inv[v] for v in everyone]
        ns = [slack[v] * inv[v] for v in everyone]
        nr = [rhs[v] * inv[v] for v in everyone]
        new_slack = list(slack)
        new_rhs = list(rhs)
        if distance < 8:
            pb, ps, pr = (from_before(item, rows, distance) for item in (nb, ns, nr))
            qa, qs, qr = (from_after(item, rows, distance) for item in (na, ns, nr))
            has_before = has_after = [True] * 8
        else:
            jump = distance // 8
            has_before = [v % 4 >= jump for v in everyone]
            has_after = [v % 4 < 4 - jump for v in everyone]
            pb, ps, pr = (
                [item[v - jump] if has_before[v] else None for v in everyone]
                for item in (nb, ns, nr)
            )
            qa, qs, qr = (
                [item[v + jump] if has_after[v] else None for v in everyone]
                for item in (na, ns, nr)
            )
        zero = jnp.zeros((8, 128), F32)
        new_below = [zero] * 8
        new_above = [zero] * 8
        for v in everyone:
            if has_before[v]:
                new_slack[v] = new_slack[v] + below[v] * ps[v]
                new_rhs[v] = new_rhs[v] + below[v] * pr[v]
                new_below[v] = below[v] * pb[v]
            if has_after[v]:
                new_slack[v] = new_slack[v] + above[v] * qs[v]
                new_rhs[v] = new_rhs[v] + above[v] * qr[v]
                new_above[v] = above[v] * qa[v]
        below, above, slack, rhs = new_below, new_above, new_slack, new_rhs
    return [rhs[v] * inverse(slack[v]) for v in everyone]


def solve_rows(turned, faces, leak, rate, wind, hold_a, hold_b, hold_c, rows):
    everyone = range(8)
    depth = 16

    def at(v, i):
        return pl.ds(v * 128 + i, 8, stride=depth)

    def keep(i, v):
        return pl.ds((i * 8 + v) * 8, 8)

    ends = [faces[at(v, depth - 1), :] * rate for v in everyone]
    before = from_before(ends, rows, 1)
    last = ends
    value = [None] * 8
    fill = [None] * 8
    slack = [None] * 8
    for i in range(depth):
        for v in everyone:
            rhs = turned[at(v, i), :]
            face = last[v] if i == depth - 1 else faces[at(v, i), :] * rate
            next_coef = face + wind
            if i == 0:
                link = before[v]
                own = jnp.ones((8, 128), F32)
                if v % 4 == 0:
                    own = jnp.where(rows == 0, 1.0 + leak[v // 4], own)
                    link = jnp.where(rows == 0, 0.0, link)
            else:
                link = before[v] * fill[v]
                own = 1.0 + before[v] * slack[v]
                rhs = rhs + before[v] * value[v]
            if i == depth - 1:
                if v % 4 == 3:
                    own = jnp.where(rows == 7, own + next_coef, own)
                    next_coef = jnp.where(rows == 7, 0.0, next_coef)
                value[v], fill[v], slack[v] = rhs, link, own
                before[v] = next_coef
                continue
            inv = inverse(next_coef + link + own)
            value[v] = rhs * inv
            fill[v] = link * inv
            slack[v] = own * inv
            upper = next_coef * inv
            hold_a[keep(i, v), :] = value[v]
            hold_b[keep(i, v), :] = fill[v]
            hold_c[keep(i, v), :] = upper
            before[v] = face
            if i == 0:
                if v == 0:
                    first_value, first_fill, first_slack, first_next = ([None] * 8 for _ in range(4))
                first_value[v], first_fill[v], first_slack[v], first_next[v] = (
                    value[v],
                    fill[v],
                    slack[v],
                    upper,
                )
            else:
                carry = first_next[v]
                first_value[v] = first_value[v] + carry * value[v]
                first_slack[v] = first_slack[v] + carry * slack[v]
                first_next[v] = carry * upper
    next_value = from_after(first_value, rows, 1)
    next_slack = from_after(first_slack, rows, 1)
    next_next = from_after(first_next, rows, 1)
    above = [before[v] * next_next[v] for v in everyone]
    slack = [slack[v] + before[v] * next_slack[v] for v in everyone]
    rhs = [value[v] + before[v] * next_value[v] for v in everyone]
    current = solve_chunks(fill, above, slack, rhs, rows)
    previous = from_before(current, rows, 1)
    for v in everyone:
        turned[at(v, depth - 1), :] = current[v]
    for i in range(depth - 2, -1, -1):
        for v in everyone:
            item = hold_a[keep(i, v), :] + hold_b[keep(i, v), :] * previous[v]
            current[v] = item + hold_c[keep(i, v), :] * current[v]
            turned[at(v, i), :] = current[v]


def inner_coefs(low_face, mid_face, high_face, wind):
    one_next = mid_face + wind
    one_inv = inverse(low_face + one_next + 1.0)
    one_fill = low_face * one_inv
    one_upper = one_next * one_inv
    two_next = high_face + wind
    two_fill = mid_face * one_fill
    two_slack = 1.0 + mid_face * one_inv
    two_inv = inverse(two_next + two_fill + two_slack)
    return one_inv, one_fill, one_upper, two_inv, two_fill, two_slack, two_next


def first_kernel(
    ids_in, weather_in, class_diff_in, scale_in, emit_in, landuse_in, cells_in, cot_in,
    sent, kept, vectors, window,
    ids, weather, class_diff, scale, emit, landuse, cells, cot,
    levels, turned, faces, hold_a, hold_b, hold_c, surf_rows, done,
):
    small = [
        pltpu.make_async_copy(source, target, done.at[n])
        for n, (source, target) in enumerate(
            (
                (ids_in, ids),
                (weather_in, weather),
                (class_diff_in, class_diff),
                (scale_in, scale),
                (emit_in, emit),
                (landuse_in, landuse),
                (cells_in, cells),
            )
        )
    ]
    halves = [
        pltpu.make_async_copy(
            cot_in.at[pl.ds(n * 512, 512), :], cot.at[pl.ds(n * 512, 512), :], done.at[7 + n]
        )
        for n in range(2)
    ]
    for copy in small + halves:
        copy.start()
    for copy in small:
        copy.wait()
    rows = sublane()
    lanes = lane()
    low = rows < 4

    def table(s, column):
        return weather[column, ids[s]]

    classes = [landuse[pl.ds(0, 8), :], landuse[pl.ds(8, 8), :]]
    surf = [[surface(item, class_diff, f) for item in classes] for f in range(2)]
    rate_y = choose((lanes // 4) % 4, [table(s, 1) for s in range(4)])
    wind_y = choose((lanes // 4) % 4, [table(s, 4) for s in range(4)])
    rate_y = rate_y * choose(lanes // 16, [scale[z] for z in range(8)])
    leak = []
    for f in range(2):
        upper, lower = surf[f]
        surf_rows[pl.ds(f * 16, 8), :] = upper
        surf_rows[pl.ds(f * 16 + 8, 8), :] = lower
        shifted = [pltpu.roll(item, 127, axis=1) for item in (upper, lower)]
        swapped = [swap_halves(item) for item in shifted]
        onward = [
            jnp.where(low, swapped[0], swapped[1]),
            jnp.where(low, swapped[1], 0.0),
        ]
        for h in range(2):
            right = jnp.where(lanes == 127, onward[h], shifted[h])
            face = (surf[f][h] + right) * 0.5
            other = swap_halves(face)
            for yb, item in (
                (2 * h, jnp.where(low, face, other)),
                (2 * h + 1, jnp.where(low, other, face)),
            ):
                tile = jnp.concatenate([item] * 16, axis=0)
                faces[pl.ds((f * 4 + yb) * 128, 128), :] = tile.T
        start = jnp.broadcast_to(upper[:, 0:1], (8, 128))
        start = jnp.where(rows == lanes % 4, start, 0.0)
        start = jnp.broadcast_to(jnp.sum(start, axis=0, keepdims=True), (8, 128))
        leak.append(start * 0.5 * rate_y)

    rate_x = choose(rows % 4, [table(s, 0) for s in range(4)])
    wind_x = choose(rows % 4, [table(s, 3) for s in range(4)])
    scales = [choose(rows // 4, [scale[2 * zp], scale[2 * zp + 1]]) for zp in range(4)]
    vectors[0] = rate_x * choose(lanes // 16 % 4, scales)
    vectors[1] = wind_x
    for f in range(2):
        factor = choose(rows % 4, [table(s, 6 + f) for s in range(4)])
        for zp in range(4):
            vectors[2 + f * 4 + zp] = factor * choose(rows // 4, [emit[2 * zp], emit[2 * zp + 1]])
    for v in range(8):
        line = [surf_rows[pl.ds(v * 4 + x, 1), :] for x in range(4)]
        steps = [(line[x] + line[x + 1]) * 0.5 for x in range(3)]
        for zp in range(4):
            j = v * 4 + zp
            rate = rate_x * scales[zp]
            one_inv, one_fill, one_upper, two_inv, two_fill, two_slack, two_next = inner_coefs(
                *(rate * step for step in steps), wind_x
            )
            for n, item in enumerate(
                (one_inv, one_fill, one_upper, two_inv, two_fill * two_inv, two_next * two_inv)
            ):
                kept[j, pl.ds(n * 8, 8), :] = item
    strips = [surf_rows[pl.ds(f * 16 + x, 4, stride=4), :] for f in range(2) for x in range(4)]
    for g, strip in enumerate(exchange(strips, lanes[0:4])):
        for yb in range(4):
            sent[pl.ds((yb * 8 + g) * SEND + 16, 1), :] = strip[yb : yb + 1, :]
    width = window.shape[0]
    start = jnp.min(cells[...] % width, axis=0, keepdims=True)
    place = lax.broadcasted_iota(jnp.int32, (width, 128), 0)
    window[...] = jnp.where((place >= start) & (place < start + 4), 1.0, 0.0).astype(jnp.bfloat16)

    solve_levels(cot, surf, scale, table, levels, hold_a, hold_c, low, halves)
    for v in range(8):
        block = pl.ds(v * 128, 128)
        turned[block, :] = levels[block, :].T
    solve_rows(turned, faces, leak, rate_y, wind_y, hold_a, hold_b, hold_c, rows)
    for v in range(8):
        block = pl.ds(v * 128, 128)
        levels[block, :] = turned[block, :].T

    for yb in range(4):
        firsts, lasts = [], []
        for f in range(2):
            v = f * 4 + yb
            line = [surf_rows[pl.ds(v * 4 + x, 1), :] for x in range(4)]
            steps = [(line[x] + line[x + 1]) * 0.5 for x in range(3)]
            for zp in range(4):
                j = v * 4 + zp
                rate = rate_x * scales[zp]
                e01, e12, e23 = (rate * step for step in steps)
                rhs = [levels[pl.ds(v * 128 + zp * 32 + x, 8, stride=4), :] for x in range(4)]
                one = rhs[1] * kept[j, pl.ds(0, 8), :]
                two = (rhs[2] + e12 * one) * kept[j, pl.ds(24, 8), :]
                one_upper = kept[j, pl.ds(16, 8), :]
                firsts.append(rhs[0] + (e01 + wind_x) * (one + one_upper * two))
                lasts.append(rhs[3] + e23 * two)
                kept[j, pl.ds(0, 8), :] = one
                kept[j, pl.ds(24, 8), :] = two
        for offset, items in ((0, firsts), (8, lasts)):
            for g, item in enumerate(exchange(items, lanes)):
                sent[pl.ds((yb * 8 + g) * SEND + offset, 8), :] = item


def middle_kernel(vectors, got, ends, spread):
    lanes = lane()
    slabs = ends.shape[0]
    for q in range(slabs // 8):
        strip = got[pl.ds(q * 8 * SEND + 16, 8, stride=SEND), :]
        turned = {d: pltpu.roll(strip, 16 * d % 128, axis=1) if d else strip for d in range(-3, 4)}
        for x in range(4):
            spread[pl.ds(x * slabs + q * 8, 8), :] = choose(
                lanes // 16 % 4, [turned[zp - x] for zp in range(4)]
            )
    rate = vectors[0]
    wind = vectors[1]
    below, above, slack, rhs = [], [], [], []
    line = None
    outer = None
    for k in range(slabs):
        line = [spread[pl.ds(x * slabs + k, 1), :] for x in range(4)]
        if k == 0:
            outer = rate * (line[0] * 0.5)
        e01, e12, e23 = (rate * ((line[x] + line[x + 1]) * 0.5) for x in range(3))
        one_inv, one_fill, one_upper, two_inv, two_fill, two_slack, two_next = inner_coefs(
            e01, e12, e23, wind
        )
        two_slack = two_slack * two_inv
        q0 = e01 + wind
        own = 1.0 + q0 * (one_inv + one_upper * two_slack)
        if k == 0:
            own = own + outer
            below.append(None)
        else:
            below.append(outer)
        above.append(q0 * (one_upper * (two_next * two_inv)))
        slack.append(own)
        rhs.append(got[pl.ds(k * SEND, 8), :])
        if k < slabs - 1:
            outer = rate * ((line[3] + spread[pl.ds(k + 1, 1), :]) * 0.5)
        else:
            outer = rate * (line[3] * 0.5)
        own = 1.0 + e23 * two_slack
        below.append(e23 * (two_fill * two_inv))
        if k < slabs - 1:
            above.append(outer + wind)
        else:
            own = own + (outer + wind)
            above.append(None)
        slack.append(own)
        rhs.append(got[pl.ds(k * SEND + 8, 8), :])

    def total(i):
        out = slack[i]
        if below[i] is not None:
            out = out + below[i]
        if above[i] is not None:
            out = out + above[i]
        return out

    count = 2 * slabs
    alive = list(range(count))
    removed = []
    while len(alive) > 1:
        gone = alive[1::2]
        stay = alive[0::2]
        normal = {}
        for i in gone:
            inv = inverse(total(i))
            normal[i] = (
                below[i] * inv,
                None if above[i] is None else above[i] * inv,
                slack[i] * inv,
                rhs[i] * inv,
            )
        for n, i in enumerate(stay):
            new_below = new_above = None
            new_slack, new_rhs = slack[i], rhs[i]
            if n > 0:
                nb, na, ns, nr = normal[gone[n - 1]]
                new_slack = new_slack + below[i] * ns
                new_rhs = new_rhs + below[i] * nr
                new_below = below[i] * nb
            if n < len(gone):
                nb, na, ns, nr = normal[gone[n]]
                new_slack = new_slack + above[i] * ns
                new_rhs = new_rhs + above[i] * nr
                new_above = None if na is None else above[i] * na
            below[i], above[i], slack[i], rhs[i] = new_below, new_above, new_slack, new_rhs
        removed.append((alive, normal))
        alive = stay
    solved = {0: rhs[0] * inverse(slack[0])}
    for order, normal in reversed(removed):
        for n in range(1, len(order), 2):
            nb, na, ns, nr = normal[order[n]]
            item = nr + nb * solved[order[n - 1]]
            if na is not None:
                item = item + na * solved[order[n + 1]]
            solved[order[n]] = item
    for k in range(slabs):
        ends[k, pl.ds(0, 8), :] = solved[2 * k]
        ends[k, pl.ds(8, 8), :] = solved[2 * k + 1]


def inner_rows(ends, kept, j):
    first = ends[j, pl.ds(0, 8), :]
    last = ends[j, pl.ds(8, 8), :]
    a1, b1, c1, a2, b2, c2 = (kept[j, pl.ds(n * 8, 8), :] for n in range(6))
    two = a2 + b2 * first + c2 * last
    one = a1 + b1 * first + c1 * two
    return first, one, two, last


def sums_kernel(vectors, window, ends, kept, grad, sorted_ends):
    parts = []
    lanes = lane()
    for yb in range(4):
        for row in (0, 8):
            items = exchange([ends[yb * 8 + g, pl.ds(row, 8), :] for g in range(8)], lanes)
            for m, item in enumerate(items):
                sorted_ends[(m // 4 * 4 + yb) * 4 + m % 4, pl.ds(row, 8), :] = item
    for v in range(8):
        total = None
        for zp in range(4):
            first, one, two, last = inner_rows(sorted_ends, kept, v * 4 + zp)
            item = vectors[2 + (v // 4) * 4 + zp] * ((first + one) + (two + last))
            total = item if total is None else total + item
        parts.append(jnp.sum(total, axis=0, keepdims=True))
    sums = [jnp.concatenate(parts[f * 4 : f * 4 + 4], axis=1) for f in range(2)]
    pieces = []
    for _ in range(3):
        piece = [item.astype(jnp.bfloat16).astype(F32) for item in sums]
        sums = [item - cut for item, cut in zip(sums, piece)]
        pieces += piece
    pieces = jnp.concatenate(pieces + [jnp.zeros((2, sums[0].shape[1]), F32)], axis=0)
    picked = jnp.dot(pieces.astype(jnp.bfloat16), window[...], preferred_element_type=F32)
    grad[...] = (picked[0:2, :] + picked[2:4, :]) + picked[4:6, :]


def state_kernel(ends, kept, state, lines):
    low = sublane() < 4
    for f in range(2):
        for yb in range(4):
            v = f * 4 + yb
            for zp in range(4):
                for x, item in enumerate(inner_rows(ends, kept, v * 4 + zp)):
                    lines[pl.ds(v * 128 + zp * 32 + x, 8, stride=4), :] = item
        for z in range(8):
            for sp in range(2):
                for h in range(2):
                    base = (f * 4 + 2 * h) * 128 + z * 16 + sp * 8
                    even, odd = pair_halves(
                        lines[pl.ds(base, 8), :], lines[pl.ds(base + 128, 8), :], low
                    )
                    for s, item in ((2 * sp, even), (2 * sp + 1, odd)):
                        state[pl.ds(s * 256 + f * 128 + z * 16 + h * 8, 8), :] = item


def rows_of(block):
    s, f, z, x, y = block.shape
    return block.reshape(s, f, z, x, y // 128, 128).transpose(0, 1, 2, 4, 3, 5).reshape(-1, 128)


def on_device(
    cotangent, scenario_ids, weather, landuse, class_diff, level_scale, emit_profile, building_cells
):
    hbm = pl.BlockSpec(memory_space=pltpu.HBM)
    vmem = pl.BlockSpec(memory_space=pltpu.VMEM)
    params = pltpu.CompilerParams(vmem_limit_bytes=32 * 1024 * 1024)
    slabs = lax.axis_size("tile")
    groups = lax.axis_size("scen")
    width = cotangent.shape[4]
    cells = building_cells.T
    classes = landuse.reshape(4, 4, 128).transpose(1, 0, 2).reshape(16, 128)
    small = (scenario_ids, weather.T, class_diff, level_scale, emit_profile)
    operands = (*small, classes, cells, rows_of(cotangent))
    sent, kept, vectors, window = pl.pallas_call(
        first_kernel,
        out_shape=(
            jax.ShapeDtypeStruct((slabs * SEND, 128), F32),
            jax.ShapeDtypeStruct((slabs, 48, 128), F32),
            jax.ShapeDtypeStruct((10, 8, 128), F32),
            jax.ShapeDtypeStruct((width, cells.shape[1]), jnp.bfloat16),
        ),
        in_specs=[hbm] * 8,
        out_specs=(vmem,) * 4,
        scratch_shapes=[pltpu.SMEM(item.shape, item.dtype) for item in small]
        + [pltpu.VMEM(item.shape, item.dtype) for item in (classes, cells)]
        + [pltpu.VMEM((1024, 128), F32)] * 7
        + [pltpu.VMEM((32, 128), F32), pltpu.SemaphoreType.DMA((9,))],
        compiler_params=params,
    )(*(pltpu.with_memory_space_constraint(item, pltpu.HBM) for item in operands))
    got = lax.all_to_all(sent.reshape(slabs, SEND, 1, 128), "tile", 0, 0).reshape(slabs * SEND, 128)
    ends = pl.pallas_call(
        middle_kernel,
        out_shape=jax.ShapeDtypeStruct((slabs, 16, 128), F32),
        in_specs=[vmem] * 2,
        out_specs=vmem,
        scratch_shapes=[pltpu.VMEM((4 * slabs, 128), F32)],
        compiler_params=params,
    )(vectors, got)
    ends = lax.all_to_all(ends, "tile", 0, 0)
    grad, ends = pl.pallas_call(
        sums_kernel,
        out_shape=(
            jax.ShapeDtypeStruct((2, cells.shape[1]), F32),
            jax.ShapeDtypeStruct((slabs, 16, 128), F32),
        ),
        in_specs=[vmem] * 4,
        out_specs=(vmem, vmem),
        compiler_params=params,
    )(vectors, window, ends, kept)
    state = pl.pallas_call(
        state_kernel,
        out_shape=jax.ShapeDtypeStruct((1024, 128), F32),
        in_specs=[vmem] * 2,
        out_specs=vmem,
        scratch_shapes=[pltpu.VMEM((1024, 128), F32)],
        compiler_params=params,
    )(ends, kept)
    for partner in (
        lambda i: i ^ 1,
        lambda i: i ^ 2,
        lambda i: groups - 2 - i + 2 * (i % 2),
    ):
        grad = grad + lax.ppermute(grad, "scen", [(i, partner(i)) for i in range(groups)])
    state = state.reshape(4, 2, 8, 4, 4, 128).transpose(0, 1, 2, 4, 3, 5).reshape(cotangent.shape)
    return (state, grad)


def solution(mesh):
    placed = (
        P("scen", None, None, "tile", None),
        P("scen"),
        P(),
        P("tile", None),
        P(),
        P(),
        P(),
        P("tile", None),
    )
    return jax.shard_map(
        on_device,
        mesh=mesh,
        in_specs=placed,
        out_specs=(P("scen", None, None, "tile", None), P(None, "tile")),
        check_vma=False,
    )
```

```python
import jax
import jax.numpy as jnp
from jax import lax
from jax.experimental import pallas as pl
from jax.experimental.pallas import tpu as pltpu
from jax.sharding import PartitionSpec as P

F32 = jnp.float32
SEND = 17


def inverse(value):
    return pltpu.reciprocal(value, approx=True)


def sublane():
    return lax.broadcasted_iota(jnp.int32, (8, 128), 0)


def lane():
    return lax.broadcasted_iota(jnp.int32, (8, 128), 1)


def choose(index, values):
    out = jnp.full((8, 128), values[-1], F32)
    for at in range(len(values) - 2, -1, -1):
        out = jnp.where(index == at, values[at], out)
    return out


def surface(classes, class_diff, field):
    out = jnp.zeros((8, 128), F32)
    for mark in range(class_diff.shape[1]):
        out = jnp.where(classes == mark, class_diff[field, mark], out)
    return out


def swap_halves(value):
    return pltpu.roll(value, 4, axis=0)


def pair_halves(first, second, low):
    return (
        jnp.where(low, first, swap_halves(second)),
        jnp.where(low, swap_halves(first), second),
    )


def pick(groups, items):
    out = items[3]
    for at in range(2, -1, -1):
        out = jnp.where(groups == at, items[at], out)
    return out


def to_strips(items, groups):
    turned = [pltpu.roll(item, 32 * m, axis=1) if m else item for m, item in enumerate(items)]
    return [pick(groups, [turned[(p - g) % 4] for p in range(4)]) for g in range(4)]


def from_strips(strips, groups):
    items = [pick(groups, [strips[(p - m) % 4] for p in range(4)]) for m in range(4)]
    return [pltpu.roll(item, 128 - 32 * m, axis=1) if m else item for m, item in enumerate(items)]


def solve_levels(cot, surf, scale, table, out, hold_a, hold_c, low, arrivals):
    half = [(scale[z] + scale[z + 1]) * 0.5 for z in range(7)]
    for pair in range(2):
        arrivals[pair].wait()
        chains = [(s, f, h) for s in (2 * pair, 2 * pair + 1) for f in range(2) for h in range(2)]
        rated = [surf[f][h] * table(s, 2) for s, f, h in chains]
        winds = [table(s, 5) for s, f, h in chains]
        values = [None] * 8
        slacks = [None] * 8
        faces = [None] * 8
        for z in range(8):
            for n, (s, f, h) in enumerate(chains):
                rhs = cot[pl.ds(s * 256 + f * 128 + z * 16 + h * 8, 8), :]
                if z == 0:
                    slack = 1.0 + rated[n] * (scale[0] * 0.5)
                else:
                    slack = 1.0 + faces[n] * slacks[n]
                    rhs = rhs + faces[n] * values[n]
                if z < 7:
                    face = rated[n] * half[z]
                    above = face + winds[n]
                    inv = inverse(above + slack)
                    values[n] = rhs * inv
                    slacks[n] = slack * inv
                    faces[n] = face
                    hold_a[pl.ds((z * 8 + n) * 8, 8), :] = values[n]
                    hold_c[pl.ds((z * 8 + n) * 8, 8), :] = above * inv
                else:
                    slack = slack + (rated[n] * (scale[7] * 0.5) + winds[n])
                    values[n] = rhs * inverse(slack)
        for z in range(7, -1, -1):
            if z < 7:
                for n in range(8):
                    at = pl.ds((z * 8 + n) * 8, 8)
                    values[n] = hold_a[at, :] + hold_c[at, :] * values[n]
            for f in range(2):
                for h in range(2):
                    n = f * 2 + h
                    even, odd = pair_halves(values[n], values[n + 4], low)
                    for yb, item in ((2 * h, even), (2 * h + 1, odd)):
                        out[pl.ds((f * 4 + yb) * 128 + z * 16 + pair * 8, 8), :] = item


def from_before(items, rows, distance):
    turned = [pltpu.roll(item, distance, axis=0) for item in items]
    return [
        turned[v] if v % 4 == 0 else jnp.where(rows < distance, turned[v - 1], turned[v])
        for v in range(8)
    ]


def from_after(items, rows, distance):
    turned = [pltpu.roll(item, 8 - distance, axis=0) for item in items]
    return [
        turned[v] if v % 4 == 3 else jnp.where(rows >= 8 - distance, turned[v + 1], turned[v])
        for v in range(8)
    ]


def solve_chunks(below, above, slack, rhs, rows):
    everyone = range(8)
    for distance in (1, 2, 4, 8, 16):
        inv = [inverse(below[v] + above[v] + slack[v]) for v in everyone]
        nb = [below[v] * inv[v] for v in everyone]
        na = [above[v] * inv[v] for v in everyone]
        ns = [slack[v] * inv[v] for v in everyone]
        nr = [rhs[v] * inv[v] for v in everyone]
        new_slack = list(slack)
        new_rhs = list(rhs)
        if distance < 8:
            pb, ps, pr = (from_before(item, rows, distance) for item in (nb, ns, nr))
            qa, qs, qr = (from_after(item, rows, distance) for item in (na, ns, nr))
            has_before = has_after = [True] * 8
        else:
            jump = distance // 8
            has_before = [v % 4 >= jump for v in everyone]
            has_after = [v % 4 < 4 - jump for v in everyone]
            pb, ps, pr = (
                [item[v - jump] if has_before[v] else None for v in everyone]
                for item in (nb, ns, nr)
            )
            qa, qs, qr = (
                [item[v + jump] if has_after[v] else None for v in everyone]
                for item in (na, ns, nr)
            )
        zero = jnp.zeros((8, 128), F32)
        new_below = [zero] * 8
        new_above = [zero] * 8
        for v in everyone:
            if has_before[v]:
                new_slack[v] = new_slack[v] + below[v] * ps[v]
                new_rhs[v] = new_rhs[v] + below[v] * pr[v]
                new_below[v] = below[v] * pb[v]
            if has_after[v]:
                new_slack[v] = new_slack[v] + above[v] * qs[v]
                new_rhs[v] = new_rhs[v] + above[v] * qr[v]
                new_above[v] = above[v] * qa[v]
        below, above, slack, rhs = new_below, new_above, new_slack, new_rhs
    return [rhs[v] * inverse(slack[v]) for v in everyone]


def solve_rows(turned, faces, leak, rate, wind, hold_a, hold_b, hold_c, rows):
    everyone = range(8)
    depth = 16

    def at(v, i):
        return pl.ds(v * 128 + i, 8, stride=depth)

    def keep(i, v):
        return pl.ds((i * 8 + v) * 8, 8)

    ends = [faces[at(v, depth - 1), :] * rate for v in everyone]
    before = from_before(ends, rows, 1)
    last = ends
    value = [None] * 8
    fill = [None] * 8
    slack = [None] * 8
    for i in range(depth):
        for v in everyone:
            rhs = turned[at(v, i), :]
            face = last[v] if i == depth - 1 else faces[at(v, i), :] * rate
            next_coef = face + wind
            if i == 0:
                link = before[v]
                own = jnp.ones((8, 128), F32)
                if v % 4 == 0:
                    own = jnp.where(rows == 0, 1.0 + leak[v // 4], own)
                    link = jnp.where(rows == 0, 0.0, link)
            else:
                link = before[v] * fill[v]
                own = 1.0 + before[v] * slack[v]
                rhs = rhs + before[v] * value[v]
            if i == depth - 1:
                if v % 4 == 3:
                    own = jnp.where(rows == 7, own + next_coef, own)
                    next_coef = jnp.where(rows == 7, 0.0, next_coef)
                value[v], fill[v], slack[v] = rhs, link, own
                before[v] = next_coef
                continue
            inv = inverse(next_coef + link + own)
            value[v] = rhs * inv
            fill[v] = link * inv
            slack[v] = own * inv
            upper = next_coef * inv
            hold_a[keep(i, v), :] = value[v]
            hold_b[keep(i, v), :] = fill[v]
            hold_c[keep(i, v), :] = upper
            before[v] = face
            if i == 0:
                if v == 0:
                    first_value, first_fill, first_slack, first_next = ([None] * 8 for _ in range(4))
                first_value[v], first_fill[v], first_slack[v], first_next[v] = (
                    value[v],
                    fill[v],
                    slack[v],
                    upper,
                )
            else:
                carry = first_next[v]
                first_value[v] = first_value[v] + carry * value[v]
                first_slack[v] = first_slack[v] + carry * slack[v]
                first_next[v] = carry * upper
    next_value = from_after(first_value, rows, 1)
    next_slack = from_after(first_slack, rows, 1)
    next_next = from_after(first_next, rows, 1)
    above = [before[v] * next_next[v] for v in everyone]
    slack = [slack[v] + before[v] * next_slack[v] for v in everyone]
    rhs = [value[v] + before[v] * next_value[v] for v in everyone]
    current = solve_chunks(fill, above, slack, rhs, rows)
    previous = from_before(current, rows, 1)
    for v in everyone:
        turned[at(v, depth - 1), :] = current[v]
    for i in range(depth - 2, -1, -1):
        for v in everyone:
            item = hold_a[keep(i, v), :] + hold_b[keep(i, v), :] * previous[v]
            current[v] = item + hold_c[keep(i, v), :] * current[v]
            turned[at(v, i), :] = current[v]


def inner_coefs(low_face, mid_face, high_face, wind):
    one_next = mid_face + wind
    one_inv = inverse(low_face + one_next + 1.0)
    one_fill = low_face * one_inv
    one_upper = one_next * one_inv
    two_next = high_face + wind
    two_fill = mid_face * one_fill
    two_slack = 1.0 + mid_face * one_inv
    two_inv = inverse(two_next + two_fill + two_slack)
    return one_inv, one_fill, one_upper, two_inv, two_fill, two_slack, two_next


def first_kernel(
    ids_in, weather_in, class_diff_in, scale_in, emit_in, landuse_in, cells_in, cot_in,
    sent, kept, vectors, window,
    ids, weather, class_diff, scale, emit, landuse, cells, cot,
    levels, turned, faces, hold_a, hold_b, hold_c, surf_rows, done,
):
    small = [
        pltpu.make_async_copy(source, target, done.at[n])
        for n, (source, target) in enumerate(
            (
                (ids_in, ids),
                (weather_in, weather),
                (class_diff_in, class_diff),
                (scale_in, scale),
                (emit_in, emit),
                (landuse_in, landuse),
                (cells_in, cells),
            )
        )
    ]
    halves = [
        pltpu.make_async_copy(
            cot_in.at[pl.ds(n * 512, 512), :], cot.at[pl.ds(n * 512, 512), :], done.at[7 + n]
        )
        for n in range(2)
    ]
    for copy in small + halves:
        copy.start()
    for copy in small:
        copy.wait()
    rows = sublane()
    lanes = lane()
    low = rows < 4

    def table(s, column):
        return weather[column, ids[s]]

    classes = [landuse[pl.ds(0, 8), :], landuse[pl.ds(8, 8), :]]
    surf = [[surface(item, class_diff, f) for item in classes] for f in range(2)]
    rate_y = choose((lanes // 4) % 4, [table(s, 1) for s in range(4)])
    wind_y = choose((lanes // 4) % 4, [table(s, 4) for s in range(4)])
    rate_y = rate_y * choose(lanes // 16, [scale[z] for z in range(8)])
    leak = []
    for f in range(2):
        upper, lower = surf[f]
        surf_rows[pl.ds(f * 16, 8), :] = upper
        surf_rows[pl.ds(f * 16 + 8, 8), :] = lower
        shifted = [pltpu.roll(item, 127, axis=1) for item in (upper, lower)]
        swapped = [swap_halves(item) for item in shifted]
        onward = [
            jnp.where(low, swapped[0], swapped[1]),
            jnp.where(low, swapped[1], 0.0),
        ]
        for h in range(2):
            right = jnp.where(lanes == 127, onward[h], shifted[h])
            face = (surf[f][h] + right) * 0.5
            other = swap_halves(face)
            for yb, item in (
                (2 * h, jnp.where(low, face, other)),
                (2 * h + 1, jnp.where(low, other, face)),
            ):
                tile = jnp.concatenate([item] * 16, axis=0)
                faces[pl.ds((f * 4 + yb) * 128, 128), :] = tile.T
        start = jnp.broadcast_to(upper[:, 0:1], (8, 128))
        start = jnp.where(rows == lanes % 4, start, 0.0)
        start = jnp.broadcast_to(jnp.sum(start, axis=0, keepdims=True), (8, 128))
        leak.append(start * 0.5 * rate_y)

    rate_x = choose(rows % 4, [table(s, 0) for s in range(4)])
    wind_x = choose(rows % 4, [table(s, 3) for s in range(4)])
    scales = [choose(rows // 4, [scale[2 * zp], scale[2 * zp + 1]]) for zp in range(4)]
    groups = lanes // 32
    for g in range(4):
        vectors[g] = rate_x * choose(groups, [scales[(p - g) % 4] for p in range(4)])
    vectors[4] = wind_x
    for f in range(2):
        factor = choose(rows % 4, [table(s, 6 + f) for s in range(4)])
        for zp in range(4):
            vectors[5 + f * 4 + zp] = factor * choose(rows // 4, [emit[2 * zp], emit[2 * zp + 1]])
    for v in range(8):
        line = [surf_rows[pl.ds(v * 4 + x, 1), :] for x in range(4)]
        steps = [(line[x] + line[x + 1]) * 0.5 for x in range(3)]
        for zp in range(4):
            j = v * 4 + zp
            rate = rate_x * scales[zp]
            one_inv, one_fill, one_upper, two_inv, two_fill, two_slack, two_next = inner_coefs(
                *(rate * step for step in steps), wind_x
            )
            for n, item in enumerate(
                (one_inv, one_fill, one_upper, two_inv, two_fill * two_inv, two_next * two_inv)
            ):
                kept[j, pl.ds(n * 8, 8), :] = item
    lines = [surf_rows[pl.ds(x, 8, stride=4), :] for x in range(4)]
    lines = [
        [pltpu.roll(item, 32 * d, axis=1) if d else item for d in range(4)] for item in lines
    ]
    strips = [pick(groups, [lines[x][(x - g) % 4] for x in range(4)]) for g in range(4)]
    for g in range(4):
        for v in range(8):
            sent[pl.ds((v * 4 + g) * SEND + 16, 1), :] = strips[g][v : v + 1, :]
    width = window.shape[0]
    start = jnp.min(cells[...] % width, axis=0, keepdims=True)
    place = lax.broadcasted_iota(jnp.int32, (width, 128), 0)
    window[...] = jnp.where((place >= start) & (place < start + 4), 1.0, 0.0).astype(jnp.bfloat16)

    solve_levels(cot, surf, scale, table, levels, hold_a, hold_c, low, halves)
    for v in range(8):
        block = pl.ds(v * 128, 128)
        turned[block, :] = levels[block, :].T
    solve_rows(turned, faces, leak, rate_y, wind_y, hold_a, hold_b, hold_c, rows)
    for v in range(8):
        block = pl.ds(v * 128, 128)
        levels[block, :] = turned[block, :].T

    for v in range(8):
        line = [surf_rows[pl.ds(v * 4 + x, 1), :] for x in range(4)]
        steps = [(line[x] + line[x + 1]) * 0.5 for x in range(3)]
        firsts, lasts = [], []
        for zp in range(4):
            j = v * 4 + zp
            rate = rate_x * scales[zp]
            e01, e12, e23 = (rate * step for step in steps)
            rhs = [levels[pl.ds(v * 128 + zp * 32 + x, 8, stride=4), :] for x in range(4)]
            one = rhs[1] * kept[j, pl.ds(0, 8), :]
            two = (rhs[2] + e12 * one) * kept[j, pl.ds(24, 8), :]
            one_upper = kept[j, pl.ds(16, 8), :]
            firsts.append(rhs[0] + (e01 + wind_x) * (one + one_upper * two))
            lasts.append(rhs[3] + e23 * two)
            kept[j, pl.ds(0, 8), :] = one
            kept[j, pl.ds(24, 8), :] = two
        for offset, items in ((0, firsts), (8, lasts)):
            for g, item in enumerate(to_strips(items, groups)):
                sent[pl.ds((v * 4 + g) * SEND + offset, 8), :] = item


def middle_kernel(vectors, got, ends, spread):
    groups = lane() // 32
    slabs = ends.shape[0]
    strip = lax.axis_index("tile") % 4
    for q in range(slabs // 8):
        shared = got[pl.ds(q * 8 * SEND + 16, 8, stride=SEND), :]
        turned = [pltpu.roll(shared, 32 * d, axis=1) if d else shared for d in range(4)]
        for x in range(4):
            spread[pl.ds(x * slabs + q * 8, 8), :] = pick(
                groups, [turned[(p - x) % 4] for p in range(4)]
            )
    rate = vectors[strip]
    wind = vectors[4]
    below, above, slack, rhs = [], [], [], []
    line = None
    outer = None
    for k in range(slabs):
        line = [spread[pl.ds(x * slabs + k, 1), :] for x in range(4)]
        if k == 0:
            outer = rate * (line[0] * 0.5)
        e01, e12, e23 = (rate * ((line[x] + line[x + 1]) * 0.5) for x in range(3))
        one_inv, one_fill, one_upper, two_inv, two_fill, two_slack, two_next = inner_coefs(
            e01, e12, e23, wind
        )
        two_slack = two_slack * two_inv
        q0 = e01 + wind
        own = 1.0 + q0 * (one_inv + one_upper * two_slack)
        if k == 0:
            own = own + outer
            below.append(None)
        else:
            below.append(outer)
        above.append(q0 * (one_upper * (two_next * two_inv)))
        slack.append(own)
        rhs.append(got[pl.ds(k * SEND, 8), :])
        if k < slabs - 1:
            outer = rate * ((line[3] + spread[pl.ds(k + 1, 1), :]) * 0.5)
        else:
            outer = rate * (line[3] * 0.5)
        own = 1.0 + e23 * two_slack
        below.append(e23 * (two_fill * two_inv))
        if k < slabs - 1:
            above.append(outer + wind)
        else:
            own = own + (outer + wind)
            above.append(None)
        slack.append(own)
        rhs.append(got[pl.ds(k * SEND + 8, 8), :])

    def total(i):
        out = slack[i]
        if below[i] is not None:
            out = out + below[i]
        if above[i] is not None:
            out = out + above[i]
        return out

    count = 2 * slabs
    alive = list(range(count))
    removed = []
    while len(alive) > 1:
        gone = alive[1::2]
        stay = alive[0::2]
        normal = {}
        for i in gone:
            inv = inverse(total(i))
            normal[i] = (
                below[i] * inv,
                None if above[i] is None else above[i] * inv,
                slack[i] * inv,
                rhs[i] * inv,
            )
        for n, i in enumerate(stay):
            new_below = new_above = None
            new_slack, new_rhs = slack[i], rhs[i]
            if n > 0:
                nb, na, ns, nr = normal[gone[n - 1]]
                new_slack = new_slack + below[i] * ns
                new_rhs = new_rhs + below[i] * nr
                new_below = below[i] * nb
            if n < len(gone):
                nb, na, ns, nr = normal[gone[n]]
                new_slack = new_slack + above[i] * ns
                new_rhs = new_rhs + above[i] * nr
                new_above = None if na is None else above[i] * na
            below[i], above[i], slack[i], rhs[i] = new_below, new_above, new_slack, new_rhs
        removed.append((alive, normal))
        alive = stay
    solved = {0: rhs[0] * inverse(slack[0])}
    for order, normal in reversed(removed):
        for n in range(1, len(order), 2):
            nb, na, ns, nr = normal[order[n]]
            item = nr + nb * solved[order[n - 1]]
            if na is not None:
                item = item + na * solved[order[n + 1]]
            solved[order[n]] = item
    for k in range(slabs):
        ends[k, pl.ds(0, 8), :] = solved[2 * k]
        ends[k, pl.ds(8, 8), :] = solved[2 * k + 1]


def inner_rows(ends, kept, j):
    first = ends[j, pl.ds(0, 8), :]
    last = ends[j, pl.ds(8, 8), :]
    a1, b1, c1, a2, b2, c2 = (kept[j, pl.ds(n * 8, 8), :] for n in range(6))
    two = a2 + b2 * first + c2 * last
    one = a1 + b1 * first + c1 * two
    return first, one, two, last


def sums_kernel(vectors, window, ends, kept, grad, sorted_ends):
    parts = []
    groups = lane() // 32
    for v in range(8):
        for row in (0, 8):
            items = from_strips([ends[v * 4 + g, pl.ds(row, 8), :] for g in range(4)], groups)
            for zp, item in enumerate(items):
                sorted_ends[v * 4 + zp, pl.ds(row, 8), :] = item
    for v in range(8):
        total = None
        for zp in range(4):
            first, one, two, last = inner_rows(sorted_ends, kept, v * 4 + zp)
            item = vectors[5 + (v // 4) * 4 + zp] * ((first + one) + (two + last))
            total = item if total is None else total + item
        parts.append(jnp.sum(total, axis=0, keepdims=True))
    sums = [jnp.concatenate(parts[f * 4 : f * 4 + 4], axis=1) for f in range(2)]
    pieces = []
    for _ in range(3):
        piece = [item.astype(jnp.bfloat16).astype(F32) for item in sums]
        sums = [item - cut for item, cut in zip(sums, piece)]
        pieces += piece
    pieces = jnp.concatenate(pieces + [jnp.zeros((2, sums[0].shape[1]), F32)], axis=0)
    picked = jnp.dot(pieces.astype(jnp.bfloat16), window[...], preferred_element_type=F32)
    grad[...] = (picked[0:2, :] + picked[2:4, :]) + picked[4:6, :]


def state_kernel(ends, kept, state, lines):
    low = sublane() < 4
    for f in range(2):
        for yb in range(4):
            v = f * 4 + yb
            for zp in range(4):
                for x, item in enumerate(inner_rows(ends, kept, v * 4 + zp)):
                    lines[pl.ds(v * 128 + zp * 32 + x, 8, stride=4), :] = item
        for z in range(8):
            for sp in range(2):
                for h in range(2):
                    base = (f * 4 + 2 * h) * 128 + z * 16 + sp * 8
                    even, odd = pair_halves(
                        lines[pl.ds(base, 8), :], lines[pl.ds(base + 128, 8), :], low
                    )
                    for s, item in ((2 * sp, even), (2 * sp + 1, odd)):
                        state[pl.ds(s * 256 + f * 128 + z * 16 + h * 8, 8), :] = item


def rows_of(block):
    s, f, z, x, y = block.shape
    return block.reshape(s, f, z, x, y // 128, 128).transpose(0, 1, 2, 4, 3, 5).reshape(-1, 128)


def on_device(
    cotangent, scenario_ids, weather, landuse, class_diff, level_scale, emit_profile, building_cells
):
    hbm = pl.BlockSpec(memory_space=pltpu.HBM)
    vmem = pl.BlockSpec(memory_space=pltpu.VMEM)
    params = pltpu.CompilerParams(vmem_limit_bytes=32 * 1024 * 1024)
    slabs = lax.axis_size("tile")
    groups = lax.axis_size("scen")
    width = cotangent.shape[4]
    cells = building_cells.T
    classes = landuse.reshape(4, 4, 128).transpose(1, 0, 2).reshape(16, 128)
    small = (scenario_ids, weather.T, class_diff, level_scale, emit_profile)
    operands = (*small, classes, cells, rows_of(cotangent))
    sent, kept, vectors, window = pl.pallas_call(
        first_kernel,
        out_shape=(
            jax.ShapeDtypeStruct((slabs * SEND, 128), F32),
            jax.ShapeDtypeStruct((slabs, 48, 128), F32),
            jax.ShapeDtypeStruct((13, 8, 128), F32),
            jax.ShapeDtypeStruct((width, cells.shape[1]), jnp.bfloat16),
        ),
        in_specs=[hbm] * 8,
        out_specs=(vmem,) * 4,
        scratch_shapes=[pltpu.SMEM(item.shape, item.dtype) for item in small]
        + [pltpu.VMEM(item.shape, item.dtype) for item in (classes, cells)]
        + [pltpu.VMEM((1024, 128), F32)] * 7
        + [pltpu.VMEM((32, 128), F32), pltpu.SemaphoreType.DMA((9,))],
        compiler_params=params,
    )(*(pltpu.with_memory_space_constraint(item, pltpu.HBM) for item in operands))
    got = lax.all_to_all(sent.reshape(slabs, SEND, 1, 128), "tile", 0, 0).reshape(slabs * SEND, 128)
    ends = pl.pallas_call(
        middle_kernel,
        out_shape=jax.ShapeDtypeStruct((slabs, 16, 128), F32),
        in_specs=[vmem] * 2,
        out_specs=vmem,
        scratch_shapes=[pltpu.VMEM((4 * slabs, 128), F32)],
        compiler_params=params,
    )(vectors, got)
    ends = lax.all_to_all(ends, "tile", 0, 0)
    grad, ends = pl.pallas_call(
        sums_kernel,
        out_shape=(
            jax.ShapeDtypeStruct((2, cells.shape[1]), F32),
            jax.ShapeDtypeStruct((slabs, 16, 128), F32),
        ),
        in_specs=[vmem] * 4,
        out_specs=(vmem, vmem),
        compiler_params=params,
    )(vectors, window, ends, kept)
    state = pl.pallas_call(
        state_kernel,
        out_shape=jax.ShapeDtypeStruct((1024, 128), F32),
        in_specs=[vmem] * 2,
        out_specs=vmem,
        scratch_shapes=[pltpu.VMEM((1024, 128), F32)],
        compiler_params=params,
    )(ends, kept)
    for partner in (
        lambda i: i ^ 1,
        lambda i: i ^ 2,
        lambda i: groups - 2 - i + 2 * (i % 2),
    ):
        grad = grad + lax.ppermute(grad, "scen", [(i, partner(i)) for i in range(groups)])
    state = state.reshape(4, 2, 8, 4, 4, 128).transpose(0, 1, 2, 4, 3, 5).reshape(cotangent.shape)
    return (state, grad)


def solution(mesh):
    placed = (
        P("scen", None, None, "tile", None),
        P("scen"),
        P(),
        P("tile", None),
        P(),
        P(),
        P(),
        P("tile", None),
    )
    return jax.shard_map(
        on_device,
        mesh=mesh,
        in_specs=placed,
        out_specs=(P("scen", None, None, "tile", None), P(None, "tile")),
        check_vma=False,
    )
```

```python
import jax
import jax.numpy as jnp
from jax import lax
from jax.experimental import pallas as pl
from jax.experimental.pallas import tpu as pltpu
from jax.sharding import PartitionSpec as P

F32 = jnp.float32
SEND = 17


def inverse(value):
    return pltpu.reciprocal(value, approx=True)


def sublane():
    return lax.broadcasted_iota(jnp.int32, (8, 128), 0)


def lane():
    return lax.broadcasted_iota(jnp.int32, (8, 128), 1)


def choose(index, values):
    out = jnp.full((8, 128), values[-1], F32)
    for at in range(len(values) - 2, -1, -1):
        out = jnp.where(index == at, values[at], out)
    return out


def surface(classes, class_diff, field):
    out = jnp.zeros((8, 128), F32)
    for mark in range(class_diff.shape[1]):
        out = jnp.where(classes == mark, class_diff[field, mark], out)
    return out


def swap_halves(value):
    return pltpu.roll(value, 4, axis=0)


def pair_halves(first, second, low):
    return (
        jnp.where(low, first, swap_halves(second)),
        jnp.where(low, swap_halves(first), second),
    )


def pick(groups, items):
    out = items[3]
    for at in range(2, -1, -1):
        out = jnp.where(groups == at, items[at], out)
    return out


def to_strips(items, groups):
    turned = [pltpu.roll(item, 32 * m, axis=1) if m else item for m, item in enumerate(items)]
    return [pick(groups, [turned[(p - g) % 4] for p in range(4)]) for g in range(4)]


def from_strips(strips, groups):
    items = [pick(groups, [strips[(p - m) % 4] for p in range(4)]) for m in range(4)]
    return [pltpu.roll(item, 128 - 32 * m, axis=1) if m else item for m, item in enumerate(items)]


def solve_levels(cot, surf, scale, table, out, hold_a, hold_c, low, arrivals):
    half = [(scale[z] + scale[z + 1]) * 0.5 for z in range(7)]
    for pair in range(2):
        arrivals[pair].wait()
        chains = [(s, f, h) for s in (2 * pair, 2 * pair + 1) for f in range(2) for h in range(2)]
        rated = [surf[f][h] * table(s, 2) for s, f, h in chains]
        winds = [table(s, 5) for s, f, h in chains]
        values = [None] * 8
        slacks = [None] * 8
        faces = [None] * 8
        for z in range(8):
            for n, (s, f, h) in enumerate(chains):
                rhs = cot[pl.ds(s * 256 + f * 128 + z * 16 + h * 8, 8), :]
                if z == 0:
                    slack = 1.0 + rated[n] * (scale[0] * 0.5)
                else:
                    slack = 1.0 + faces[n] * slacks[n]
                    rhs = rhs + faces[n] * values[n]
                if z < 7:
                    face = rated[n] * half[z]
                    above = face + winds[n]
                    inv = inverse(above + slack)
                    values[n] = rhs * inv
                    slacks[n] = slack * inv
                    faces[n] = face
                    hold_a[pl.ds((z * 8 + n) * 8, 8), :] = values[n]
                    hold_c[pl.ds((z * 8 + n) * 8, 8), :] = above * inv
                else:
                    slack = slack + (rated[n] * (scale[7] * 0.5) + winds[n])
                    values[n] = rhs * inverse(slack)
        for z in range(7, -1, -1):
            if z < 7:
                for n in range(8):
                    at = pl.ds((z * 8 + n) * 8, 8)
                    values[n] = hold_a[at, :] + hold_c[at, :] * values[n]
            for f in range(2):
                for h in range(2):
                    n = f * 2 + h
                    even, odd = pair_halves(values[n], values[n + 4], low)
                    for yb, item in ((2 * h, even), (2 * h + 1, odd)):
                        out[pl.ds((f * 4 + yb) * 128 + z * 16 + pair * 8, 8), :] = item


def from_before(items, rows, distance):
    turned = [pltpu.roll(item, distance, axis=0) for item in items]
    return [
        turned[v] if v % 4 == 0 else jnp.where(rows < distance, turned[v - 1], turned[v])
        for v in range(8)
    ]


def from_after(items, rows, distance):
    turned = [pltpu.roll(item, 8 - distance, axis=0) for item in items]
    return [
        turned[v] if v % 4 == 3 else jnp.where(rows >= 8 - distance, turned[v + 1], turned[v])
        for v in range(8)
    ]


def solve_chunks(below, above, slack, rhs, rows):
    everyone = range(8)
    for distance in (1, 2, 4, 8, 16):
        inv = [inverse(below[v] + above[v] + slack[v]) for v in everyone]
        nb = [below[v] * inv[v] for v in everyone]
        na = [above[v] * inv[v] for v in everyone]
        ns = [slack[v] * inv[v] for v in everyone]
        nr = [rhs[v] * inv[v] for v in everyone]
        new_slack = list(slack)
        new_rhs = list(rhs)
        if distance < 8:
            pb, ps, pr = (from_before(item, rows, distance) for item in (nb, ns, nr))
            qa, qs, qr = (from_after(item, rows, distance) for item in (na, ns, nr))
            has_before = has_after = [True] * 8
        else:
            jump = distance // 8
            has_before = [v % 4 >= jump for v in everyone]
            has_after = [v % 4 < 4 - jump for v in everyone]
            pb, ps, pr = (
                [item[v - jump] if has_before[v] else None for v in everyone]
                for item in (nb, ns, nr)
            )
            qa, qs, qr = (
                [item[v + jump] if has_after[v] else None for v in everyone]
                for item in (na, ns, nr)
            )
        zero = jnp.zeros((8, 128), F32)
        new_below = [zero] * 8
        new_above = [zero] * 8
        for v in everyone:
            if has_before[v]:
                new_slack[v] = new_slack[v] + below[v] * ps[v]
                new_rhs[v] = new_rhs[v] + below[v] * pr[v]
                new_below[v] = below[v] * pb[v]
            if has_after[v]:
                new_slack[v] = new_slack[v] + above[v] * qs[v]
                new_rhs[v] = new_rhs[v] + above[v] * qr[v]
                new_above[v] = above[v] * qa[v]
        below, above, slack, rhs = new_below, new_above, new_slack, new_rhs
    return [rhs[v] * inverse(slack[v]) for v in everyone]


def solve_rows(turned, faces, leak, rate, wind, hold_a, hold_b, hold_c, rows):
    everyone = range(8)
    depth = 16

    def at(v, i):
        return pl.ds(v * 128 + i, 8, stride=depth)

    def keep(i, v):
        return pl.ds((i * 8 + v) * 8, 8)

    ends = [faces[at(v, depth - 1), :] * rate for v in everyone]
    before = from_before(ends, rows, 1)
    last = ends
    value = [None] * 8
    fill = [None] * 8
    slack = [None] * 8
    for i in range(depth):
        for v in everyone:
            rhs = turned[at(v, i), :]
            face = last[v] if i == depth - 1 else faces[at(v, i), :] * rate
            next_coef = face + wind
            if i == 0:
                link = before[v]
                own = jnp.ones((8, 128), F32)
                if v % 4 == 0:
                    own = jnp.where(rows == 0, 1.0 + leak[v // 4], own)
                    link = jnp.where(rows == 0, 0.0, link)
            else:
                link = before[v] * fill[v]
                own = 1.0 + before[v] * slack[v]
                rhs = rhs + before[v] * value[v]
            if i == depth - 1:
                if v % 4 == 3:
                    own = jnp.where(rows == 7, own + next_coef, own)
                    next_coef = jnp.where(rows == 7, 0.0, next_coef)
                value[v], fill[v], slack[v] = rhs, link, own
                before[v] = next_coef
                continue
            inv = inverse(next_coef + link + own)
            value[v] = rhs * inv
            fill[v] = link * inv
            slack[v] = own * inv
            upper = next_coef * inv
            hold_a[keep(i, v), :] = value[v]
            hold_b[keep(i, v), :] = fill[v]
            hold_c[keep(i, v), :] = upper
            before[v] = face
            if i == 0:
                if v == 0:
                    first_value, first_fill, first_slack, first_next = ([None] * 8 for _ in range(4))
                first_value[v], first_fill[v], first_slack[v], first_next[v] = (
                    value[v],
                    fill[v],
                    slack[v],
                    upper,
                )
            else:
                carry = first_next[v]
                first_value[v] = first_value[v] + carry * value[v]
                first_slack[v] = first_slack[v] + carry * slack[v]
                first_next[v] = carry * upper
    next_value = from_after(first_value, rows, 1)
    next_slack = from_after(first_slack, rows, 1)
    next_next = from_after(first_next, rows, 1)
    above = [before[v] * next_next[v] for v in everyone]
    slack = [slack[v] + before[v] * next_slack[v] for v in everyone]
    rhs = [value[v] + before[v] * next_value[v] for v in everyone]
    current = solve_chunks(fill, above, slack, rhs, rows)
    previous = from_before(current, rows, 1)
    for v in everyone:
        turned[at(v, depth - 1), :] = current[v]
    for i in range(depth - 2, -1, -1):
        for v in everyone:
            item = hold_a[keep(i, v), :] + hold_b[keep(i, v), :] * previous[v]
            current[v] = item + hold_c[keep(i, v), :] * current[v]
            turned[at(v, i), :] = current[v]


def inner_coefs(low_face, mid_face, high_face, wind):
    one_next = mid_face + wind
    one_inv = inverse(low_face + one_next + 1.0)
    one_fill = low_face * one_inv
    one_upper = one_next * one_inv
    two_next = high_face + wind
    two_fill = mid_face * one_fill
    two_slack = 1.0 + mid_face * one_inv
    two_inv = inverse(two_next + two_fill + two_slack)
    return one_inv, one_fill, one_upper, two_inv, two_fill, two_slack, two_next


def first_kernel(
    ids_in, weather_in, class_diff_in, scale_in, emit_in, landuse_in, cells_in, cot_in,
    sent, kept, vectors, window,
    ids, weather, class_diff, scale, emit, landuse, cells, cot,
    levels, turned, faces, hold_a, hold_b, hold_c, surf_rows, done,
):
    small = [
        pltpu.make_async_copy(source, target, done.at[n])
        for n, (source, target) in enumerate(
            (
                (ids_in, ids),
                (weather_in, weather),
                (class_diff_in, class_diff),
                (scale_in, scale),
                (emit_in, emit),
                (landuse_in, landuse),
                (cells_in, cells),
            )
        )
    ]
    halves = [
        pltpu.make_async_copy(
            cot_in.at[pl.ds(n * 512, 512), :], cot.at[pl.ds(n * 512, 512), :], done.at[7 + n]
        )
        for n in range(2)
    ]
    for copy in small + halves:
        copy.start()
    for copy in small:
        copy.wait()
    rows = sublane()
    lanes = lane()
    low = rows < 4

    def table(s, column):
        return weather[column, ids[s]]

    classes = [landuse[pl.ds(0, 8), :], landuse[pl.ds(8, 8), :]]
    surf = [[surface(item, class_diff, f) for item in classes] for f in range(2)]
    rate_y = choose((lanes // 4) % 4, [table(s, 1) for s in range(4)])
    wind_y = choose((lanes // 4) % 4, [table(s, 4) for s in range(4)])
    rate_y = rate_y * choose(lanes // 16, [scale[z] for z in range(8)])
    leak = []
    for f in range(2):
        upper, lower = surf[f]
        surf_rows[pl.ds(f * 16, 8), :] = upper
        surf_rows[pl.ds(f * 16 + 8, 8), :] = lower
        shifted = [pltpu.roll(item, 127, axis=1) for item in (upper, lower)]
        swapped = [swap_halves(item) for item in shifted]
        onward = [
            jnp.where(low, swapped[0], swapped[1]),
            jnp.where(low, swapped[1], 0.0),
        ]
        for h in range(2):
            right = jnp.where(lanes == 127, onward[h], shifted[h])
            face = (surf[f][h] + right) * 0.5
            other = swap_halves(face)
            for yb, item in (
                (2 * h, jnp.where(low, face, other)),
                (2 * h + 1, jnp.where(low, other, face)),
            ):
                tile = jnp.concatenate([item] * 16, axis=0)
                faces[pl.ds((f * 4 + yb) * 128, 128), :] = tile.T
        start = jnp.broadcast_to(upper[:, 0:1], (8, 128))
        start = jnp.where(rows == lanes % 4, start, 0.0)
        start = jnp.broadcast_to(jnp.sum(start, axis=0, keepdims=True), (8, 128))
        leak.append(start * 0.5 * rate_y)

    rate_x = choose(rows % 4, [table(s, 0) for s in range(4)])
    wind_x = choose(rows % 4, [table(s, 3) for s in range(4)])
    scales = [choose(rows // 4, [scale[2 * zp], scale[2 * zp + 1]]) for zp in range(4)]
    groups = lanes // 32
    for g in range(4):
        vectors[g] = rate_x * choose(groups, [scales[(p - g) % 4] for p in range(4)])
    vectors[4] = wind_x
    for f in range(2):
        factor = choose(rows % 4, [table(s, 6 + f) for s in range(4)])
        for zp in range(4):
            vectors[5 + f * 4 + zp] = factor * choose(rows // 4, [emit[2 * zp], emit[2 * zp + 1]])
    for v in range(8):
        line = [surf_rows[pl.ds(v * 4 + x, 1), :] for x in range(4)]
        steps = [(line[x] + line[x + 1]) * 0.5 for x in range(3)]
        for zp in range(4):
            j = v * 4 + zp
            rate = rate_x * scales[zp]
            one_inv, one_fill, one_upper, two_inv, two_fill, two_slack, two_next = inner_coefs(
                *(rate * step for step in steps), wind_x
            )
            for n, item in enumerate(
                (one_inv, one_fill, one_upper, two_inv, two_fill * two_inv, two_next * two_inv)
            ):
                kept[j, pl.ds(n * 8, 8), :] = item
    lines = [surf_rows[pl.ds(x, 8, stride=4), :] for x in range(4)]
    lines = [
        [pltpu.roll(item, 32 * d, axis=1) if d else item for d in range(4)] for item in lines
    ]
    strips = [pick(groups, [lines[x][(x - g) % 4] for x in range(4)]) for g in range(4)]
    for g in range(4):
        for v in range(8):
            sent[pl.ds((v * 4 + g) * SEND + 16, 1), :] = strips[g][v : v + 1, :]
    width = window.shape[0]
    start = jnp.min(cells[...] % width, axis=0, keepdims=True)
    place = lax.broadcasted_iota(jnp.int32, (width, 128), 0)
    window[...] = jnp.where((place >= start) & (place < start + 4), 1.0, 0.0).astype(jnp.bfloat16)

    solve_levels(cot, surf, scale, table, levels, hold_a, hold_c, low, halves)
    for v in range(8):
        block = pl.ds(v * 128, 128)
        turned[block, :] = levels[block, :].T
    solve_rows(turned, faces, leak, rate_y, wind_y, hold_a, hold_b, hold_c, rows)
    for v in range(8):
        block = pl.ds(v * 128, 128)
        levels[block, :] = turned[block, :].T

    for v in range(8):
        line = [surf_rows[pl.ds(v * 4 + x, 1), :] for x in range(4)]
        steps = [(line[x] + line[x + 1]) * 0.5 for x in range(3)]
        firsts, lasts = [], []
        for zp in range(4):
            j = v * 4 + zp
            rate = rate_x * scales[zp]
            e01, e12, e23 = (rate * step for step in steps)
            rhs = [levels[pl.ds(v * 128 + zp * 32 + x, 8, stride=4), :] for x in range(4)]
            one = rhs[1] * kept[j, pl.ds(0, 8), :]
            two = (rhs[2] + e12 * one) * kept[j, pl.ds(24, 8), :]
            one_upper = kept[j, pl.ds(16, 8), :]
            firsts.append(rhs[0] + (e01 + wind_x) * (one + one_upper * two))
            lasts.append(rhs[3] + e23 * two)
            kept[j, pl.ds(0, 8), :] = one
            kept[j, pl.ds(24, 8), :] = two
        for offset, items in ((0, firsts), (8, lasts)):
            for g, item in enumerate(to_strips(items, groups)):
                sent[pl.ds((v * 4 + g) * SEND + offset, 8), :] = item


def middle_kernel(vectors, got, ends, spread):
    groups = lane() // 32
    slabs = ends.shape[0]
    strip = lax.axis_index("tile") % 4
    for q in range(slabs // 8):
        shared = got[pl.ds(q * 8 * SEND + 16, 8, stride=SEND), :]
        turned = [pltpu.roll(shared, 32 * d, axis=1) if d else shared for d in range(4)]
        for x in range(4):
            spread[pl.ds(x * slabs + q * 8, 8), :] = pick(
                groups, [turned[(p - x) % 4] for p in range(4)]
            )
    rate = vectors[strip]
    wind = vectors[4]
    below, above, slack, rhs = [], [], [], []
    line = None
    outer = None
    for k in range(slabs):
        line = [spread[pl.ds(x * slabs + k, 1), :] for x in range(4)]
        if k == 0:
            outer = rate * (line[0] * 0.5)
        e01, e12, e23 = (rate * ((line[x] + line[x + 1]) * 0.5) for x in range(3))
        one_inv, one_fill, one_upper, two_inv, two_fill, two_slack, two_next = inner_coefs(
            e01, e12, e23, wind
        )
        two_slack = two_slack * two_inv
        q0 = e01 + wind
        own = 1.0 + q0 * (one_inv + one_upper * two_slack)
        if k == 0:
            own = own + outer
            below.append(None)
        else:
            below.append(outer)
        above.append(q0 * (one_upper * (two_next * two_inv)))
        slack.append(own)
        rhs.append(got[pl.ds(k * SEND, 8), :])
        if k < slabs - 1:
            outer = rate * ((line[3] + spread[pl.ds(k + 1, 1), :]) * 0.5)
        else:
            outer = rate * (line[3] * 0.5)
        own = 1.0 + e23 * two_slack
        below.append(e23 * (two_fill * two_inv))
        if k < slabs - 1:
            above.append(outer + wind)
        else:
            own = own + (outer + wind)
            above.append(None)
        slack.append(own)
        rhs.append(got[pl.ds(k * SEND + 8, 8), :])

    def total(i):
        out = slack[i]
        if below[i] is not None:
            out = out + below[i]
        if above[i] is not None:
            out = out + above[i]
        return out

    count = 2 * slabs
    alive = list(range(count))
    removed = []
    while len(alive) > 1:
        gone = alive[1::2]
        stay = alive[0::2]
        normal = {}
        for i in gone:
            inv = inverse(total(i))
            normal[i] = (
                below[i] * inv,
                None if above[i] is None else above[i] * inv,
                slack[i] * inv,
                rhs[i] * inv,
            )
        for n, i in enumerate(stay):
            new_below = new_above = None
            new_slack, new_rhs = slack[i], rhs[i]
            if n > 0:
                nb, na, ns, nr = normal[gone[n - 1]]
                new_slack = new_slack + below[i] * ns
                new_rhs = new_rhs + below[i] * nr
                new_below = below[i] * nb
            if n < len(gone):
                nb, na, ns, nr = normal[gone[n]]
                new_slack = new_slack + above[i] * ns
                new_rhs = new_rhs + above[i] * nr
                new_above = None if na is None else above[i] * na
            below[i], above[i], slack[i], rhs[i] = new_below, new_above, new_slack, new_rhs
        removed.append((alive, normal))
        alive = stay
    solved = {0: rhs[0] * inverse(slack[0])}
    for order, normal in reversed(removed):
        for n in range(1, len(order), 2):
            nb, na, ns, nr = normal[order[n]]
            item = nr + nb * solved[order[n - 1]]
            if na is not None:
                item = item + na * solved[order[n + 1]]
            solved[order[n]] = item
    for k in range(slabs):
        ends[k, pl.ds(0, 8), :] = solved[2 * k]
        ends[k, pl.ds(8, 8), :] = solved[2 * k + 1]


def inner_rows(ends, kept, j):
    first = ends[j, pl.ds(0, 8), :]
    last = ends[j, pl.ds(8, 8), :]
    a1, b1, c1, a2, b2, c2 = (kept[j, pl.ds(n * 8, 8), :] for n in range(6))
    two = a2 + b2 * first + c2 * last
    one = a1 + b1 * first + c1 * two
    return first, one, two, last


def sums_kernel(vectors, window, ends, kept, grad, sorted_ends):
    parts = []
    groups = lane() // 32
    for v in range(8):
        for row in (0, 8):
            items = from_strips([ends[v * 4 + g, pl.ds(row, 8), :] for g in range(4)], groups)
            for zp, item in enumerate(items):
                sorted_ends[v * 4 + zp, pl.ds(row, 8), :] = item
    for v in range(8):
        total = None
        for zp in range(4):
            first, one, two, last = inner_rows(sorted_ends, kept, v * 4 + zp)
            item = vectors[5 + (v // 4) * 4 + zp] * ((first + one) + (two + last))
            total = item if total is None else total + item
        parts.append(jnp.sum(total, axis=0, keepdims=True))
    sums = [jnp.concatenate(parts[f * 4 : f * 4 + 4], axis=1) for f in range(2)]
    pieces = []
    for _ in range(3):
        piece = [item.astype(jnp.bfloat16).astype(F32) for item in sums]
        sums = [item - cut for item, cut in zip(sums, piece)]
        pieces += piece
    pieces = jnp.concatenate(pieces + [jnp.zeros((2, sums[0].shape[1]), F32)], axis=0)
    picked = jnp.dot(pieces.astype(jnp.bfloat16), window[...], preferred_element_type=F32)
    grad[...] = (picked[0:2, :] + picked[2:4, :]) + picked[4:6, :]


def state_kernel(ends, kept, state, lines):
    low = sublane() < 4
    for f in range(2):
        for yb in range(4):
            v = f * 4 + yb
            for zp in range(4):
                for x, item in enumerate(inner_rows(ends, kept, v * 4 + zp)):
                    lines[pl.ds(v * 128 + zp * 32 + x, 8, stride=4), :] = item
        for z in range(8):
            for sp in range(2):
                for h in range(2):
                    base = (f * 4 + 2 * h) * 128 + z * 16 + sp * 8
                    even, odd = pair_halves(
                        lines[pl.ds(base, 8), :], lines[pl.ds(base + 128, 8), :], low
                    )
                    for s, item in ((2 * sp, even), (2 * sp + 1, odd)):
                        state[pl.ds(s * 256 + f * 128 + z * 16 + h * 8, 8), :] = item


def rows_of(block):
    s, f, z, x, y = block.shape
    return block.reshape(s, f, z, x, y // 128, 128).transpose(0, 1, 2, 4, 3, 5).reshape(-1, 128)


def on_device(
    cotangent, scenario_ids, weather, landuse, class_diff, level_scale, emit_profile, building_cells
):
    hbm = pl.BlockSpec(memory_space=pltpu.HBM)
    vmem = pl.BlockSpec(memory_space=pltpu.VMEM)
    params = pltpu.CompilerParams(vmem_limit_bytes=32 * 1024 * 1024)
    slabs = lax.axis_size("tile")
    groups = lax.axis_size("scen")
    width = cotangent.shape[4]
    cells = building_cells.T
    classes = landuse.reshape(4, 4, 128).transpose(1, 0, 2).reshape(16, 128)
    small = (scenario_ids, weather.T, class_diff, level_scale, emit_profile)
    operands = (*small, classes, cells, rows_of(cotangent))
    sent, kept, vectors, window = pl.pallas_call(
        first_kernel,
        out_shape=(
            jax.ShapeDtypeStruct((slabs * SEND, 128), F32),
            jax.ShapeDtypeStruct((slabs, 48, 128), F32),
            jax.ShapeDtypeStruct((13, 8, 128), F32),
            jax.ShapeDtypeStruct((width, cells.shape[1]), jnp.bfloat16),
        ),
        in_specs=[hbm] * 8,
        out_specs=(vmem,) * 4,
        scratch_shapes=[pltpu.SMEM(item.shape, item.dtype) for item in small]
        + [pltpu.VMEM(item.shape, item.dtype) for item in (classes, cells)]
        + [pltpu.VMEM((1024, 128), F32)] * 7
        + [pltpu.VMEM((32, 128), F32), pltpu.SemaphoreType.DMA((9,))],
        compiler_params=params,
    )(*(pltpu.with_memory_space_constraint(item, pltpu.HBM) for item in operands))
    got = lax.all_to_all(sent.reshape(slabs, SEND, 1, 128), "tile", 0, 0).reshape(slabs * SEND, 128)
    ends = pl.pallas_call(
        middle_kernel,
        out_shape=jax.ShapeDtypeStruct((slabs, 16, 128), F32),
        in_specs=[vmem] * 2,
        out_specs=vmem,
        scratch_shapes=[pltpu.VMEM((4 * slabs, 128), F32)],
        compiler_params=params,
    )(vectors, got)
    ends = lax.all_to_all(ends, "tile", 0, 0)
    grad, ends = pl.pallas_call(
        sums_kernel,
        out_shape=(
            jax.ShapeDtypeStruct((2, cells.shape[1]), F32),
            jax.ShapeDtypeStruct((slabs, 16, 128), F32),
        ),
        in_specs=[vmem] * 4,
        out_specs=(vmem, vmem),
        compiler_params=params,
    )(vectors, window, ends, kept)
    state = pl.pallas_call(
        state_kernel,
        out_shape=jax.ShapeDtypeStruct((1024, 128), F32),
        in_specs=[vmem] * 2,
        out_specs=vmem,
        scratch_shapes=[pltpu.VMEM((1024, 128), F32)],
        compiler_params=params,
    )(ends, kept)
    grad = grad + lax.ppermute(grad, "scen", [(i, i ^ 1) for i in range(groups)])
    shifted = [
        lax.ppermute(grad, "scen", [(i, i ^ step) for i in range(groups)]) for step in (2, 4, 6)
    ]
    grad = (grad + shifted[0]) + (shifted[1] + shifted[2])
    state = state.reshape(4, 2, 8, 4, 4, 128).transpose(0, 1, 2, 4, 3, 5).reshape(cotangent.shape)
    return (state, grad)


def solution(mesh):
    placed = (
        P("scen", None, None, "tile", None),
        P("scen"),
        P(),
        P("tile", None),
        P(),
        P(),
        P(),
        P("tile", None),
    )
    return jax.shard_map(
        on_device,
        mesh=mesh,
        in_specs=placed,
        out_specs=(P("scen", None, None, "tile", None), P(None, "tile")),
        check_vma=False,
    )
```

```python
import jax
import jax.numpy as jnp
from jax import lax
from jax.experimental import pallas as pl
from jax.experimental.pallas import tpu as pltpu
from jax.sharding import PartitionSpec as P

F32 = jnp.float32
SEND = 17


def inverse(value):
    return pltpu.reciprocal(value, approx=True)


def sublane():
    return lax.broadcasted_iota(jnp.int32, (8, 128), 0)


def lane():
    return lax.broadcasted_iota(jnp.int32, (8, 128), 1)


def choose(index, values):
    out = jnp.full((8, 128), values[-1], F32)
    for at in range(len(values) - 2, -1, -1):
        out = jnp.where(index == at, values[at], out)
    return out


def surface(classes, class_diff, field):
    out = jnp.zeros((8, 128), F32)
    for mark in range(class_diff.shape[1]):
        out = jnp.where(classes == mark, class_diff[field, mark], out)
    return out


def swap_halves(value):
    return pltpu.roll(value, 4, axis=0)


def pair_halves(first, second, low):
    return (
        jnp.where(low, first, swap_halves(second)),
        jnp.where(low, swap_halves(first), second),
    )


def pick(groups, items):
    out = items[3]
    for at in range(2, -1, -1):
        out = jnp.where(groups == at, items[at], out)
    return out


def to_strips(items, groups):
    turned = [pltpu.roll(item, 32 * m, axis=1) if m else item for m, item in enumerate(items)]
    return [pick(groups, [turned[(p - g) % 4] for p in range(4)]) for g in range(4)]


def from_strips(strips, groups):
    items = [pick(groups, [strips[(p - m) % 4] for p in range(4)]) for m in range(4)]
    return [pltpu.roll(item, 128 - 32 * m, axis=1) if m else item for m, item in enumerate(items)]


def solve_levels(cot, surf, scale, table, out, hold_a, hold_c, low, arrivals):
    half = [(scale[z] + scale[z + 1]) * 0.5 for z in range(7)]
    for pair in range(2):
        arrivals[pair].wait()
        chains = [(s, f, h) for s in (2 * pair, 2 * pair + 1) for f in range(2) for h in range(2)]
        rated = [surf[f][h] * table(s, 2) for s, f, h in chains]
        winds = [table(s, 5) for s, f, h in chains]
        values = [None] * 8
        slacks = [None] * 8
        faces = [None] * 8
        for z in range(8):
            for n, (s, f, h) in enumerate(chains):
                rhs = cot[pl.ds(s * 256 + f * 128 + z * 16 + h * 8, 8), :]
                if z == 0:
                    slack = 1.0 + rated[n] * (scale[0] * 0.5)
                else:
                    slack = 1.0 + faces[n] * slacks[n]
                    rhs = rhs + faces[n] * values[n]
                if z < 7:
                    face = rated[n] * half[z]
                    above = face + winds[n]
                    inv = inverse(above + slack)
                    values[n] = rhs * inv
                    slacks[n] = slack * inv
                    faces[n] = face
                    hold_a[pl.ds((z * 8 + n) * 8, 8), :] = values[n]
                    hold_c[pl.ds((z * 8 + n) * 8, 8), :] = above * inv
                else:
                    slack = slack + (rated[n] * (scale[7] * 0.5) + winds[n])
                    values[n] = rhs * inverse(slack)
        for z in range(7, -1, -1):
            if z < 7:
                for n in range(8):
                    at = pl.ds((z * 8 + n) * 8, 8)
                    values[n] = hold_a[at, :] + hold_c[at, :] * values[n]
            for f in range(2):
                for h in range(2):
                    n = f * 2 + h
                    even, odd = pair_halves(values[n], values[n + 4], low)
                    for yb, item in ((2 * h, even), (2 * h + 1, odd)):
                        out[pl.ds((f * 4 + yb) * 128 + z * 16 + pair * 8, 8), :] = item


def from_before(items, rows, distance):
    turned = [pltpu.roll(item, distance, axis=0) for item in items]
    return [
        turned[v] if v % 4 == 0 else jnp.where(rows < distance, turned[v - 1], turned[v])
        for v in range(8)
    ]


def from_after(items, rows, distance):
    turned = [pltpu.roll(item, 8 - distance, axis=0) for item in items]
    return [
        turned[v] if v % 4 == 3 else jnp.where(rows >= 8 - distance, turned[v + 1], turned[v])
        for v in range(8)
    ]


def solve_chunks(below, above, slack, rhs, rows):
    everyone = range(8)
    for distance in (1, 2, 4, 8, 16):
        inv = [inverse(below[v] + above[v] + slack[v]) for v in everyone]
        nb = [below[v] * inv[v] for v in everyone]
        na = [above[v] * inv[v] for v in everyone]
        ns = [slack[v] * inv[v] for v in everyone]
        nr = [rhs[v] * inv[v] for v in everyone]
        new_slack = list(slack)
        new_rhs = list(rhs)
        if distance < 8:
            pb, ps, pr = (from_before(item, rows, distance) for item in (nb, ns, nr))
            qa, qs, qr = (from_after(item, rows, distance) for item in (na, ns, nr))
            has_before = has_after = [True] * 8
        else:
            jump = distance // 8
            has_before = [v % 4 >= jump for v in everyone]
            has_after = [v % 4 < 4 - jump for v in everyone]
            pb, ps, pr = (
                [item[v - jump] if has_before[v] else None for v in everyone]
                for item in (nb, ns, nr)
            )
            qa, qs, qr = (
                [item[v + jump] if has_after[v] else None for v in everyone]
                for item in (na, ns, nr)
            )
        zero = jnp.zeros((8, 128), F32)
        new_below = [zero] * 8
        new_above = [zero] * 8
        for v in everyone:
            if has_before[v]:
                new_slack[v] = new_slack[v] + below[v] * ps[v]
                new_rhs[v] = new_rhs[v] + below[v] * pr[v]
                new_below[v] = below[v] * pb[v]
            if has_after[v]:
                new_slack[v] = new_slack[v] + above[v] * qs[v]
                new_rhs[v] = new_rhs[v] + above[v] * qr[v]
                new_above[v] = above[v] * qa[v]
        below, above, slack, rhs = new_below, new_above, new_slack, new_rhs
    return [rhs[v] * inverse(slack[v]) for v in everyone]


PITCH = 17


def store_turned(target, v, block):
    for n in range(16):
        target[pl.ds(v * 8 * PITCH + n // 2 * PITCH + n % 2 * 8, 8), :] = block[8 * n : 8 * n + 8, :]


def load_turned(source, v):
    return jnp.concatenate(
        [source[pl.ds(v * 8 * PITCH + n // 2 * PITCH + n % 2 * 8, 8), :] for n in range(16)], axis=0
    )


def solve_rows(turned, faces, leak, rate, wind, hold_a, hold_b, hold_c, rows):
    everyone = range(8)
    depth = 16

    def at(v, i):
        return pl.ds(v * 8 * PITCH + i, 8, stride=PITCH)

    def keep(i, v):
        return pl.ds((i * 8 + v) * 8, 8)

    ends = [faces[at(v, depth - 1), :] * rate for v in everyone]
    before = from_before(ends, rows, 1)
    last = ends
    value = [None] * 8
    fill = [None] * 8
    slack = [None] * 8
    for i in range(depth):
        for v in everyone:
            rhs = turned[at(v, i), :]
            face = last[v] if i == depth - 1 else faces[at(v, i), :] * rate
            next_coef = face + wind
            if i == 0:
                link = before[v]
                own = jnp.ones((8, 128), F32)
                if v % 4 == 0:
                    own = jnp.where(rows == 0, 1.0 + leak[v // 4], own)
                    link = jnp.where(rows == 0, 0.0, link)
            else:
                link = before[v] * fill[v]
                own = 1.0 + before[v] * slack[v]
                rhs = rhs + before[v] * value[v]
            if i == depth - 1:
                if v % 4 == 3:
                    own = jnp.where(rows == 7, own + next_coef, own)
                    next_coef = jnp.where(rows == 7, 0.0, next_coef)
                value[v], fill[v], slack[v] = rhs, link, own
                before[v] = next_coef
                continue
            inv = inverse(next_coef + link + own)
            value[v] = rhs * inv
            fill[v] = link * inv
            slack[v] = own * inv
            upper = next_coef * inv
            hold_a[keep(i, v), :] = value[v]
            hold_b[keep(i, v), :] = fill[v]
            hold_c[keep(i, v), :] = upper
            before[v] = face
            if i == 0:
                if v == 0:
                    first_value, first_fill, first_slack, first_next = ([None] * 8 for _ in range(4))
                first_value[v], first_fill[v], first_slack[v], first_next[v] = (
                    value[v],
                    fill[v],
                    slack[v],
                    upper,
                )
            else:
                carry = first_next[v]
                first_value[v] = first_value[v] + carry * value[v]
                first_slack[v] = first_slack[v] + carry * slack[v]
                first_next[v] = carry * upper
    next_value = from_after(first_value, rows, 1)
    next_slack = from_after(first_slack, rows, 1)
    next_next = from_after(first_next, rows, 1)
    above = [before[v] * next_next[v] for v in everyone]
    slack = [slack[v] + before[v] * next_slack[v] for v in everyone]
    rhs = [value[v] + before[v] * next_value[v] for v in everyone]
    current = solve_chunks(fill, above, slack, rhs, rows)
    previous = from_before(current, rows, 1)
    for v in everyone:
        turned[at(v, depth - 1), :] = current[v]
    for i in range(depth - 2, -1, -1):
        for v in everyone:
            item = hold_a[keep(i, v), :] + hold_b[keep(i, v), :] * previous[v]
            current[v] = item + hold_c[keep(i, v), :] * current[v]
            turned[at(v, i), :] = current[v]


def inner_coefs(low_face, mid_face, high_face, wind):
    one_next = mid_face + wind
    one_inv = inverse(low_face + one_next + 1.0)
    one_fill = low_face * one_inv
    one_upper = one_next * one_inv
    two_next = high_face + wind
    two_fill = mid_face * one_fill
    two_slack = 1.0 + mid_face * one_inv
    two_inv = inverse(two_next + two_fill + two_slack)
    return one_inv, one_fill, one_upper, two_inv, two_fill, two_slack, two_next


def first_kernel(
    ids_in, weather_in, class_diff_in, scale_in, emit_in, landuse_in, cells_in, cot_in,
    sent, kept, vectors, window,
    ids, weather, class_diff, scale, emit, landuse, cells, cot,
    levels, turned, faces, hold_a, hold_b, hold_c, surf_rows, done,
):
    small = [
        pltpu.make_async_copy(source, target, done.at[n])
        for n, (source, target) in enumerate(
            (
                (ids_in, ids),
                (weather_in, weather),
                (class_diff_in, class_diff),
                (scale_in, scale),
                (emit_in, emit),
                (landuse_in, landuse),
                (cells_in, cells),
            )
        )
    ]
    halves = [
        pltpu.make_async_copy(
            cot_in.at[pl.ds(n * 512, 512), :], cot.at[pl.ds(n * 512, 512), :], done.at[7 + n]
        )
        for n in range(2)
    ]
    for copy in small + halves:
        copy.start()
    for copy in small:
        copy.wait()
    rows = sublane()
    lanes = lane()
    low = rows < 4

    def table(s, column):
        return weather[column, ids[s]]

    classes = [landuse[pl.ds(0, 8), :], landuse[pl.ds(8, 8), :]]
    surf = [[surface(item, class_diff, f) for item in classes] for f in range(2)]
    rate_y = choose((lanes // 4) % 4, [table(s, 1) for s in range(4)])
    wind_y = choose((lanes // 4) % 4, [table(s, 4) for s in range(4)])
    rate_y = rate_y * choose(lanes // 16, [scale[z] for z in range(8)])
    leak = []
    for f in range(2):
        upper, lower = surf[f]
        surf_rows[pl.ds(f * 16, 8), :] = upper
        surf_rows[pl.ds(f * 16 + 8, 8), :] = lower
        shifted = [pltpu.roll(item, 127, axis=1) for item in (upper, lower)]
        swapped = [swap_halves(item) for item in shifted]
        onward = [
            jnp.where(low, swapped[0], swapped[1]),
            jnp.where(low, swapped[1], 0.0),
        ]
        for h in range(2):
            right = jnp.where(lanes == 127, onward[h], shifted[h])
            face = (surf[f][h] + right) * 0.5
            other = swap_halves(face)
            for yb, item in (
                (2 * h, jnp.where(low, face, other)),
                (2 * h + 1, jnp.where(low, other, face)),
            ):
                tile = jnp.concatenate([item] * 16, axis=0)
                store_turned(faces, f * 4 + yb, tile.T)
        start = jnp.broadcast_to(upper[:, 0:1], (8, 128))
        start = jnp.where(rows == lanes % 4, start, 0.0)
        start = jnp.broadcast_to(jnp.sum(start, axis=0, keepdims=True), (8, 128))
        leak.append(start * 0.5 * rate_y)

    rate_x = choose(rows % 4, [table(s, 0) for s in range(4)])
    wind_x = choose(rows % 4, [table(s, 3) for s in range(4)])
    scales = [choose(rows // 4, [scale[2 * zp], scale[2 * zp + 1]]) for zp in range(4)]
    groups = lanes // 32
    for g in range(4):
        vectors[g] = rate_x * choose(groups, [scales[(p - g) % 4] for p in range(4)])
    vectors[4] = wind_x
    for f in range(2):
        factor = choose(rows % 4, [table(s, 6 + f) for s in range(4)])
        for zp in range(4):
            vectors[5 + f * 4 + zp] = factor * choose(rows // 4, [emit[2 * zp], emit[2 * zp + 1]])
    for v in range(8):
        line = [surf_rows[pl.ds(v * 4 + x, 1), :] for x in range(4)]
        steps = [(line[x] + line[x + 1]) * 0.5 for x in range(3)]
        for zp in range(4):
            j = v * 4 + zp
            rate = rate_x * scales[zp]
            one_inv, one_fill, one_upper, two_inv, two_fill, two_slack, two_next = inner_coefs(
                *(rate * step for step in steps), wind_x
            )
            for n, item in enumerate(
                (one_inv, one_fill, one_upper, two_inv, two_fill * two_inv, two_next * two_inv)
            ):
                kept[j, pl.ds(n * 8, 8), :] = item
    lines = [surf_rows[pl.ds(x, 8, stride=4), :] for x in range(4)]
    lines = [
        [pltpu.roll(item, 32 * d, axis=1) if d else item for d in range(4)] for item in lines
    ]
    strips = [pick(groups, [lines[x][(x - g) % 4] for x in range(4)]) for g in range(4)]
    for g in range(4):
        for v in range(8):
            sent[pl.ds((v * 4 + g) * SEND + 16, 1), :] = strips[g][v : v + 1, :]
    width = window.shape[0]
    start = jnp.min(cells[...] % width, axis=0, keepdims=True)
    place = lax.broadcasted_iota(jnp.int32, (width, 128), 0)
    window[...] = jnp.where((place >= start) & (place < start + 4), 1.0, 0.0).astype(jnp.bfloat16)

    solve_levels(cot, surf, scale, table, levels, hold_a, hold_c, low, halves)
    for v in range(8):
        store_turned(turned, v, levels[pl.ds(v * 128, 128), :].T)
    solve_rows(turned, faces, leak, rate_y, wind_y, hold_a, hold_b, hold_c, rows)
    for v in range(8):
        levels[pl.ds(v * 128, 128), :] = load_turned(turned, v).T

    for v in range(8):
        line = [surf_rows[pl.ds(v * 4 + x, 1), :] for x in range(4)]
        steps = [(line[x] + line[x + 1]) * 0.5 for x in range(3)]
        firsts, lasts = [], []
        for zp in range(4):
            j = v * 4 + zp
            rate = rate_x * scales[zp]
            e01, e12, e23 = (rate * step for step in steps)
            rhs = [levels[pl.ds(v * 128 + zp * 32 + x, 8, stride=4), :] for x in range(4)]
            one = rhs[1] * kept[j, pl.ds(0, 8), :]
            two = (rhs[2] + e12 * one) * kept[j, pl.ds(24, 8), :]
            one_upper = kept[j, pl.ds(16, 8), :]
            firsts.append(rhs[0] + (e01 + wind_x) * (one + one_upper * two))
            lasts.append(rhs[3] + e23 * two)
            kept[j, pl.ds(0, 8), :] = one
            kept[j, pl.ds(24, 8), :] = two
        for offset, items in ((0, firsts), (8, lasts)):
            for g, item in enumerate(to_strips(items, groups)):
                sent[pl.ds((v * 4 + g) * SEND + offset, 8), :] = item


def middle_kernel(vectors, got, ends, spread):
    groups = lane() // 32
    slabs = ends.shape[0]
    strip = lax.axis_index("tile") % 4
    for q in range(slabs // 8):
        shared = got[pl.ds(q * 8 * SEND + 16, 8, stride=SEND), :]
        turned = [pltpu.roll(shared, 32 * d, axis=1) if d else shared for d in range(4)]
        for x in range(4):
            spread[pl.ds(x * slabs + q * 8, 8), :] = pick(
                groups, [turned[(p - x) % 4] for p in range(4)]
            )
    rate = vectors[strip]
    wind = vectors[4]
    below, above, slack, rhs = [], [], [], []
    line = None
    outer = None
    for k in range(slabs):
        line = [spread[pl.ds(x * slabs + k, 1), :] for x in range(4)]
        if k == 0:
            outer = rate * (line[0] * 0.5)
        e01, e12, e23 = (rate * ((line[x] + line[x + 1]) * 0.5) for x in range(3))
        one_inv, one_fill, one_upper, two_inv, two_fill, two_slack, two_next = inner_coefs(
            e01, e12, e23, wind
        )
        two_slack = two_slack * two_inv
        q0 = e01 + wind
        own = 1.0 + q0 * (one_inv + one_upper * two_slack)
        if k == 0:
            own = own + outer
            below.append(None)
        else:
            below.append(outer)
        above.append(q0 * (one_upper * (two_next * two_inv)))
        slack.append(own)
        rhs.append(got[pl.ds(k * SEND, 8), :])
        if k < slabs - 1:
            outer = rate * ((line[3] + spread[pl.ds(k + 1, 1), :]) * 0.5)
        else:
            outer = rate * (line[3] * 0.5)
        own = 1.0 + e23 * two_slack
        below.append(e23 * (two_fill * two_inv))
        if k < slabs - 1:
            above.append(outer + wind)
        else:
            own = own + (outer + wind)
            above.append(None)
        slack.append(own)
        rhs.append(got[pl.ds(k * SEND + 8, 8), :])

    def total(i):
        out = slack[i]
        if below[i] is not None:
            out = out + below[i]
        if above[i] is not None:
            out = out + above[i]
        return out

    count = 2 * slabs
    alive = list(range(count))
    removed = []
    while len(alive) > 1:
        gone = alive[1::2]
        stay = alive[0::2]
        normal = {}
        for i in gone:
            inv = inverse(total(i))
            normal[i] = (
                below[i] * inv,
                None if above[i] is None else above[i] * inv,
                slack[i] * inv,
                rhs[i] * inv,
            )
        for n, i in enumerate(stay):
            new_below = new_above = None
            new_slack, new_rhs = slack[i], rhs[i]
            if n > 0:
                nb, na, ns, nr = normal[gone[n - 1]]
                new_slack = new_slack + below[i] * ns
                new_rhs = new_rhs + below[i] * nr
                new_below = below[i] * nb
            if n < len(gone):
                nb, na, ns, nr = normal[gone[n]]
                new_slack = new_slack + above[i] * ns
                new_rhs = new_rhs + above[i] * nr
                new_above = None if na is None else above[i] * na
            below[i], above[i], slack[i], rhs[i] = new_below, new_above, new_slack, new_rhs
        removed.append((alive, normal))
        alive = stay
    solved = {0: rhs[0] * inverse(slack[0])}
    for order, normal in reversed(removed):
        for n in range(1, len(order), 2):
            nb, na, ns, nr = normal[order[n]]
            item = nr + nb * solved[order[n - 1]]
            if na is not None:
                item = item + na * solved[order[n + 1]]
            solved[order[n]] = item
    for k in range(slabs):
        ends[k, pl.ds(0, 8), :] = solved[2 * k]
        ends[k, pl.ds(8, 8), :] = solved[2 * k + 1]


def inner_rows(ends, kept, j):
    first = ends[j, pl.ds(0, 8), :]
    last = ends[j, pl.ds(8, 8), :]
    a1, b1, c1, a2, b2, c2 = (kept[j, pl.ds(n * 8, 8), :] for n in range(6))
    two = a2 + b2 * first + c2 * last
    one = a1 + b1 * first + c1 * two
    return first, one, two, last


def sums_kernel(vectors, window, ends, kept, grad, sorted_ends):
    parts = []
    groups = lane() // 32
    for v in range(8):
        for row in (0, 8):
            items = from_strips([ends[v * 4 + g, pl.ds(row, 8), :] for g in range(4)], groups)
            for zp, item in enumerate(items):
                sorted_ends[v * 4 + zp, pl.ds(row, 8), :] = item
    for v in range(8):
        total = None
        for zp in range(4):
            first, one, two, last = inner_rows(sorted_ends, kept, v * 4 + zp)
            item = vectors[5 + (v // 4) * 4 + zp] * ((first + one) + (two + last))
            total = item if total is None else total + item
        parts.append(jnp.sum(total, axis=0, keepdims=True))
    sums = [jnp.concatenate(parts[f * 4 : f * 4 + 4], axis=1) for f in range(2)]
    pieces = []
    for _ in range(3):
        piece = [item.astype(jnp.bfloat16).astype(F32) for item in sums]
        sums = [item - cut for item, cut in zip(sums, piece)]
        pieces += piece
    pieces = jnp.concatenate(pieces + [jnp.zeros((2, sums[0].shape[1]), F32)], axis=0)
    picked = jnp.dot(pieces.astype(jnp.bfloat16), window[...], preferred_element_type=F32)
    grad[...] = (picked[0:2, :] + picked[2:4, :]) + picked[4:6, :]


def state_kernel(ends, kept, state, lines):
    low = sublane() < 4
    for f in range(2):
        for yb in range(4):
            v = f * 4 + yb
            for zp in range(4):
                for x, item in enumerate(inner_rows(ends, kept, v * 4 + zp)):
                    lines[pl.ds(v * 128 + zp * 32 + x, 8, stride=4), :] = item
        for z in range(8):
            for sp in range(2):
                for h in range(2):
                    base = (f * 4 + 2 * h) * 128 + z * 16 + sp * 8
                    even, odd = pair_halves(
                        lines[pl.ds(base, 8), :], lines[pl.ds(base + 128, 8), :], low
                    )
                    for s, item in ((2 * sp, even), (2 * sp + 1, odd)):
                        state[pl.ds(s * 256 + f * 128 + z * 16 + h * 8, 8), :] = item


def rows_of(block):
    s, f, z, x, y = block.shape
    return block.reshape(s, f, z, x, y // 128, 128).transpose(0, 1, 2, 4, 3, 5).reshape(-1, 128)


def on_device(
    cotangent, scenario_ids, weather, landuse, class_diff, level_scale, emit_profile, building_cells
):
    hbm = pl.BlockSpec(memory_space=pltpu.HBM)
    vmem = pl.BlockSpec(memory_space=pltpu.VMEM)
    params = pltpu.CompilerParams(vmem_limit_bytes=32 * 1024 * 1024)
    slabs = lax.axis_size("tile")
    groups = lax.axis_size("scen")
    width = cotangent.shape[4]
    cells = building_cells.T
    classes = landuse.reshape(4, 4, 128).transpose(1, 0, 2).reshape(16, 128)
    small = (scenario_ids, weather.T, class_diff, level_scale, emit_profile)
    operands = (*small, classes, cells, rows_of(cotangent))
    sent, kept, vectors, window = pl.pallas_call(
        first_kernel,
        out_shape=(
            jax.ShapeDtypeStruct((slabs * SEND, 128), F32),
            jax.ShapeDtypeStruct((slabs, 48, 128), F32),
            jax.ShapeDtypeStruct((13, 8, 128), F32),
            jax.ShapeDtypeStruct((width, cells.shape[1]), jnp.bfloat16),
        ),
        in_specs=[hbm] * 8,
        out_specs=(vmem,) * 4,
        scratch_shapes=[pltpu.SMEM(item.shape, item.dtype) for item in small]
        + [pltpu.VMEM(item.shape, item.dtype) for item in (classes, cells)]
        + [pltpu.VMEM((1024, 128), F32)] * 2
        + [pltpu.VMEM((64 * PITCH, 128), F32)] * 2
        + [pltpu.VMEM((1024, 128), F32)] * 3
        + [pltpu.VMEM((32, 128), F32), pltpu.SemaphoreType.DMA((9,))],
        compiler_params=params,
    )(*(pltpu.with_memory_space_constraint(item, pltpu.HBM) for item in operands))
    got = lax.all_to_all(sent.reshape(slabs, SEND, 1, 128), "tile", 0, 0).reshape(slabs * SEND, 128)
    ends = pl.pallas_call(
        middle_kernel,
        out_shape=jax.ShapeDtypeStruct((slabs, 16, 128), F32),
        in_specs=[vmem] * 2,
        out_specs=vmem,
        scratch_shapes=[pltpu.VMEM((4 * slabs, 128), F32)],
        compiler_params=params,
    )(vectors, got)
    ends = lax.all_to_all(ends, "tile", 0, 0)
    grad, ends = pl.pallas_call(
        sums_kernel,
        out_shape=(
            jax.ShapeDtypeStruct((2, cells.shape[1]), F32),
            jax.ShapeDtypeStruct((slabs, 16, 128), F32),
        ),
        in_specs=[vmem] * 4,
        out_specs=(vmem, vmem),
        compiler_params=params,
    )(vectors, window, ends, kept)
    state = pl.pallas_call(
        state_kernel,
        out_shape=jax.ShapeDtypeStruct((1024, 128), F32),
        in_specs=[vmem] * 2,
        out_specs=vmem,
        scratch_shapes=[pltpu.VMEM((1024, 128), F32)],
        compiler_params=params,
    )(ends, kept)
    grad = grad + lax.ppermute(grad, "scen", [(i, i ^ 1) for i in range(groups)])
    shifted = [
        lax.ppermute(grad, "scen", [(i, i ^ step) for i in range(groups)]) for step in (2, 4, 6)
    ]
    grad = (grad + shifted[0]) + (shifted[1] + shifted[2])
    state = state.reshape(4, 2, 8, 4, 4, 128).transpose(0, 1, 2, 4, 3, 5).reshape(cotangent.shape)
    return (state, grad)


def solution(mesh):
    placed = (
        P("scen", None, None, "tile", None),
        P("scen"),
        P(),
        P("tile", None),
        P(),
        P(),
        P(),
        P("tile", None),
    )
    return jax.shard_map(
        on_device,
        mesh=mesh,
        in_specs=placed,
        out_specs=(P("scen", None, None, "tile", None), P(None, "tile")),
        check_vma=False,
    )
```

```python
import jax
import jax.numpy as jnp
from jax import lax
from jax.experimental import pallas as pl
from jax.experimental.pallas import tpu as pltpu
from jax.sharding import PartitionSpec as P

F32 = jnp.float32
SEND = 17


def inverse(value):
    return pltpu.reciprocal(value, approx=True)


def sublane():
    return lax.broadcasted_iota(jnp.int32, (8, 128), 0)


def lane():
    return lax.broadcasted_iota(jnp.int32, (8, 128), 1)


def choose(index, values):
    out = jnp.full((8, 128), values[-1], F32)
    for at in range(len(values) - 2, -1, -1):
        out = jnp.where(index == at, values[at], out)
    return out


def surface(classes, class_diff, field):
    out = jnp.zeros((8, 128), F32)
    for mark in range(class_diff.shape[1]):
        out = jnp.where(classes == mark, class_diff[field, mark], out)
    return out


def swap_halves(value):
    return pltpu.roll(value, 4, axis=0)


def pair_halves(first, second, low):
    return (
        jnp.where(low, first, swap_halves(second)),
        jnp.where(low, swap_halves(first), second),
    )


def pick(groups, items):
    out = items[3]
    for at in range(2, -1, -1):
        out = jnp.where(groups == at, items[at], out)
    return out


def to_strips(items, groups):
    turned = [pltpu.roll(item, 32 * m, axis=1) if m else item for m, item in enumerate(items)]
    return [pick(groups, [turned[(p - g) % 4] for p in range(4)]) for g in range(4)]


def from_strips(strips, groups):
    items = [pick(groups, [strips[(p - m) % 4] for p in range(4)]) for m in range(4)]
    return [pltpu.roll(item, 128 - 32 * m, axis=1) if m else item for m, item in enumerate(items)]


def solve_levels(cot, surf, scale, table, out, hold_a, hold_c, low, arrivals):
    half = [(scale[z] + scale[z + 1]) * 0.5 for z in range(7)]
    for pair in range(2):
        arrivals[pair].wait()
        chains = [(s, f, h) for s in (2 * pair, 2 * pair + 1) for f in range(2) for h in range(2)]
        rated = [surf[f][h] * table(s, 2) for s, f, h in chains]
        winds = [table(s, 5) for s, f, h in chains]
        values = [None] * 8
        slacks = [None] * 8
        faces = [None] * 8
        for z in range(8):
            for n, (s, f, h) in enumerate(chains):
                rhs = cot[pl.ds(s * 256 + f * 128 + z * 16 + h * 8, 8), :]
                if z == 0:
                    slack = 1.0 + rated[n] * (scale[0] * 0.5)
                else:
                    slack = 1.0 + faces[n] * slacks[n]
                    rhs = rhs + faces[n] * values[n]
                if z < 7:
                    face = rated[n] * half[z]
                    above = face + winds[n]
                    inv = inverse(above + slack)
                    values[n] = rhs * inv
                    slacks[n] = slack * inv
                    faces[n] = face
                    hold_a[pl.ds((z * 8 + n) * 8, 8), :] = values[n]
                    hold_c[pl.ds((z * 8 + n) * 8, 8), :] = above * inv
                else:
                    slack = slack + (rated[n] * (scale[7] * 0.5) + winds[n])
                    values[n] = rhs * inverse(slack)
        for z in range(7, -1, -1):
            if z < 7:
                for n in range(8):
                    at = pl.ds((z * 8 + n) * 8, 8)
                    values[n] = hold_a[at, :] + hold_c[at, :] * values[n]
            for f in range(2):
                for h in range(2):
                    n = f * 2 + h
                    even, odd = pair_halves(values[n], values[n + 4], low)
                    for yb, item in ((2 * h, even), (2 * h + 1, odd)):
                        out[pl.ds((f * 4 + yb) * 128 + z * 16 + pair * 8, 8), :] = item


def from_before(items, rows, distance):
    turned = [pltpu.roll(item, distance, axis=0) for item in items]
    return [
        turned[v] if v % 4 == 0 else jnp.where(rows < distance, turned[v - 1], turned[v])
        for v in range(8)
    ]


def from_after(items, rows, distance):
    turned = [pltpu.roll(item, 8 - distance, axis=0) for item in items]
    return [
        turned[v] if v % 4 == 3 else jnp.where(rows >= 8 - distance, turned[v + 1], turned[v])
        for v in range(8)
    ]


def solve_chunks(below, above, slack, rhs, rows):
    everyone = range(8)
    for distance in (1, 2, 4, 8, 16):
        inv = [inverse(below[v] + above[v] + slack[v]) for v in everyone]
        nb = [below[v] * inv[v] for v in everyone]
        na = [above[v] * inv[v] for v in everyone]
        ns = [slack[v] * inv[v] for v in everyone]
        nr = [rhs[v] * inv[v] for v in everyone]
        new_slack = list(slack)
        new_rhs = list(rhs)
        if distance < 8:
            pb, ps, pr = (from_before(item, rows, distance) for item in (nb, ns, nr))
            qa, qs, qr = (from_after(item, rows, distance) for item in (na, ns, nr))
            has_before = has_after = [True] * 8
        else:
            jump = distance // 8
            has_before = [v % 4 >= jump for v in everyone]
            has_after = [v % 4 < 4 - jump for v in everyone]
            pb, ps, pr = (
                [item[v - jump] if has_before[v] else None for v in everyone]
                for item in (nb, ns, nr)
            )
            qa, qs, qr = (
                [item[v + jump] if has_after[v] else None for v in everyone]
                for item in (na, ns, nr)
            )
        zero = jnp.zeros((8, 128), F32)
        new_below = [zero] * 8
        new_above = [zero] * 8
        for v in everyone:
            if has_before[v]:
                new_slack[v] = new_slack[v] + below[v] * ps[v]
                new_rhs[v] = new_rhs[v] + below[v] * pr[v]
                new_below[v] = below[v] * pb[v]
            if has_after[v]:
                new_slack[v] = new_slack[v] + above[v] * qs[v]
                new_rhs[v] = new_rhs[v] + above[v] * qr[v]
                new_above[v] = above[v] * qa[v]
        below, above, slack, rhs = new_below, new_above, new_slack, new_rhs
    return [rhs[v] * inverse(slack[v]) for v in everyone]


PITCH = 17


def store_turned(target, v, block):
    for n in range(16):
        target[pl.ds(v * 8 * PITCH + n // 2 * PITCH + n % 2 * 8, 8), :] = block[8 * n : 8 * n + 8, :]


def load_turned(source, v):
    return jnp.concatenate(
        [source[pl.ds(v * 8 * PITCH + n // 2 * PITCH + n % 2 * 8, 8), :] for n in range(16)], axis=0
    )


def solve_rows(turned, faces, leak, rate, wind, hold_a, hold_b, hold_c, rows):
    everyone = range(8)
    depth = 16

    def at(v, i):
        return pl.ds(v * 8 * PITCH + i, 8, stride=PITCH)

    def keep(i, v):
        return pl.ds((i * 8 + v) * 8, 8)

    ends = [faces[at(v, depth - 1), :] * rate for v in everyone]
    before = from_before(ends, rows, 1)
    last = ends
    value = [None] * 8
    fill = [None] * 8
    slack = [None] * 8
    for i in range(depth):
        for v in everyone:
            rhs = turned[at(v, i), :]
            face = last[v] if i == depth - 1 else faces[at(v, i), :] * rate
            next_coef = face + wind
            if i == 0:
                link = before[v]
                own = jnp.ones((8, 128), F32)
                if v % 4 == 0:
                    own = jnp.where(rows == 0, 1.0 + leak[v // 4], own)
                    link = jnp.where(rows == 0, 0.0, link)
            else:
                link = before[v] * fill[v]
                own = 1.0 + before[v] * slack[v]
                rhs = rhs + before[v] * value[v]
            if i == depth - 1:
                if v % 4 == 3:
                    own = jnp.where(rows == 7, own + next_coef, own)
                    next_coef = jnp.where(rows == 7, 0.0, next_coef)
                value[v], fill[v], slack[v] = rhs, link, own
                before[v] = next_coef
                continue
            inv = inverse(next_coef + link + own)
            value[v] = rhs * inv
            fill[v] = link * inv
            slack[v] = own * inv
            upper = next_coef * inv
            hold_a[keep(i, v), :] = value[v]
            hold_b[keep(i, v), :] = fill[v]
            hold_c[keep(i, v), :] = upper
            before[v] = face
            if i == 0:
                if v == 0:
                    first_value, first_fill, first_slack, first_next = ([None] * 8 for _ in range(4))
                first_value[v], first_fill[v], first_slack[v], first_next[v] = (
                    value[v],
                    fill[v],
                    slack[v],
                    upper,
                )
            else:
                carry = first_next[v]
                first_value[v] = first_value[v] + carry * value[v]
                first_slack[v] = first_slack[v] + carry * slack[v]
                first_next[v] = carry * upper
    next_value = from_after(first_value, rows, 1)
    next_slack = from_after(first_slack, rows, 1)
    next_next = from_after(first_next, rows, 1)
    above = [before[v] * next_next[v] for v in everyone]
    slack = [slack[v] + before[v] * next_slack[v] for v in everyone]
    rhs = [value[v] + before[v] * next_value[v] for v in everyone]
    current = solve_chunks(fill, above, slack, rhs, rows)
    previous = from_before(current, rows, 1)
    for v in everyone:
        turned[at(v, depth - 1), :] = current[v]
    for i in range(depth - 2, -1, -1):
        for v in everyone:
            item = hold_a[keep(i, v), :] + hold_b[keep(i, v), :] * previous[v]
            current[v] = item + hold_c[keep(i, v), :] * current[v]
            turned[at(v, i), :] = current[v]


def inner_coefs(low_face, mid_face, high_face, wind):
    one_next = mid_face + wind
    one_inv = inverse(low_face + one_next + 1.0)
    one_fill = low_face * one_inv
    one_upper = one_next * one_inv
    two_next = high_face + wind
    two_fill = mid_face * one_fill
    two_slack = 1.0 + mid_face * one_inv
    two_inv = inverse(two_next + two_fill + two_slack)
    return one_inv, one_fill, one_upper, two_inv, two_fill, two_slack, two_next


def first_kernel(
    ids_in, weather_in, class_diff_in, scale_in, emit_in, landuse_in, cells_in, cot_in,
    sent, kept, vectors, window,
    ids, weather, class_diff, scale, emit, landuse, cells, cot,
    levels, turned, faces, hold_a, hold_b, hold_c, surf_rows, done,
):
    small = [
        pltpu.make_async_copy(source, target, done.at[n])
        for n, (source, target) in enumerate(
            (
                (ids_in, ids),
                (weather_in, weather),
                (class_diff_in, class_diff),
                (scale_in, scale),
                (emit_in, emit),
                (landuse_in, landuse),
                (cells_in, cells),
            )
        )
    ]
    halves = [
        pltpu.make_async_copy(
            cot_in.at[pl.ds(n * 512, 512), :], cot.at[pl.ds(n * 512, 512), :], done.at[7 + n]
        )
        for n in range(2)
    ]
    for copy in small + halves:
        copy.start()
    for copy in small:
        copy.wait()
    rows = sublane()
    lanes = lane()
    low = rows < 4

    def table(s, column):
        return weather[column, ids[s]]

    classes = [landuse[pl.ds(0, 8), :], landuse[pl.ds(8, 8), :]]
    surf = [[surface(item, class_diff, f) for item in classes] for f in range(2)]
    rate_y = choose((lanes // 4) % 4, [table(s, 1) for s in range(4)])
    wind_y = choose((lanes // 4) % 4, [table(s, 4) for s in range(4)])
    rate_y = rate_y * choose(lanes // 16, [scale[z] for z in range(8)])
    leak = []
    for f in range(2):
        upper, lower = surf[f]
        surf_rows[pl.ds(f * 16, 8), :] = upper
        surf_rows[pl.ds(f * 16 + 8, 8), :] = lower
        shifted = [pltpu.roll(item, 127, axis=1) for item in (upper, lower)]
        swapped = [swap_halves(item) for item in shifted]
        onward = [
            jnp.where(low, swapped[0], swapped[1]),
            jnp.where(low, swapped[1], 0.0),
        ]
        for h in range(2):
            right = jnp.where(lanes == 127, onward[h], shifted[h])
            face = (surf[f][h] + right) * 0.5
            other = swap_halves(face)
            for yb, item in (
                (2 * h, jnp.where(low, face, other)),
                (2 * h + 1, jnp.where(low, other, face)),
            ):
                tile = jnp.concatenate([item] * 16, axis=0)
                store_turned(faces, f * 4 + yb, tile.T)
        start = jnp.broadcast_to(upper[:, 0:1], (8, 128))
        start = jnp.where(rows == lanes % 4, start, 0.0)
        start = jnp.broadcast_to(jnp.sum(start, axis=0, keepdims=True), (8, 128))
        leak.append(start * 0.5 * rate_y)

    rate_x = choose(rows % 4, [table(s, 0) for s in range(4)])
    wind_x = choose(rows % 4, [table(s, 3) for s in range(4)])
    scales = [choose(rows // 4, [scale[2 * zp], scale[2 * zp + 1]]) for zp in range(4)]
    groups = lanes // 32
    for g in range(4):
        vectors[g] = rate_x * choose(groups, [scales[(p - g) % 4] for p in range(4)])
    vectors[4] = wind_x
    for f in range(2):
        factor = choose(rows % 4, [table(s, 6 + f) for s in range(4)])
        for zp in range(4):
            vectors[5 + f * 4 + zp] = factor * choose(rows // 4, [emit[2 * zp], emit[2 * zp + 1]])
    for v in range(8):
        line = [surf_rows[pl.ds(v * 4 + x, 1), :] for x in range(4)]
        steps = [(line[x] + line[x + 1]) * 0.5 for x in range(3)]
        for zp in range(4):
            j = v * 4 + zp
            rate = rate_x * scales[zp]
            one_inv, one_fill, one_upper, two_inv, two_fill, two_slack, two_next = inner_coefs(
                *(rate * step for step in steps), wind_x
            )
            for n, item in enumerate(
                (one_inv, one_fill, one_upper, two_inv, two_fill * two_inv, two_next * two_inv)
            ):
                kept[j, pl.ds(n * 8, 8), :] = item
    lines = [surf_rows[pl.ds(x, 8, stride=4), :] for x in range(4)]
    lines = [
        [pltpu.roll(item, 32 * d, axis=1) if d else item for d in range(4)] for item in lines
    ]
    strips = [pick(groups, [lines[x][(x - g) % 4] for x in range(4)]) for g in range(4)]
    for g in range(4):
        for v in range(8):
            sent[pl.ds((v * 4 + g) * SEND + 16, 1), :] = strips[g][v : v + 1, :]
    width = window.shape[0]
    start = jnp.min(cells[...] % width, axis=0, keepdims=True)
    place = lax.broadcasted_iota(jnp.int32, (width, 128), 0)
    window[...] = jnp.where((place >= start) & (place < start + 4), 1.0, 0.0).astype(jnp.bfloat16)

    solve_levels(cot, surf, scale, table, levels, hold_a, hold_c, low, halves)
    for v in range(8):
        store_turned(turned, v, levels[pl.ds(v * 128, 128), :].T)
    solve_rows(turned, faces, leak, rate_y, wind_y, hold_a, hold_b, hold_c, rows)
    for v in range(8):
        levels[pl.ds(v * 128, 128), :] = load_turned(turned, v).T

    for v in range(8):
        line = [surf_rows[pl.ds(v * 4 + x, 1), :] for x in range(4)]
        steps = [(line[x] + line[x + 1]) * 0.5 for x in range(3)]
        firsts, lasts = [], []
        for zp in range(4):
            j = v * 4 + zp
            rate = rate_x * scales[zp]
            e01, e12, e23 = (rate * step for step in steps)
            rhs = [levels[pl.ds(v * 128 + zp * 32 + x, 8, stride=4), :] for x in range(4)]
            one = rhs[1] * kept[j, pl.ds(0, 8), :]
            two = (rhs[2] + e12 * one) * kept[j, pl.ds(24, 8), :]
            one_upper = kept[j, pl.ds(16, 8), :]
            firsts.append(rhs[0] + (e01 + wind_x) * (one + one_upper * two))
            lasts.append(rhs[3] + e23 * two)
            kept[j, pl.ds(0, 8), :] = one
            kept[j, pl.ds(24, 8), :] = two
        for offset, items in ((0, firsts), (8, lasts)):
            for g, item in enumerate(to_strips(items, groups)):
                sent[pl.ds((v * 4 + g) * SEND + offset, 8), :] = item


def middle_kernel(vectors, got, ends, spread):
    groups = lane() // 32
    slabs = ends.shape[0]
    strip = lax.axis_index("tile") % 4
    lasts = []
    spread[pl.ds(5 * slabs, 8), :] = jnp.zeros((8, 128), F32)
    for q in range(slabs // 8):
        shared = got[pl.ds(q * 8 * SEND + 16, 8, stride=SEND), :]
        turned = [pltpu.roll(shared, 32 * d, axis=1) if d else shared for d in range(4)]
        line = [pick(groups, [turned[(p - x) % 4] for p in range(4)]) for x in range(4)]
        for x in range(3):
            spread[pl.ds(x * slabs + q * 8, 8), :] = (line[x] + line[x + 1]) * 0.5
        spread[pl.ds(4 * slabs + q * 8, 8), :] = line[0]
        lasts.append(line[3])
    for q in range(slabs // 8):
        onward = spread[pl.ds(4 * slabs + q * 8 + 1, 8), :]
        spread[pl.ds(3 * slabs + q * 8, 8), :] = (lasts[q] + onward) * 0.5
    rate = vectors[strip]
    wind = vectors[4]
    below, above, slack, rhs = [], [], [], []
    outer = rate * (spread[pl.ds(4 * slabs, 1), :] * 0.5)
    for k in range(slabs):
        e01, e12, e23 = (rate * spread[pl.ds(x * slabs + k, 1), :] for x in range(3))
        one_inv, one_fill, one_upper, two_inv, two_fill, two_slack, two_next = inner_coefs(
            e01, e12, e23, wind
        )
        two_slack = two_slack * two_inv
        q0 = e01 + wind
        own = 1.0 + q0 * (one_inv + one_upper * two_slack)
        if k == 0:
            own = own + outer
            below.append(None)
        else:
            below.append(outer)
        above.append(q0 * (one_upper * (two_next * two_inv)))
        slack.append(own)
        rhs.append(got[pl.ds(k * SEND, 8), :])
        outer = rate * spread[pl.ds(3 * slabs + k, 1), :]
        own = 1.0 + e23 * two_slack
        below.append(e23 * (two_fill * two_inv))
        if k < slabs - 1:
            above.append(outer + wind)
        else:
            own = own + (outer + wind)
            above.append(None)
        slack.append(own)
        rhs.append(got[pl.ds(k * SEND + 8, 8), :])

    def total(i):
        out = slack[i]
        if below[i] is not None:
            out = out + below[i]
        if above[i] is not None:
            out = out + above[i]
        return out

    count = 2 * slabs
    alive = list(range(count))
    removed = []
    while len(alive) > 1:
        gone = alive[1::2]
        stay = alive[0::2]
        normal = {}
        for i in gone:
            inv = inverse(total(i))
            normal[i] = (
                below[i] * inv,
                None if above[i] is None else above[i] * inv,
                slack[i] * inv,
                rhs[i] * inv,
            )
        for n, i in enumerate(stay):
            new_below = new_above = None
            new_slack, new_rhs = slack[i], rhs[i]
            if n > 0:
                nb, na, ns, nr = normal[gone[n - 1]]
                new_slack = new_slack + below[i] * ns
                new_rhs = new_rhs + below[i] * nr
                new_below = below[i] * nb
            if n < len(gone):
                nb, na, ns, nr = normal[gone[n]]
                new_slack = new_slack + above[i] * ns
                new_rhs = new_rhs + above[i] * nr
                new_above = None if na is None else above[i] * na
            below[i], above[i], slack[i], rhs[i] = new_below, new_above, new_slack, new_rhs
        removed.append((alive, normal))
        alive = stay
    solved = {0: rhs[0] * inverse(slack[0])}
    for order, normal in reversed(removed):
        for n in range(1, len(order), 2):
            nb, na, ns, nr = normal[order[n]]
            item = nr + nb * solved[order[n - 1]]
            if na is not None:
                item = item + na * solved[order[n + 1]]
            solved[order[n]] = item
    for k in range(slabs):
        ends[k, pl.ds(0, 8), :] = solved[2 * k]
        ends[k, pl.ds(8, 8), :] = solved[2 * k + 1]


def inner_rows(ends, kept, j):
    first = ends[j, pl.ds(0, 8), :]
    last = ends[j, pl.ds(8, 8), :]
    a1, b1, c1, a2, b2, c2 = (kept[j, pl.ds(n * 8, 8), :] for n in range(6))
    two = a2 + b2 * first + c2 * last
    one = a1 + b1 * first + c1 * two
    return first, one, two, last


def sums_kernel(vectors, window, ends, kept, grad, sorted_ends):
    parts = []
    groups = lane() // 32
    for v in range(8):
        for row in (0, 8):
            items = from_strips([ends[v * 4 + g, pl.ds(row, 8), :] for g in range(4)], groups)
            for zp, item in enumerate(items):
                sorted_ends[v * 4 + zp, pl.ds(row, 8), :] = item
    for v in range(8):
        total = None
        for zp in range(4):
            first, one, two, last = inner_rows(sorted_ends, kept, v * 4 + zp)
            item = vectors[5 + (v // 4) * 4 + zp] * ((first + one) + (two + last))
            total = item if total is None else total + item
        parts.append(jnp.sum(total, axis=0, keepdims=True))
    sums = [jnp.concatenate(parts[f * 4 : f * 4 + 4], axis=1) for f in range(2)]
    pieces = []
    for _ in range(3):
        piece = [item.astype(jnp.bfloat16).astype(F32) for item in sums]
        sums = [item - cut for item, cut in zip(sums, piece)]
        pieces += piece
    pieces = jnp.concatenate(pieces + [jnp.zeros((2, sums[0].shape[1]), F32)], axis=0)
    picked = jnp.dot(pieces.astype(jnp.bfloat16), window[...], preferred_element_type=F32)
    grad[...] = (picked[0:2, :] + picked[2:4, :]) + picked[4:6, :]


def state_kernel(ends, kept, state, lines):
    low = sublane() < 4
    for f in range(2):
        for yb in range(4):
            v = f * 4 + yb
            for zp in range(4):
                for x, item in enumerate(inner_rows(ends, kept, v * 4 + zp)):
                    lines[pl.ds(v * 128 + zp * 32 + x, 8, stride=4), :] = item
        for z in range(8):
            for sp in range(2):
                for h in range(2):
                    base = (f * 4 + 2 * h) * 128 + z * 16 + sp * 8
                    even, odd = pair_halves(
                        lines[pl.ds(base, 8), :], lines[pl.ds(base + 128, 8), :], low
                    )
                    for s, item in ((2 * sp, even), (2 * sp + 1, odd)):
                        state[pl.ds(s * 256 + f * 128 + z * 16 + h * 8, 8), :] = item


def rows_of(block):
    s, f, z, x, y = block.shape
    return block.reshape(s, f, z, x, y // 128, 128).transpose(0, 1, 2, 4, 3, 5).reshape(-1, 128)


def on_device(
    cotangent, scenario_ids, weather, landuse, class_diff, level_scale, emit_profile, building_cells
):
    hbm = pl.BlockSpec(memory_space=pltpu.HBM)
    vmem = pl.BlockSpec(memory_space=pltpu.VMEM)
    params = pltpu.CompilerParams(vmem_limit_bytes=32 * 1024 * 1024)
    slabs = lax.axis_size("tile")
    groups = lax.axis_size("scen")
    width = cotangent.shape[4]
    cells = building_cells.T
    classes = landuse.reshape(4, 4, 128).transpose(1, 0, 2).reshape(16, 128)
    small = (scenario_ids, weather.T, class_diff, level_scale, emit_profile)
    operands = (*small, classes, cells, rows_of(cotangent))
    sent, kept, vectors, window = pl.pallas_call(
        first_kernel,
        out_shape=(
            jax.ShapeDtypeStruct((slabs * SEND, 128), F32),
            jax.ShapeDtypeStruct((slabs, 48, 128), F32),
            jax.ShapeDtypeStruct((13, 8, 128), F32),
            jax.ShapeDtypeStruct((width, cells.shape[1]), jnp.bfloat16),
        ),
        in_specs=[hbm] * 8,
        out_specs=(vmem,) * 4,
        scratch_shapes=[pltpu.SMEM(item.shape, item.dtype) for item in small]
        + [pltpu.VMEM(item.shape, item.dtype) for item in (classes, cells)]
        + [pltpu.VMEM((1024, 128), F32)] * 2
        + [pltpu.VMEM((64 * PITCH, 128), F32)] * 2
        + [pltpu.VMEM((1024, 128), F32)] * 3
        + [pltpu.VMEM((32, 128), F32), pltpu.SemaphoreType.DMA((9,))],
        compiler_params=params,
    )(*(pltpu.with_memory_space_constraint(item, pltpu.HBM) for item in operands))
    got = lax.all_to_all(sent.reshape(slabs, SEND, 1, 128), "tile", 0, 0).reshape(slabs * SEND, 128)
    ends = pl.pallas_call(
        middle_kernel,
        out_shape=jax.ShapeDtypeStruct((slabs, 16, 128), F32),
        in_specs=[vmem] * 2,
        out_specs=vmem,
        scratch_shapes=[pltpu.VMEM((5 * slabs + 8, 128), F32)],
        compiler_params=params,
    )(vectors, got)
    ends = lax.all_to_all(ends, "tile", 0, 0)
    grad, ends = pl.pallas_call(
        sums_kernel,
        out_shape=(
            jax.ShapeDtypeStruct((2, cells.shape[1]), F32),
            jax.ShapeDtypeStruct((slabs, 16, 128), F32),
        ),
        in_specs=[vmem] * 4,
        out_specs=(vmem, vmem),
        compiler_params=params,
    )(vectors, window, ends, kept)
    state = pl.pallas_call(
        state_kernel,
        out_shape=jax.ShapeDtypeStruct((1024, 128), F32),
        in_specs=[vmem] * 2,
        out_specs=vmem,
        scratch_shapes=[pltpu.VMEM((1024, 128), F32)],
        compiler_params=params,
    )(ends, kept)
    grad = grad + lax.ppermute(grad, "scen", [(i, i ^ 1) for i in range(groups)])
    shifted = [
        lax.ppermute(grad, "scen", [(i, i ^ step) for i in range(groups)]) for step in (2, 4, 6)
    ]
    grad = (grad + shifted[0]) + (shifted[1] + shifted[2])
    state = state.reshape(4, 2, 8, 4, 4, 128).transpose(0, 1, 2, 4, 3, 5).reshape(cotangent.shape)
    return (state, grad)


def solution(mesh):
    placed = (
        P("scen", None, None, "tile", None),
        P("scen"),
        P(),
        P("tile", None),
        P(),
        P(),
        P(),
        P("tile", None),
    )
    return jax.shard_map(
        on_device,
        mesh=mesh,
        in_specs=placed,
        out_specs=(P("scen", None, None, "tile", None), P(None, "tile")),
        check_vma=False,
    )
```

```python
import jax
import jax.numpy as jnp
from jax import lax
from jax.experimental import pallas as pl
from jax.experimental.pallas import tpu as pltpu
from jax.sharding import PartitionSpec as P

F32 = jnp.float32
SEND = 17


def inverse(value):
    return pltpu.reciprocal(value, approx=True)


def sublane():
    return lax.broadcasted_iota(jnp.int32, (8, 128), 0)


def lane():
    return lax.broadcasted_iota(jnp.int32, (8, 128), 1)


def choose(index, values):
    out = jnp.full((8, 128), values[-1], F32)
    for at in range(len(values) - 2, -1, -1):
        out = jnp.where(index == at, values[at], out)
    return out


def surface(classes, class_diff, field):
    out = jnp.zeros((8, 128), F32)
    for mark in range(class_diff.shape[1]):
        out = jnp.where(classes == mark, class_diff[field, mark], out)
    return out


def swap_halves(value):
    return pltpu.roll(value, 4, axis=0)


def pair_halves(first, second, low):
    return (
        jnp.where(low, first, swap_halves(second)),
        jnp.where(low, swap_halves(first), second),
    )


def pick(groups, items):
    out = items[3]
    for at in range(2, -1, -1):
        out = jnp.where(groups == at, items[at], out)
    return out


def to_strips(items, groups):
    turned = [pltpu.roll(item, 32 * m, axis=1) if m else item for m, item in enumerate(items)]
    return [pick(groups, [turned[(p - g) % 4] for p in range(4)]) for g in range(4)]


def from_strips(strips, groups):
    items = [pick(groups, [strips[(p - m) % 4] for p in range(4)]) for m in range(4)]
    return [pltpu.roll(item, 128 - 32 * m, axis=1) if m else item for m, item in enumerate(items)]


def solve_levels(cot, surf, scale, table, out, hold_a, hold_c, low, arrivals):
    half = [(scale[z] + scale[z + 1]) * 0.5 for z in range(7)]
    for pair in range(2):
        arrivals[pair].wait()
        chains = [(s, f, h) for s in (2 * pair, 2 * pair + 1) for f in range(2) for h in range(2)]
        rated = [surf[f][h] * table(s, 2) for s, f, h in chains]
        winds = [table(s, 5) for s, f, h in chains]
        values = [None] * 8
        slacks = [None] * 8
        faces = [None] * 8
        for z in range(8):
            for n, (s, f, h) in enumerate(chains):
                rhs = cot[pl.ds(s * 256 + f * 128 + z * 16 + h * 8, 8), :]
                if z == 0:
                    slack = 1.0 + rated[n] * (scale[0] * 0.5)
                else:
                    slack = 1.0 + faces[n] * slacks[n]
                    rhs = rhs + faces[n] * values[n]
                if z < 7:
                    face = rated[n] * half[z]
                    above = face + winds[n]
                    inv = inverse(above + slack)
                    values[n] = rhs * inv
                    slacks[n] = slack * inv
                    faces[n] = face
                    hold_a[pl.ds((z * 8 + n) * 8, 8), :] = values[n]
                    hold_c[pl.ds((z * 8 + n) * 8, 8), :] = above * inv
                else:
                    slack = slack + (rated[n] * (scale[7] * 0.5) + winds[n])
                    values[n] = rhs * inverse(slack)
        for z in range(7, -1, -1):
            if z < 7:
                for n in range(8):
                    at = pl.ds((z * 8 + n) * 8, 8)
                    values[n] = hold_a[at, :] + hold_c[at, :] * values[n]
            for f in range(2):
                for h in range(2):
                    n = f * 2 + h
                    even, odd = pair_halves(values[n], values[n + 4], low)
                    for yb, item in ((2 * h, even), (2 * h + 1, odd)):
                        out[pl.ds((f * 4 + yb) * 128 + z * 16 + pair * 8, 8), :] = item


def from_before(items, rows, distance):
    turned = [pltpu.roll(item, distance, axis=0) for item in items]
    return [
        turned[v] if v % 4 == 0 else jnp.where(rows < distance, turned[v - 1], turned[v])
        for v in range(8)
    ]


def from_after(items, rows, distance):
    turned = [pltpu.roll(item, 8 - distance, axis=0) for item in items]
    return [
        turned[v] if v % 4 == 3 else jnp.where(rows >= 8 - distance, turned[v + 1], turned[v])
        for v in range(8)
    ]


def solve_chunks(below, above, slack, rhs, rows):
    everyone = range(8)
    for distance in (1, 2, 4, 8, 16):
        inv = [inverse(below[v] + above[v] + slack[v]) for v in everyone]
        nb = [below[v] * inv[v] for v in everyone]
        na = [above[v] * inv[v] for v in everyone]
        ns = [slack[v] * inv[v] for v in everyone]
        nr = [rhs[v] * inv[v] for v in everyone]
        new_slack = list(slack)
        new_rhs = list(rhs)
        if distance < 8:
            pb, ps, pr = (from_before(item, rows, distance) for item in (nb, ns, nr))
            qa, qs, qr = (from_after(item, rows, distance) for item in (na, ns, nr))
            has_before = has_after = [True] * 8
        else:
            jump = distance // 8
            has_before = [v % 4 >= jump for v in everyone]
            has_after = [v % 4 < 4 - jump for v in everyone]
            pb, ps, pr = (
                [item[v - jump] if has_before[v] else None for v in everyone]
                for item in (nb, ns, nr)
            )
            qa, qs, qr = (
                [item[v + jump] if has_after[v] else None for v in everyone]
                for item in (na, ns, nr)
            )
        zero = jnp.zeros((8, 128), F32)
        new_below = [zero] * 8
        new_above = [zero] * 8
        for v in everyone:
            if has_before[v]:
                new_slack[v] = new_slack[v] + below[v] * ps[v]
                new_rhs[v] = new_rhs[v] + below[v] * pr[v]
                new_below[v] = below[v] * pb[v]
            if has_after[v]:
                new_slack[v] = new_slack[v] + above[v] * qs[v]
                new_rhs[v] = new_rhs[v] + above[v] * qr[v]
                new_above[v] = above[v] * qa[v]
        below, above, slack, rhs = new_below, new_above, new_slack, new_rhs
    return [rhs[v] * inverse(slack[v]) for v in everyone]


PITCH = 17


def store_turned(target, v, block):
    for n in range(16):
        target[pl.ds(v * 8 * PITCH + n // 2 * PITCH + n % 2 * 8, 8), :] = block[8 * n : 8 * n + 8, :]


def load_turned(source, v):
    return jnp.concatenate(
        [source[pl.ds(v * 8 * PITCH + n // 2 * PITCH + n % 2 * 8, 8), :] for n in range(16)], axis=0
    )


def solve_rows(turned, faces, leak, rate, wind, hold_a, hold_b, hold_c, rows):
    everyone = range(8)
    depth = 16

    def at(v, i):
        return pl.ds(v * 8 * PITCH + i, 8, stride=PITCH)

    def keep(i, v):
        return pl.ds((i * 8 + v) * 8, 8)

    ends = [faces[at(v, depth - 1), :] * rate for v in everyone]
    before = from_before(ends, rows, 1)
    last = ends
    value = [None] * 8
    fill = [None] * 8
    slack = [None] * 8
    for i in range(depth):
        for v in everyone:
            rhs = turned[at(v, i), :]
            face = last[v] if i == depth - 1 else faces[at(v, i), :] * rate
            next_coef = face + wind
            if i == 0:
                link = before[v]
                own = jnp.ones((8, 128), F32)
                if v % 4 == 0:
                    own = jnp.where(rows == 0, 1.0 + leak[v // 4], own)
                    link = jnp.where(rows == 0, 0.0, link)
            else:
                link = before[v] * fill[v]
                own = 1.0 + before[v] * slack[v]
                rhs = rhs + before[v] * value[v]
            if i == depth - 1:
                if v % 4 == 3:
                    own = jnp.where(rows == 7, own + next_coef, own)
                    next_coef = jnp.where(rows == 7, 0.0, next_coef)
                value[v], fill[v], slack[v] = rhs, link, own
                before[v] = next_coef
                continue
            inv = inverse(next_coef + link + own)
            value[v] = rhs * inv
            fill[v] = link * inv
            slack[v] = own * inv
            upper = next_coef * inv
            hold_a[keep(i, v), :] = value[v]
            hold_b[keep(i, v), :] = fill[v]
            hold_c[keep(i, v), :] = upper
            before[v] = face
            if i == 0:
                if v == 0:
                    first_value, first_fill, first_slack, first_next = ([None] * 8 for _ in range(4))
                first_value[v], first_fill[v], first_slack[v], first_next[v] = (
                    value[v],
                    fill[v],
                    slack[v],
                    upper,
                )
            else:
                carry = first_next[v]
                first_value[v] = first_value[v] + carry * value[v]
                first_slack[v] = first_slack[v] + carry * slack[v]
                first_next[v] = carry * upper
    next_value = from_after(first_value, rows, 1)
    next_slack = from_after(first_slack, rows, 1)
    next_next = from_after(first_next, rows, 1)
    above = [before[v] * next_next[v] for v in everyone]
    slack = [slack[v] + before[v] * next_slack[v] for v in everyone]
    rhs = [value[v] + before[v] * next_value[v] for v in everyone]
    current = solve_chunks(fill, above, slack, rhs, rows)
    previous = from_before(current, rows, 1)
    for v in everyone:
        turned[at(v, depth - 1), :] = current[v]
    for i in range(depth - 2, -1, -1):
        for v in everyone:
            item = hold_a[keep(i, v), :] + hold_b[keep(i, v), :] * previous[v]
            current[v] = item + hold_c[keep(i, v), :] * current[v]
            turned[at(v, i), :] = current[v]


def inner_coefs(low_face, mid_face, high_face, wind):
    one_next = mid_face + wind
    one_inv = inverse(low_face + one_next + 1.0)
    one_fill = low_face * one_inv
    one_upper = one_next * one_inv
    two_next = high_face + wind
    two_fill = mid_face * one_fill
    two_slack = 1.0 + mid_face * one_inv
    two_inv = inverse(two_next + two_fill + two_slack)
    return one_inv, one_fill, one_upper, two_inv, two_fill, two_slack, two_next


def first_kernel(
    ids_in, weather_in, class_diff_in, scale_in, emit_in, landuse_in, cells_in, cot_in,
    sent, kept, vectors, window,
    ids, weather, class_diff, scale, emit, landuse, cells, cot,
    levels, turned, faces, hold_a, hold_b, hold_c, surf_rows, done,
):
    small = [
        pltpu.make_async_copy(source, target, done.at[n])
        for n, (source, target) in enumerate(
            (
                (ids_in, ids),
                (weather_in, weather),
                (class_diff_in, class_diff),
                (scale_in, scale),
                (emit_in, emit),
                (landuse_in, landuse),
                (cells_in, cells),
            )
        )
    ]
    halves = [
        pltpu.make_async_copy(
            cot_in.at[pl.ds(n * 512, 512), :], cot.at[pl.ds(n * 512, 512), :], done.at[7 + n]
        )
        for n in range(2)
    ]
    for copy in small + halves:
        copy.start()
    for copy in small:
        copy.wait()
    rows = sublane()
    lanes = lane()
    low = rows < 4

    def table(s, column):
        return weather[column, ids[s]]

    classes = [landuse[pl.ds(0, 8), :], landuse[pl.ds(8, 8), :]]
    surf = [[surface(item, class_diff, f) for item in classes] for f in range(2)]
    rate_y = choose((lanes // 4) % 4, [table(s, 1) for s in range(4)])
    wind_y = choose((lanes // 4) % 4, [table(s, 4) for s in range(4)])
    rate_y = rate_y * choose(lanes // 16, [scale[z] for z in range(8)])
    leak = []
    for f in range(2):
        upper, lower = surf[f]
        surf_rows[pl.ds(f * 16, 8), :] = upper
        surf_rows[pl.ds(f * 16 + 8, 8), :] = lower
        shifted = [pltpu.roll(item, 127, axis=1) for item in (upper, lower)]
        swapped = [swap_halves(item) for item in shifted]
        onward = [
            jnp.where(low, swapped[0], swapped[1]),
            jnp.where(low, swapped[1], 0.0),
        ]
        for h in range(2):
            right = jnp.where(lanes == 127, onward[h], shifted[h])
            face = (surf[f][h] + right) * 0.5
            other = swap_halves(face)
            for yb, item in (
                (2 * h, jnp.where(low, face, other)),
                (2 * h + 1, jnp.where(low, other, face)),
            ):
                tile = jnp.concatenate([item] * 16, axis=0)
                store_turned(faces, f * 4 + yb, tile.T)
        start = jnp.broadcast_to(upper[:, 0:1], (8, 128))
        start = jnp.where(rows == lanes % 4, start, 0.0)
        start = jnp.broadcast_to(jnp.sum(start, axis=0, keepdims=True), (8, 128))
        leak.append(start * 0.5 * rate_y)

    rate_x = choose(rows % 4, [table(s, 0) for s in range(4)])
    wind_x = choose(rows % 4, [table(s, 3) for s in range(4)])
    scales = [choose(rows // 4, [scale[2 * zp], scale[2 * zp + 1]]) for zp in range(4)]
    groups = lanes // 32
    for g in range(4):
        vectors[g] = rate_x * choose(groups, [scales[(p - g) % 4] for p in range(4)])
    vectors[4] = wind_x
    for f in range(2):
        factor = choose(rows % 4, [table(s, 6 + f) for s in range(4)])
        for zp in range(4):
            vectors[5 + f * 4 + zp] = factor * choose(rows // 4, [emit[2 * zp], emit[2 * zp + 1]])
    for v in range(8):
        line = [surf_rows[pl.ds(v * 4 + x, 1), :] for x in range(4)]
        steps = [(line[x] + line[x + 1]) * 0.5 for x in range(3)]
        for zp in range(4):
            j = v * 4 + zp
            rate = rate_x * scales[zp]
            one_inv, one_fill, one_upper, two_inv, two_fill, two_slack, two_next = inner_coefs(
                *(rate * step for step in steps), wind_x
            )
            for n, item in enumerate(
                (one_inv, one_fill, one_upper, two_inv, two_fill * two_inv, two_next * two_inv)
            ):
                kept[j, pl.ds(n * 8, 8), :] = item
    lines = [surf_rows[pl.ds(x, 8, stride=4), :] for x in range(4)]
    lines = [
        [pltpu.roll(item, 32 * d, axis=1) if d else item for d in range(4)] for item in lines
    ]
    strips = [pick(groups, [lines[x][(x - g) % 4] for x in range(4)]) for g in range(4)]
    for g in range(4):
        for v in range(8):
            sent[pl.ds((v * 4 + g) * SEND + 16, 1), :] = strips[g][v : v + 1, :]
    width = window.shape[0]
    start = jnp.min(cells[...] % width, axis=0, keepdims=True)
    place = lax.broadcasted_iota(jnp.int32, (width, 128), 0)
    window[...] = jnp.where((place >= start) & (place < start + 4), 1.0, 0.0).astype(jnp.bfloat16)

    solve_levels(cot, surf, scale, table, levels, hold_a, hold_c, low, halves)
    for v in range(8):
        store_turned(turned, v, levels[pl.ds(v * 128, 128), :].T)
    solve_rows(turned, faces, leak, rate_y, wind_y, hold_a, hold_b, hold_c, rows)
    for v in range(8):
        levels[pl.ds(v * 128, 128), :] = load_turned(turned, v).T

    for v in range(8):
        line = [surf_rows[pl.ds(v * 4 + x, 1), :] for x in range(4)]
        steps = [(line[x] + line[x + 1]) * 0.5 for x in range(3)]
        firsts, lasts = [], []
        for zp in range(4):
            j = v * 4 + zp
            rate = rate_x * scales[zp]
            e01, e12, e23 = (rate * step for step in steps)
            rhs = [levels[pl.ds(v * 128 + zp * 32 + x, 8, stride=4), :] for x in range(4)]
            one = rhs[1] * kept[j, pl.ds(0, 8), :]
            two = (rhs[2] + e12 * one) * kept[j, pl.ds(24, 8), :]
            one_upper = kept[j, pl.ds(16, 8), :]
            firsts.append(rhs[0] + (e01 + wind_x) * (one + one_upper * two))
            lasts.append(rhs[3] + e23 * two)
            kept[j, pl.ds(0, 8), :] = one
            kept[j, pl.ds(24, 8), :] = two
        for offset, items in ((0, firsts), (8, lasts)):
            for g, item in enumerate(to_strips(items, groups)):
                sent[pl.ds((v * 4 + g) * SEND + offset, 8), :] = item


def middle_kernel(vectors, got, ends, spread):
    groups = lane() // 32
    slabs = ends.shape[0]
    strip = lax.axis_index("tile") % 4
    for q in range(slabs // 8):
        shared = got[pl.ds(q * 8 * SEND + 16, 8, stride=SEND), :]
        turned = [pltpu.roll(shared, 32 * d, axis=1) if d else shared for d in range(4)]
        for x in range(4):
            spread[pl.ds(x * slabs + q * 8, 8), :] = pick(
                groups, [turned[(p - x) % 4] for p in range(4)]
            )
    rate = vectors[strip]
    wind = vectors[4]
    below, above, slack, rhs = [], [], [], []
    line = None
    outer = None
    for k in range(slabs):
        line = [spread[pl.ds(x * slabs + k, 1), :] for x in range(4)]
        if k == 0:
            outer = rate * (line[0] * 0.5)
        e01, e12, e23 = (rate * ((line[x] + line[x + 1]) * 0.5) for x in range(3))
        one_inv, one_fill, one_upper, two_inv, two_fill, two_slack, two_next = inner_coefs(
            e01, e12, e23, wind
        )
        two_slack = two_slack * two_inv
        q0 = e01 + wind
        own = 1.0 + q0 * (one_inv + one_upper * two_slack)
        if k == 0:
            own = own + outer
            below.append(None)
        else:
            below.append(outer)
        above.append(q0 * (one_upper * (two_next * two_inv)))
        slack.append(own)
        rhs.append(got[pl.ds(k * SEND, 8), :])
        if k < slabs - 1:
            outer = rate * ((line[3] + spread[pl.ds(k + 1, 1), :]) * 0.5)
        else:
            outer = rate * (line[3] * 0.5)
        own = 1.0 + e23 * two_slack
        below.append(e23 * (two_fill * two_inv))
        if k < slabs - 1:
            above.append(outer + wind)
        else:
            own = own + (outer + wind)
            above.append(None)
        slack.append(own)
        rhs.append(got[pl.ds(k * SEND + 8, 8), :])

    def total(i):
        out = slack[i]
        if below[i] is not None:
            out = out + below[i]
        if above[i] is not None:
            out = out + above[i]
        return out

    count = 2 * slabs
    alive = list(range(count))
    removed = []
    while len(alive) > 1:
        gone = alive[1::2]
        stay = alive[0::2]
        normal = {}
        for i in gone:
            inv = inverse(total(i))
            normal[i] = (
                below[i] * inv,
                None if above[i] is None else above[i] * inv,
                slack[i] * inv,
                rhs[i] * inv,
            )
        for n, i in enumerate(stay):
            new_below = new_above = None
            new_slack, new_rhs = slack[i], rhs[i]
            if n > 0:
                nb, na, ns, nr = normal[gone[n - 1]]
                new_slack = new_slack + below[i] * ns
                new_rhs = new_rhs + below[i] * nr
                new_below = below[i] * nb
            if n < len(gone):
                nb, na, ns, nr = normal[gone[n]]
                new_slack = new_slack + above[i] * ns
                new_rhs = new_rhs + above[i] * nr
                new_above = None if na is None else above[i] * na
            below[i], above[i], slack[i], rhs[i] = new_below, new_above, new_slack, new_rhs
        removed.append((alive, normal))
        alive = stay
    solved = {0: rhs[0] * inverse(slack[0])}
    for order, normal in reversed(removed):
        for n in range(1, len(order), 2):
            nb, na, ns, nr = normal[order[n]]
            item = nr + nb * solved[order[n - 1]]
            if na is not None:
                item = item + na * solved[order[n + 1]]
            solved[order[n]] = item
    for k in range(slabs):
        ends[k, pl.ds(0, 8), :] = solved[2 * k]
        ends[k, pl.ds(8, 8), :] = solved[2 * k + 1]


def inner_rows(ends, kept, j):
    first = ends[j, pl.ds(0, 8), :]
    last = ends[j, pl.ds(8, 8), :]
    a1, b1, c1, a2, b2, c2 = (kept[j, pl.ds(n * 8, 8), :] for n in range(6))
    two = a2 + b2 * first + c2 * last
    one = a1 + b1 * first + c1 * two
    return first, one, two, last


def sums_kernel(vectors, window, ends, kept, grad, sorted_ends):
    parts = []
    groups = lane() // 32
    for v in range(8):
        for row in (0, 8):
            items = from_strips([ends[v * 4 + g, pl.ds(row, 8), :] for g in range(4)], groups)
            for zp, item in enumerate(items):
                sorted_ends[v * 4 + zp, pl.ds(row, 8), :] = item
    for v in range(8):
        total = None
        for zp in range(4):
            first, one, two, last = inner_rows(sorted_ends, kept, v * 4 + zp)
            item = vectors[5 + (v // 4) * 4 + zp] * ((first + one) + (two + last))
            total = item if total is None else total + item
        parts.append(jnp.sum(total, axis=0, keepdims=True))
    sums = [jnp.concatenate(parts[f * 4 : f * 4 + 4], axis=1) for f in range(2)]
    pieces = []
    for _ in range(3):
        piece = [item.astype(jnp.bfloat16).astype(F32) for item in sums]
        sums = [item - cut for item, cut in zip(sums, piece)]
        pieces += piece
    pieces = jnp.concatenate(pieces + [jnp.zeros((2, sums[0].shape[1]), F32)], axis=0)
    picked = jnp.dot(pieces.astype(jnp.bfloat16), window[...], preferred_element_type=F32)
    grad[...] = (picked[0:2, :] + picked[2:4, :]) + picked[4:6, :]


def state_kernel(ends, kept, state, lines):
    low = sublane() < 4
    for f in range(2):
        for yb in range(4):
            v = f * 4 + yb
            for zp in range(4):
                for x, item in enumerate(inner_rows(ends, kept, v * 4 + zp)):
                    lines[pl.ds(v * 128 + zp * 32 + x, 8, stride=4), :] = item
        for z in range(8):
            for sp in range(2):
                for h in range(2):
                    base = (f * 4 + 2 * h) * 128 + z * 16 + sp * 8
                    even, odd = pair_halves(
                        lines[pl.ds(base, 8), :], lines[pl.ds(base + 128, 8), :], low
                    )
                    for s, item in ((2 * sp, even), (2 * sp + 1, odd)):
                        state[pl.ds(s * 256 + f * 128 + z * 16 + h * 8, 8), :] = item


def rows_of(block):
    s, f, z, x, y = block.shape
    return block.reshape(s, f, z, x, y // 128, 128).transpose(0, 1, 2, 4, 3, 5).reshape(-1, 128)


def on_device(
    cotangent, scenario_ids, weather, landuse, class_diff, level_scale, emit_profile, building_cells
):
    hbm = pl.BlockSpec(memory_space=pltpu.HBM)
    vmem = pl.BlockSpec(memory_space=pltpu.VMEM)
    params = pltpu.CompilerParams(vmem_limit_bytes=32 * 1024 * 1024)
    slabs = lax.axis_size("tile")
    groups = lax.axis_size("scen")
    width = cotangent.shape[4]
    cells = building_cells.T
    classes = landuse.reshape(4, 4, 128).transpose(1, 0, 2).reshape(16, 128)
    small = (scenario_ids, weather.T, class_diff, level_scale, emit_profile)
    operands = (*small, classes, cells, rows_of(cotangent))
    sent, kept, vectors, window = pl.pallas_call(
        first_kernel,
        out_shape=(
            jax.ShapeDtypeStruct((slabs * SEND, 128), F32),
            jax.ShapeDtypeStruct((slabs, 48, 128), F32),
            jax.ShapeDtypeStruct((13, 8, 128), F32),
            jax.ShapeDtypeStruct((width, cells.shape[1]), jnp.bfloat16),
        ),
        in_specs=[hbm] * 8,
        out_specs=(vmem,) * 4,
        scratch_shapes=[pltpu.SMEM(item.shape, item.dtype) for item in small]
        + [pltpu.VMEM(item.shape, item.dtype) for item in (classes, cells)]
        + [pltpu.VMEM((1024, 128), F32)] * 2
        + [pltpu.VMEM((64 * PITCH, 128), F32)] * 2
        + [pltpu.VMEM((1024, 128), F32)] * 3
        + [pltpu.VMEM((32, 128), F32), pltpu.SemaphoreType.DMA((9,))],
        compiler_params=params,
    )(*(pltpu.with_memory_space_constraint(item, pltpu.HBM) for item in operands))
    got = lax.all_to_all(sent.reshape(slabs, SEND, 1, 128), "tile", 0, 0).reshape(slabs * SEND, 128)
    ends = pl.pallas_call(
        middle_kernel,
        out_shape=jax.ShapeDtypeStruct((slabs, 16, 128), F32),
        in_specs=[vmem] * 2,
        out_specs=vmem,
        scratch_shapes=[pltpu.VMEM((4 * slabs, 128), F32)],
        compiler_params=params,
    )(vectors, got)
    ends = lax.all_to_all(ends, "tile", 0, 0)
    grad, ends = pl.pallas_call(
        sums_kernel,
        out_shape=(
            jax.ShapeDtypeStruct((2, cells.shape[1]), F32),
            jax.ShapeDtypeStruct((slabs, 16, 128), F32),
        ),
        in_specs=[vmem] * 4,
        out_specs=(vmem, vmem),
        compiler_params=params,
    )(vectors, window, ends, kept)
    state = pl.pallas_call(
        state_kernel,
        out_shape=jax.ShapeDtypeStruct((1024, 128), F32),
        in_specs=[vmem] * 2,
        out_specs=vmem,
        scratch_shapes=[pltpu.VMEM((1024, 128), F32)],
        compiler_params=params,
    )(ends, kept)
    grad = grad + lax.ppermute(grad, "scen", [(i, i ^ 1) for i in range(groups)])
    shifted = [
        lax.ppermute(grad, "scen", [(i, i ^ step) for i in range(groups)]) for step in (2, 6, 4)
    ]
    grad = (grad + shifted[0]) + (shifted[1] + shifted[2])
    state = state.reshape(4, 2, 8, 4, 4, 128).transpose(0, 1, 2, 4, 3, 5).reshape(cotangent.shape)
    return (state, grad)


def solution(mesh):
    placed = (
        P("scen", None, None, "tile", None),
        P("scen"),
        P(),
        P("tile", None),
        P(),
        P(),
        P(),
        P("tile", None),
    )
    return jax.shard_map(
        on_device,
        mesh=mesh,
        in_specs=placed,
        out_specs=(P("scen", None, None, "tile", None), P(None, "tile")),
        check_vma=False,
    )
```

```python
import jax
import jax.numpy as jnp
from jax import lax
from jax.experimental import pallas as pl
from jax.experimental.pallas import tpu as pltpu
from jax.sharding import PartitionSpec as P

F32 = jnp.float32
SEND = 17


def inverse(value):
    return pltpu.reciprocal(value, approx=True)


def sublane():
    return lax.broadcasted_iota(jnp.int32, (8, 128), 0)


def lane():
    return lax.broadcasted_iota(jnp.int32, (8, 128), 1)


def choose(index, values):
    out = jnp.full((8, 128), values[-1], F32)
    for at in range(len(values) - 2, -1, -1):
        out = jnp.where(index == at, values[at], out)
    return out


def surface(classes, class_diff, field):
    out = jnp.zeros((8, 128), F32)
    for mark in range(class_diff.shape[1]):
        out = jnp.where(classes == mark, class_diff[field, mark], out)
    return out


def swap_halves(value):
    return pltpu.roll(value, 4, axis=0)


def pair_halves(first, second, low):
    return (
        jnp.where(low, first, swap_halves(second)),
        jnp.where(low, swap_halves(first), second),
    )


def pick(groups, items):
    out = items[3]
    for at in range(2, -1, -1):
        out = jnp.where(groups == at, items[at], out)
    return out


def to_strips(items, groups):
    turned = [pltpu.roll(item, 32 * m, axis=1) if m else item for m, item in enumerate(items)]
    return [pick(groups, [turned[(p - g) % 4] for p in range(4)]) for g in range(4)]


def from_strips(strips, groups):
    items = [pick(groups, [strips[(p - m) % 4] for p in range(4)]) for m in range(4)]
    return [pltpu.roll(item, 128 - 32 * m, axis=1) if m else item for m, item in enumerate(items)]


def solve_levels(cot, surf, scale, table, out, hold_a, hold_c, low, arrivals):
    half = [(scale[z] + scale[z + 1]) * 0.5 for z in range(7)]
    for pair in range(2):
        arrivals[pair].wait()
        chains = [(s, f, h) for s in (2 * pair, 2 * pair + 1) for f in range(2) for h in range(2)]
        rated = [surf[f][h] * table(s, 2) for s, f, h in chains]
        winds = [table(s, 5) for s, f, h in chains]
        values = [None] * 8
        slacks = [None] * 8
        faces = [None] * 8
        for z in range(8):
            for n, (s, f, h) in enumerate(chains):
                rhs = cot[pl.ds(s * 256 + f * 128 + z * 16 + h * 8, 8), :]
                if z == 0:
                    slack = 1.0 + rated[n] * (scale[0] * 0.5)
                else:
                    slack = 1.0 + faces[n] * slacks[n]
                    rhs = rhs + faces[n] * values[n]
                if z < 7:
                    face = rated[n] * half[z]
                    above = face + winds[n]
                    inv = inverse(above + slack)
                    values[n] = rhs * inv
                    slacks[n] = slack * inv
                    faces[n] = face
                    hold_a[pl.ds((z * 8 + n) * 8, 8), :] = values[n]
                    hold_c[pl.ds((z * 8 + n) * 8, 8), :] = above * inv
                else:
                    slack = slack + (rated[n] * (scale[7] * 0.5) + winds[n])
                    values[n] = rhs * inverse(slack)
        for z in range(7, -1, -1):
            if z < 7:
                for n in range(8):
                    at = pl.ds((z * 8 + n) * 8, 8)
                    values[n] = hold_a[at, :] + hold_c[at, :] * values[n]
            for f in range(2):
                for h in range(2):
                    n = f * 2 + h
                    even, odd = pair_halves(values[n], values[n + 4], low)
                    for yb, item in ((2 * h, even), (2 * h + 1, odd)):
                        out[pl.ds((f * 4 + yb) * 128 + z * 16 + pair * 8, 8), :] = item


def from_before(items, rows, distance):
    turned = [pltpu.roll(item, distance, axis=0) for item in items]
    return [
        turned[v] if v % 4 == 0 else jnp.where(rows < distance, turned[v - 1], turned[v])
        for v in range(8)
    ]


def from_after(items, rows, distance):
    turned = [pltpu.roll(item, 8 - distance, axis=0) for item in items]
    return [
        turned[v] if v % 4 == 3 else jnp.where(rows >= 8 - distance, turned[v + 1], turned[v])
        for v in range(8)
    ]


def solve_chunks(below, above, slack, rhs, rows):
    everyone = range(8)
    for distance in (1, 2, 4, 8, 16):
        inv = [inverse(below[v] + above[v] + slack[v]) for v in everyone]
        nb = [below[v] * inv[v] for v in everyone]
        na = [above[v] * inv[v] for v in everyone]
        ns = [slack[v] * inv[v] for v in everyone]
        nr = [rhs[v] * inv[v] for v in everyone]
        new_slack = list(slack)
        new_rhs = list(rhs)
        if distance < 8:
            pb, ps, pr = (from_before(item, rows, distance) for item in (nb, ns, nr))
            qa, qs, qr = (from_after(item, rows, distance) for item in (na, ns, nr))
            has_before = has_after = [True] * 8
        else:
            jump = distance // 8
            has_before = [v % 4 >= jump for v in everyone]
            has_after = [v % 4 < 4 - jump for v in everyone]
            pb, ps, pr = (
                [item[v - jump] if has_before[v] else None for v in everyone]
                for item in (nb, ns, nr)
            )
            qa, qs, qr = (
                [item[v + jump] if has_after[v] else None for v in everyone]
                for item in (na, ns, nr)
            )
        zero = jnp.zeros((8, 128), F32)
        new_below = [zero] * 8
        new_above = [zero] * 8
        for v in everyone:
            if has_before[v]:
                new_slack[v] = new_slack[v] + below[v] * ps[v]
                new_rhs[v] = new_rhs[v] + below[v] * pr[v]
                new_below[v] = below[v] * pb[v]
            if has_after[v]:
                new_slack[v] = new_slack[v] + above[v] * qs[v]
                new_rhs[v] = new_rhs[v] + above[v] * qr[v]
                new_above[v] = above[v] * qa[v]
        below, above, slack, rhs = new_below, new_above, new_slack, new_rhs
    return [rhs[v] * inverse(slack[v]) for v in everyone]


PITCH = 17


def store_turned(target, v, block):
    for n in range(16):
        target[pl.ds(v * 8 * PITCH + n // 2 * PITCH + n % 2 * 8, 8), :] = block[8 * n : 8 * n + 8, :]


def load_turned(source, v):
    return jnp.concatenate(
        [source[pl.ds(v * 8 * PITCH + n // 2 * PITCH + n % 2 * 8, 8), :] for n in range(16)], axis=0
    )


def solve_rows(turned, faces, leak, rate, wind, hold_a, hold_b, hold_c, rows):
    everyone = range(8)
    depth = 16

    def at(v, i):
        return pl.ds(v * 8 * PITCH + i, 8, stride=PITCH)

    def keep(i, v):
        return pl.ds((i * 8 + v) * 8, 8)

    ends = [faces[at(v, depth - 1), :] * rate for v in everyone]
    before = from_before(ends, rows, 1)
    last = ends
    value = [None] * 8
    fill = [None] * 8
    slack = [None] * 8
    for i in range(depth):
        for v in everyone:
            rhs = turned[at(v, i), :]
            face = last[v] if i == depth - 1 else faces[at(v, i), :] * rate
            next_coef = face + wind
            if i == 0:
                link = before[v]
                own = jnp.ones((8, 128), F32)
                if v % 4 == 0:
                    own = jnp.where(rows == 0, 1.0 + leak[v // 4], own)
                    link = jnp.where(rows == 0, 0.0, link)
            else:
                link = before[v] * fill[v]
                own = 1.0 + before[v] * slack[v]
                rhs = rhs + before[v] * value[v]
            if i == depth - 1:
                if v % 4 == 3:
                    own = jnp.where(rows == 7, own + next_coef, own)
                    next_coef = jnp.where(rows == 7, 0.0, next_coef)
                value[v], fill[v], slack[v] = rhs, link, own
                before[v] = next_coef
                continue
            inv = inverse(next_coef + link + own)
            value[v] = rhs * inv
            fill[v] = link * inv
            slack[v] = own * inv
            upper = next_coef * inv
            hold_a[keep(i, v), :] = value[v]
            hold_b[keep(i, v), :] = fill[v]
            hold_c[keep(i, v), :] = upper
            before[v] = face
            if i == 0:
                if v == 0:
                    first_value, first_fill, first_slack, first_next = ([None] * 8 for _ in range(4))
                first_value[v], first_fill[v], first_slack[v], first_next[v] = (
                    value[v],
                    fill[v],
                    slack[v],
                    upper,
                )
            else:
                carry = first_next[v]
                first_value[v] = first_value[v] + carry * value[v]
                first_slack[v] = first_slack[v] + carry * slack[v]
                first_next[v] = carry * upper
    next_value = from_after(first_value, rows, 1)
    next_slack = from_after(first_slack, rows, 1)
    next_next = from_after(first_next, rows, 1)
    above = [before[v] * next_next[v] for v in everyone]
    slack = [slack[v] + before[v] * next_slack[v] for v in everyone]
    rhs = [value[v] + before[v] * next_value[v] for v in everyone]
    current = solve_chunks(fill, above, slack, rhs, rows)
    previous = from_before(current, rows, 1)
    for v in everyone:
        turned[at(v, depth - 1), :] = current[v]
    for i in range(depth - 2, -1, -1):
        for v in everyone:
            item = hold_a[keep(i, v), :] + hold_b[keep(i, v), :] * previous[v]
            current[v] = item + hold_c[keep(i, v), :] * current[v]
            turned[at(v, i), :] = current[v]


def inner_coefs(low_face, mid_face, high_face, wind):
    one_next = mid_face + wind
    one_inv = inverse(low_face + one_next + 1.0)
    one_fill = low_face * one_inv
    one_upper = one_next * one_inv
    two_next = high_face + wind
    two_fill = mid_face * one_fill
    two_slack = 1.0 + mid_face * one_inv
    two_inv = inverse(two_next + two_fill + two_slack)
    return one_inv, one_fill, one_upper, two_inv, two_fill, two_slack, two_next


def first_kernel(
    ids_in, weather_in, class_diff_in, scale_in, emit_in, landuse_in, cells_in, cot_in,
    sent, kept, vectors, window,
    ids, weather, class_diff, scale, emit, landuse, cells, cot,
    levels, turned, faces, hold_a, hold_b, hold_c, surf_rows, done,
):
    small = [
        pltpu.make_async_copy(source, target, done.at[n])
        for n, (source, target) in enumerate(
            (
                (ids_in, ids),
                (weather_in, weather),
                (class_diff_in, class_diff),
                (scale_in, scale),
                (emit_in, emit),
                (landuse_in, landuse),
                (cells_in, cells),
            )
        )
    ]
    halves = [
        pltpu.make_async_copy(
            cot_in.at[pl.ds(n * 512, 512), :], cot.at[pl.ds(n * 512, 512), :], done.at[7 + n]
        )
        for n in range(2)
    ]
    for copy in small + halves:
        copy.start()
    for copy in small:
        copy.wait()
    rows = sublane()
    lanes = lane()
    low = rows < 4

    def table(s, column):
        return weather[column, ids[s]]

    classes = [landuse[pl.ds(0, 8), :], landuse[pl.ds(8, 8), :]]
    surf = [[surface(item, class_diff, f) for item in classes] for f in range(2)]
    rate_y = choose((lanes // 4) % 4, [table(s, 1) for s in range(4)])
    wind_y = choose((lanes // 4) % 4, [table(s, 4) for s in range(4)])
    rate_y = rate_y * choose(lanes // 16, [scale[z] for z in range(8)])
    leak = []
    for f in range(2):
        upper, lower = surf[f]
        surf_rows[pl.ds(f * 16, 8), :] = upper
        surf_rows[pl.ds(f * 16 + 8, 8), :] = lower
        shifted = [pltpu.roll(item, 127, axis=1) for item in (upper, lower)]
        swapped = [swap_halves(item) for item in shifted]
        onward = [
            jnp.where(low, swapped[0], swapped[1]),
            jnp.where(low, swapped[1], 0.0),
        ]
        for h in range(2):
            right = jnp.where(lanes == 127, onward[h], shifted[h])
            face = (surf[f][h] + right) * 0.5
            other = swap_halves(face)
            for yb, item in (
                (2 * h, jnp.where(low, face, other)),
                (2 * h + 1, jnp.where(low, other, face)),
            ):
                tile = jnp.concatenate([item] * 16, axis=0)
                store_turned(faces, f * 4 + yb, tile.T)
        start = jnp.broadcast_to(upper[:, 0:1], (8, 128))
        start = jnp.where(rows == lanes % 4, start, 0.0)
        start = jnp.broadcast_to(jnp.sum(start, axis=0, keepdims=True), (8, 128))
        leak.append(start * 0.5 * rate_y)

    rate_x = choose(rows % 4, [table(s, 0) for s in range(4)])
    wind_x = choose(rows % 4, [table(s, 3) for s in range(4)])
    scales = [choose(rows // 4, [scale[2 * zp], scale[2 * zp + 1]]) for zp in range(4)]
    groups = lanes // 32
    for g in range(4):
        vectors[g] = rate_x * choose(groups, [scales[(p - g) % 4] for p in range(4)])
    vectors[4] = wind_x
    for f in range(2):
        factor = choose(rows % 4, [table(s, 6 + f) for s in range(4)])
        for zp in range(4):
            vectors[5 + f * 4 + zp] = factor * choose(rows // 4, [emit[2 * zp], emit[2 * zp + 1]])
    for v in range(8):
        line = [surf_rows[pl.ds(v * 4 + x, 1), :] for x in range(4)]
        steps = [(line[x] + line[x + 1]) * 0.5 for x in range(3)]
        for zp in range(4):
            j = v * 4 + zp
            rate = rate_x * scales[zp]
            one_inv, one_fill, one_upper, two_inv, two_fill, two_slack, two_next = inner_coefs(
                *(rate * step for step in steps), wind_x
            )
            for n, item in enumerate(
                (one_inv, one_fill, one_upper, two_inv, two_fill * two_inv, two_next * two_inv)
            ):
                kept[j, pl.ds(n * 8, 8), :] = item
    lines = [surf_rows[pl.ds(x, 8, stride=4), :] for x in range(4)]
    lines = [
        [pltpu.roll(item, 32 * d, axis=1) if d else item for d in range(4)] for item in lines
    ]
    strips = [pick(groups, [lines[x][(x - g) % 4] for x in range(4)]) for g in range(4)]
    for g in range(4):
        for v in range(8):
            sent[pl.ds((v * 4 + g) * SEND + 16, 1), :] = strips[g][v : v + 1, :]
    width = window.shape[0]
    start = jnp.min(cells[...] % width, axis=0, keepdims=True)
    place = lax.broadcasted_iota(jnp.int32, (width, 128), 0)
    window[...] = jnp.where((place >= start) & (place < start + 4), 1.0, 0.0).astype(jnp.bfloat16)

    solve_levels(cot, surf, scale, table, levels, hold_a, hold_c, low, halves)
    for v in range(8):
        store_turned(turned, v, levels[pl.ds(v * 128, 128), :].T)
    solve_rows(turned, faces, leak, rate_y, wind_y, hold_a, hold_b, hold_c, rows)
    for v in range(8):
        levels[pl.ds(v * 128, 128), :] = load_turned(turned, v).T

    for v in range(8):
        line = [surf_rows[pl.ds(v * 4 + x, 1), :] for x in range(4)]
        steps = [(line[x] + line[x + 1]) * 0.5 for x in range(3)]
        firsts, lasts = [], []
        for zp in range(4):
            j = v * 4 + zp
            rate = rate_x * scales[zp]
            e01, e12, e23 = (rate * step for step in steps)
            rhs = [levels[pl.ds(v * 128 + zp * 32 + x, 8, stride=4), :] for x in range(4)]
            one = rhs[1] * kept[j, pl.ds(0, 8), :]
            two = (rhs[2] + e12 * one) * kept[j, pl.ds(24, 8), :]
            one_upper = kept[j, pl.ds(16, 8), :]
            firsts.append(rhs[0] + (e01 + wind_x) * (one + one_upper * two))
            lasts.append(rhs[3] + e23 * two)
            kept[j, pl.ds(0, 8), :] = one
            kept[j, pl.ds(24, 8), :] = two
        for offset, items in ((0, firsts), (8, lasts)):
            for g, item in enumerate(to_strips(items, groups)):
                sent[pl.ds((v * 4 + g) * SEND + offset, 8), :] = item


def middle_kernel(vectors, got, ends, spread):
    groups = lane() // 32
    slabs = ends.shape[0]
    strip = lax.axis_index("tile") % 4
    lasts = []
    spread[pl.ds(5 * slabs, 8), :] = jnp.zeros((8, 128), F32)
    for q in range(slabs // 8):
        shared = got[pl.ds(q * 8 * SEND + 16, 8, stride=SEND), :]
        turned = [pltpu.roll(shared, 32 * d, axis=1) if d else shared for d in range(4)]
        line = [pick(groups, [turned[(p - x) % 4] for p in range(4)]) for x in range(4)]
        for x in range(3):
            spread[pl.ds(x * slabs + q * 8, 8), :] = (line[x] + line[x + 1]) * 0.5
        spread[pl.ds(4 * slabs + q * 8, 8), :] = line[0]
        lasts.append(line[3])
    for q in range(slabs // 8):
        onward = spread[pl.ds(4 * slabs + q * 8 + 1, 8), :]
        spread[pl.ds(3 * slabs + q * 8, 8), :] = (lasts[q] + onward) * 0.5
    rate = vectors[strip]
    wind = vectors[4]
    below, above, slack, rhs = [], [], [], []
    outer = rate * (spread[pl.ds(4 * slabs, 1), :] * 0.5)
    for k in range(slabs):
        e01, e12, e23 = (rate * spread[pl.ds(x * slabs + k, 1), :] for x in range(3))
        one_inv, one_fill, one_upper, two_inv, two_fill, two_slack, two_next = inner_coefs(
            e01, e12, e23, wind
        )
        two_slack = two_slack * two_inv
        q0 = e01 + wind
        own = 1.0 + q0 * (one_inv + one_upper * two_slack)
        if k == 0:
            own = own + outer
            below.append(None)
        else:
            below.append(outer)
        above.append(q0 * (one_upper * (two_next * two_inv)))
        slack.append(own)
        rhs.append(got[pl.ds(k * SEND, 8), :])
        outer = rate * spread[pl.ds(3 * slabs + k, 1), :]
        own = 1.0 + e23 * two_slack
        below.append(e23 * (two_fill * two_inv))
        if k < slabs - 1:
            above.append(outer + wind)
        else:
            own = own + (outer + wind)
            above.append(None)
        slack.append(own)
        rhs.append(got[pl.ds(k * SEND + 8, 8), :])

    def total(i):
        out = slack[i]
        if below[i] is not None:
            out = out + below[i]
        if above[i] is not None:
            out = out + above[i]
        return out

    count = 2 * slabs
    alive = list(range(count))
    removed = []
    while len(alive) > 1:
        gone = alive[1::2]
        stay = alive[0::2]
        normal = {}
        for i in gone:
            inv = inverse(total(i))
            normal[i] = (
                below[i] * inv,
                None if above[i] is None else above[i] * inv,
                slack[i] * inv,
                rhs[i] * inv,
            )
        for n, i in enumerate(stay):
            new_below = new_above = None
            new_slack, new_rhs = slack[i], rhs[i]
            if n > 0:
                nb, na, ns, nr = normal[gone[n - 1]]
                new_slack = new_slack + below[i] * ns
                new_rhs = new_rhs + below[i] * nr
                new_below = below[i] * nb
            if n < len(gone):
                nb, na, ns, nr = normal[gone[n]]
                new_slack = new_slack + above[i] * ns
                new_rhs = new_rhs + above[i] * nr
                new_above = None if na is None else above[i] * na
            below[i], above[i], slack[i], rhs[i] = new_below, new_above, new_slack, new_rhs
        removed.append((alive, normal))
        alive = stay
    solved = {0: rhs[0] * inverse(slack[0])}
    for order, normal in reversed(removed):
        for n in range(1, len(order), 2):
            nb, na, ns, nr = normal[order[n]]
            item = nr + nb * solved[order[n - 1]]
            if na is not None:
                item = item + na * solved[order[n + 1]]
            solved[order[n]] = item
    for k in range(slabs):
        ends[k, pl.ds(0, 8), :] = solved[2 * k]
        ends[k, pl.ds(8, 8), :] = solved[2 * k + 1]


def inner_rows(ends, kept, j):
    first = ends[j, pl.ds(0, 8), :]
    last = ends[j, pl.ds(8, 8), :]
    a1, b1, c1, a2, b2, c2 = (kept[j, pl.ds(n * 8, 8), :] for n in range(6))
    two = a2 + b2 * first + c2 * last
    one = a1 + b1 * first + c1 * two
    return first, one, two, last


def sums_kernel(vectors, window, ends, kept, grad, sorted_ends):
    parts = []
    groups = lane() // 32
    for v in range(8):
        for row in (0, 8):
            items = from_strips([ends[v * 4 + g, pl.ds(row, 8), :] for g in range(4)], groups)
            for zp, item in enumerate(items):
                sorted_ends[v * 4 + zp, pl.ds(row, 8), :] = item
    for v in range(8):
        total = None
        for zp in range(4):
            first, one, two, last = inner_rows(sorted_ends, kept, v * 4 + zp)
            item = vectors[5 + (v // 4) * 4 + zp] * ((first + one) + (two + last))
            total = item if total is None else total + item
        parts.append(jnp.sum(total, axis=0, keepdims=True))
    sums = [jnp.concatenate(parts[f * 4 : f * 4 + 4], axis=1) for f in range(2)]
    pieces = []
    for _ in range(3):
        piece = [item.astype(jnp.bfloat16).astype(F32) for item in sums]
        sums = [item - cut for item, cut in zip(sums, piece)]
        pieces += piece
    pieces = jnp.concatenate(pieces + [jnp.zeros((2, sums[0].shape[1]), F32)], axis=0)
    picked = jnp.dot(pieces.astype(jnp.bfloat16), window[...], preferred_element_type=F32)
    grad[...] = (picked[0:2, :] + picked[2:4, :]) + picked[4:6, :]


def state_kernel(ends, kept, state, lines):
    low = sublane() < 4
    for f in range(2):
        for yb in range(4):
            v = f * 4 + yb
            for zp in range(4):
                for x, item in enumerate(inner_rows(ends, kept, v * 4 + zp)):
                    lines[pl.ds(v * 128 + zp * 32 + x, 8, stride=4), :] = item
        for z in range(8):
            for sp in range(2):
                for h in range(2):
                    base = (f * 4 + 2 * h) * 128 + z * 16 + sp * 8
                    even, odd = pair_halves(
                        lines[pl.ds(base, 8), :], lines[pl.ds(base + 128, 8), :], low
                    )
                    for s, item in ((2 * sp, even), (2 * sp + 1, odd)):
                        state[pl.ds(s * 256 + f * 128 + z * 16 + h * 8, 8), :] = item


def rows_of(block):
    s, f, z, x, y = block.shape
    return block.reshape(s, f, z, x, y // 128, 128).transpose(0, 1, 2, 4, 3, 5).reshape(-1, 128)


def on_device(
    cotangent, scenario_ids, weather, landuse, class_diff, level_scale, emit_profile, building_cells
):
    hbm = pl.BlockSpec(memory_space=pltpu.HBM)
    vmem = pl.BlockSpec(memory_space=pltpu.VMEM)
    params = pltpu.CompilerParams(vmem_limit_bytes=32 * 1024 * 1024)
    slabs = lax.axis_size("tile")
    groups = lax.axis_size("scen")
    width = cotangent.shape[4]
    cells = building_cells.T
    classes = landuse.reshape(4, 4, 128).transpose(1, 0, 2).reshape(16, 128)
    small = (scenario_ids, weather.T, class_diff, level_scale, emit_profile)
    operands = (*small, classes, cells, rows_of(cotangent))
    sent, kept, vectors, window = pl.pallas_call(
        first_kernel,
        out_shape=(
            jax.ShapeDtypeStruct((slabs * SEND, 128), F32),
            jax.ShapeDtypeStruct((slabs, 48, 128), F32),
            jax.ShapeDtypeStruct((13, 8, 128), F32),
            jax.ShapeDtypeStruct((width, cells.shape[1]), jnp.bfloat16),
        ),
        in_specs=[hbm] * 8,
        out_specs=(vmem,) * 4,
        scratch_shapes=[pltpu.SMEM(item.shape, item.dtype) for item in small]
        + [pltpu.VMEM(item.shape, item.dtype) for item in (classes, cells)]
        + [pltpu.VMEM((1024, 128), F32)] * 2
        + [pltpu.VMEM((64 * PITCH, 128), F32)] * 2
        + [pltpu.VMEM((1024, 128), F32)] * 3
        + [pltpu.VMEM((32, 128), F32), pltpu.SemaphoreType.DMA((9,))],
        compiler_params=params,
    )(*(pltpu.with_memory_space_constraint(item, pltpu.HBM) for item in operands))
    got = lax.all_to_all(sent.reshape(slabs, SEND, 1, 128), "tile", 0, 0).reshape(slabs * SEND, 128)
    ends = pl.pallas_call(
        middle_kernel,
        out_shape=jax.ShapeDtypeStruct((slabs, 16, 128), F32),
        in_specs=[vmem] * 2,
        out_specs=vmem,
        scratch_shapes=[pltpu.VMEM((5 * slabs + 8, 128), F32)],
        compiler_params=params,
    )(vectors, got)
    ends = lax.all_to_all(ends, "tile", 0, 0)
    grad, ends = pl.pallas_call(
        sums_kernel,
        out_shape=(
            jax.ShapeDtypeStruct((2, cells.shape[1]), F32),
            jax.ShapeDtypeStruct((slabs, 16, 128), F32),
        ),
        in_specs=[vmem] * 4,
        out_specs=(vmem, vmem),
        compiler_params=params,
    )(vectors, window, ends, kept)
    state = pl.pallas_call(
        state_kernel,
        out_shape=jax.ShapeDtypeStruct((1024, 128), F32),
        in_specs=[vmem] * 2,
        out_specs=vmem,
        scratch_shapes=[pltpu.VMEM((1024, 128), F32)],
        compiler_params=params,
    )(ends, kept)
    grad = grad + lax.ppermute(grad, "scen", [(i, i ^ 1) for i in range(groups)])
    shifted = [
        lax.ppermute(grad, "scen", [(i, i ^ step) for i in range(groups)]) for step in (2, 6, 4)
    ]
    grad = (grad + shifted[0]) + (shifted[1] + shifted[2])
    state = state.reshape(4, 2, 8, 4, 4, 128).transpose(0, 1, 2, 4, 3, 5).reshape(cotangent.shape)
    return (state, grad)


def solution(mesh):
    placed = (
        P("scen", None, None, "tile", None),
        P("scen"),
        P(),
        P("tile", None),
        P(),
        P(),
        P(),
        P("tile", None),
    )
    return jax.shard_map(
        on_device,
        mesh=mesh,
        in_specs=placed,
        out_specs=(P("scen", None, None, "tile", None), P(None, "tile")),
        check_vma=False,
    )
```

```python
import jax
import jax.numpy as jnp
from jax import lax
from jax.experimental import pallas as pl
from jax.experimental.pallas import tpu as pltpu
from jax.sharding import PartitionSpec as P

F32 = jnp.float32
SEND = 17


def inverse(value):
    return pltpu.reciprocal(value, approx=True)


def sublane():
    return lax.broadcasted_iota(jnp.int32, (8, 128), 0)


def lane():
    return lax.broadcasted_iota(jnp.int32, (8, 128), 1)


def choose(index, values):
    out = jnp.full((8, 128), values[-1], F32)
    for at in range(len(values) - 2, -1, -1):
        out = jnp.where(index == at, values[at], out)
    return out


def surface(classes, class_diff, field):
    out = jnp.zeros((8, 128), F32)
    for mark in range(class_diff.shape[1]):
        out = jnp.where(classes == mark, class_diff[field, mark], out)
    return out


def swap_halves(value):
    return pltpu.roll(value, 4, axis=0)


def pair_halves(first, second, low):
    return (
        jnp.where(low, first, swap_halves(second)),
        jnp.where(low, swap_halves(first), second),
    )


def pick(groups, items):
    out = items[3]
    for at in range(2, -1, -1):
        out = jnp.where(groups == at, items[at], out)
    return out


def to_strips(items, groups):
    turned = [pltpu.roll(item, 32 * m, axis=1) if m else item for m, item in enumerate(items)]
    return [pick(groups, [turned[(p - g) % 4] for p in range(4)]) for g in range(4)]


def from_strips(strips, groups):
    items = [pick(groups, [strips[(p - m) % 4] for p in range(4)]) for m in range(4)]
    return [pltpu.roll(item, 128 - 32 * m, axis=1) if m else item for m, item in enumerate(items)]


def solve_levels(cot, surf, scale, table, out, hold_a, hold_c, low, arrivals):
    half = [(scale[z] + scale[z + 1]) * 0.5 for z in range(7)]
    for pair in range(2):
        arrivals[pair].wait()
        chains = [(s, f, h) for s in (2 * pair, 2 * pair + 1) for f in range(2) for h in range(2)]
        rated = [surf[f][h] * table(s, 2) for s, f, h in chains]
        winds = [table(s, 5) for s, f, h in chains]
        values = [None] * 8
        slacks = [None] * 8
        faces = [None] * 8
        for z in range(8):
            for n, (s, f, h) in enumerate(chains):
                rhs = cot[pl.ds(s * 256 + f * 128 + z * 16 + h * 8, 8), :]
                if z == 0:
                    slack = 1.0 + rated[n] * (scale[0] * 0.5)
                else:
                    slack = 1.0 + faces[n] * slacks[n]
                    rhs = rhs + faces[n] * values[n]
                if z < 7:
                    face = rated[n] * half[z]
                    above = face + winds[n]
                    inv = inverse(above + slack)
                    values[n] = rhs * inv
                    slacks[n] = slack * inv
                    faces[n] = face
                    hold_a[pl.ds((z * 8 + n) * 8, 8), :] = values[n]
                    hold_c[pl.ds((z * 8 + n) * 8, 8), :] = above * inv
                else:
                    slack = slack + (rated[n] * (scale[7] * 0.5) + winds[n])
                    values[n] = rhs * inverse(slack)
        for z in range(7, -1, -1):
            if z < 7:
                for n in range(8):
                    at = pl.ds((z * 8 + n) * 8, 8)
                    values[n] = hold_a[at, :] + hold_c[at, :] * values[n]
            for f in range(2):
                for h in range(2):
                    n = f * 2 + h
                    even, odd = pair_halves(values[n], values[n + 4], low)
                    for yb, item in ((2 * h, even), (2 * h + 1, odd)):
                        out[pl.ds((f * 4 + yb) * 128 + z * 16 + pair * 8, 8), :] = item


def from_before(items, rows, distance):
    turned = [pltpu.roll(item, distance, axis=0) for item in items]
    return [
        turned[v] if v % 4 == 0 else jnp.where(rows < distance, turned[v - 1], turned[v])
        for v in range(8)
    ]


def from_after(items, rows, distance):
    turned = [pltpu.roll(item, 8 - distance, axis=0) for item in items]
    return [
        turned[v] if v % 4 == 3 else jnp.where(rows >= 8 - distance, turned[v + 1], turned[v])
        for v in range(8)
    ]


def solve_chunks(below, above, slack, rhs, rows):
    everyone = range(8)
    for distance in (1, 2, 4, 8, 16):
        inv = [inverse(below[v] + above[v] + slack[v]) for v in everyone]
        nb = [below[v] * inv[v] for v in everyone]
        na = [above[v] * inv[v] for v in everyone]
        ns = [slack[v] * inv[v] for v in everyone]
        nr = [rhs[v] * inv[v] for v in everyone]
        new_slack = list(slack)
        new_rhs = list(rhs)
        if distance < 8:
            pb, ps, pr = (from_before(item, rows, distance) for item in (nb, ns, nr))
            qa, qs, qr = (from_after(item, rows, distance) for item in (na, ns, nr))
            has_before = has_after = [True] * 8
        else:
            jump = distance // 8
            has_before = [v % 4 >= jump for v in everyone]
            has_after = [v % 4 < 4 - jump for v in everyone]
            pb, ps, pr = (
                [item[v - jump] if has_before[v] else None for v in everyone]
                for item in (nb, ns, nr)
            )
            qa, qs, qr = (
                [item[v + jump] if has_after[v] else None for v in everyone]
                for item in (na, ns, nr)
            )
        zero = jnp.zeros((8, 128), F32)
        new_below = [zero] * 8
        new_above = [zero] * 8
        for v in everyone:
            if has_before[v]:
                new_slack[v] = new_slack[v] + below[v] * ps[v]
                new_rhs[v] = new_rhs[v] + below[v] * pr[v]
                new_below[v] = below[v] * pb[v]
            if has_after[v]:
                new_slack[v] = new_slack[v] + above[v] * qs[v]
                new_rhs[v] = new_rhs[v] + above[v] * qr[v]
                new_above[v] = above[v] * qa[v]
        below, above, slack, rhs = new_below, new_above, new_slack, new_rhs
    return [rhs[v] * inverse(slack[v]) for v in everyone]


PITCH = 17


def store_turned(target, v, block):
    for n in range(16):
        target[pl.ds(v * 8 * PITCH + n // 2 * PITCH + n % 2 * 8, 8), :] = block[8 * n : 8 * n + 8, :]


def load_turned(source, v):
    return jnp.concatenate(
        [source[pl.ds(v * 8 * PITCH + n // 2 * PITCH + n % 2 * 8, 8), :] for n in range(16)], axis=0
    )


def solve_rows(turned, faces, leak, rate, wind, hold_a, hold_b, hold_c, rows):
    everyone = range(8)
    depth = 16

    def at(v, i):
        return pl.ds(v * 8 * PITCH + i, 8, stride=PITCH)

    def keep(i, v):
        return pl.ds((i * 8 + v) * 8, 8)

    ends = [faces[at(v, depth - 1), :] * rate for v in everyone]
    before = from_before(ends, rows, 1)
    last = ends
    value = [None] * 8
    fill = [None] * 8
    slack = [None] * 8
    for i in range(depth):
        for v in everyone:
            rhs = turned[at(v, i), :]
            face = last[v] if i == depth - 1 else faces[at(v, i), :] * rate
            next_coef = face + wind
            if i == 0:
                link = before[v]
                own = jnp.ones((8, 128), F32)
                if v % 4 == 0:
                    own = jnp.where(rows == 0, 1.0 + leak[v // 4], own)
                    link = jnp.where(rows == 0, 0.0, link)
            else:
                link = before[v] * fill[v]
                own = 1.0 + before[v] * slack[v]
                rhs = rhs + before[v] * value[v]
            if i == depth - 1:
                if v % 4 == 3:
                    own = jnp.where(rows == 7, own + next_coef, own)
                    next_coef = jnp.where(rows == 7, 0.0, next_coef)
                value[v], fill[v], slack[v] = rhs, link, own
                before[v] = next_coef
                continue
            inv = inverse(next_coef + link + own)
            value[v] = rhs * inv
            fill[v] = link * inv
            slack[v] = own * inv
            upper = next_coef * inv
            hold_a[keep(i, v), :] = value[v]
            hold_b[keep(i, v), :] = fill[v]
            hold_c[keep(i, v), :] = upper
            before[v] = face
            if i == 0:
                if v == 0:
                    first_value, first_fill, first_slack, first_next = ([None] * 8 for _ in range(4))
                first_value[v], first_fill[v], first_slack[v], first_next[v] = (
                    value[v],
                    fill[v],
                    slack[v],
                    upper,
                )
            else:
                carry = first_next[v]
                first_value[v] = first_value[v] + carry * value[v]
                first_slack[v] = first_slack[v] + carry * slack[v]
                first_next[v] = carry * upper
    next_value = from_after(first_value, rows, 1)
    next_slack = from_after(first_slack, rows, 1)
    next_next = from_after(first_next, rows, 1)
    above = [before[v] * next_next[v] for v in everyone]
    slack = [slack[v] + before[v] * next_slack[v] for v in everyone]
    rhs = [value[v] + before[v] * next_value[v] for v in everyone]
    current = solve_chunks(fill, above, slack, rhs, rows)
    previous = from_before(current, rows, 1)
    for v in everyone:
        turned[at(v, depth - 1), :] = current[v]
    for i in range(depth - 2, -1, -1):
        for v in everyone:
            item = hold_a[keep(i, v), :] + hold_b[keep(i, v), :] * previous[v]
            current[v] = item + hold_c[keep(i, v), :] * current[v]
            turned[at(v, i), :] = current[v]


def inner_coefs(low_face, mid_face, high_face, wind):
    one_next = mid_face + wind
    one_inv = inverse(low_face + one_next + 1.0)
    one_fill = low_face * one_inv
    one_upper = one_next * one_inv
    two_next = high_face + wind
    two_fill = mid_face * one_fill
    two_slack = 1.0 + mid_face * one_inv
    two_inv = inverse(two_next + two_fill + two_slack)
    return one_inv, one_fill, one_upper, two_inv, two_fill, two_slack, two_next


def first_kernel(
    ids_in, weather_in, class_diff_in, scale_in, emit_in, landuse_in, cells_in, cot_in,
    sent, kept, vectors, window,
    ids, weather, class_diff, scale, emit, landuse, cells, cot,
    levels, turned, faces, hold_a, hold_b, hold_c, surf_rows, done,
):
    small = [
        pltpu.make_async_copy(source, target, done.at[n])
        for n, (source, target) in enumerate(
            (
                (ids_in, ids),
                (weather_in, weather),
                (class_diff_in, class_diff),
                (scale_in, scale),
                (emit_in, emit),
                (landuse_in, landuse),
                (cells_in, cells),
            )
        )
    ]
    halves = [
        pltpu.make_async_copy(
            cot_in.at[pl.ds(n * 512, 512), :], cot.at[pl.ds(n * 512, 512), :], done.at[7 + n]
        )
        for n in range(2)
    ]
    for copy in small + halves:
        copy.start()
    for copy in small:
        copy.wait()
    rows = sublane()
    lanes = lane()
    low = rows < 4

    def table(s, column):
        return weather[column, ids[s]]

    classes = [landuse[pl.ds(0, 8), :], landuse[pl.ds(8, 8), :]]
    surf = [[surface(item, class_diff, f) for item in classes] for f in range(2)]
    rate_y = choose((lanes // 4) % 4, [table(s, 1) for s in range(4)])
    wind_y = choose((lanes // 4) % 4, [table(s, 4) for s in range(4)])
    rate_y = rate_y * choose(lanes // 16, [scale[z] for z in range(8)])
    leak = []
    for f in range(2):
        upper, lower = surf[f]
        surf_rows[pl.ds(f * 16, 8), :] = upper
        surf_rows[pl.ds(f * 16 + 8, 8), :] = lower
        shifted = [pltpu.roll(item, 127, axis=1) for item in (upper, lower)]
        swapped = [swap_halves(item) for item in shifted]
        onward = [
            jnp.where(low, swapped[0], swapped[1]),
            jnp.where(low, swapped[1], 0.0),
        ]
        for h in range(2):
            right = jnp.where(lanes == 127, onward[h], shifted[h])
            face = (surf[f][h] + right) * 0.5
            other = swap_halves(face)
            for yb, item in (
                (2 * h, jnp.where(low, face, other)),
                (2 * h + 1, jnp.where(low, other, face)),
            ):
                tile = jnp.concatenate([item] * 16, axis=0)
                store_turned(faces, f * 4 + yb, tile.T)
        start = jnp.broadcast_to(upper[:, 0:1], (8, 128))
        start = jnp.where(rows == lanes % 4, start, 0.0)
        start = jnp.broadcast_to(jnp.sum(start, axis=0, keepdims=True), (8, 128))
        leak.append(start * 0.5 * rate_y)

    rate_x = choose(rows % 4, [table(s, 0) for s in range(4)])
    wind_x = choose(rows % 4, [table(s, 3) for s in range(4)])
    scales = [choose(rows // 4, [scale[2 * zp], scale[2 * zp + 1]]) for zp in range(4)]
    groups = lanes // 32
    for g in range(4):
        vectors[g] = rate_x * choose(groups, [scales[(p - g) % 4] for p in range(4)])
    vectors[4] = wind_x
    for f in range(2):
        factor = choose(rows % 4, [table(s, 6 + f) for s in range(4)])
        for zp in range(4):
            vectors[5 + f * 4 + zp] = factor * choose(rows // 4, [emit[2 * zp], emit[2 * zp + 1]])
    for v in range(8):
        line = [surf_rows[pl.ds(v * 4 + x, 1), :] for x in range(4)]
        steps = [(line[x] + line[x + 1]) * 0.5 for x in range(3)]
        for zp in range(4):
            j = v * 4 + zp
            rate = rate_x * scales[zp]
            one_inv, one_fill, one_upper, two_inv, two_fill, two_slack, two_next = inner_coefs(
                *(rate * step for step in steps), wind_x
            )
            for n, item in enumerate(
                (one_inv, one_fill, one_upper, two_inv, two_fill * two_inv, two_next * two_inv)
            ):
                kept[j, pl.ds(n * 8, 8), :] = item
    lines = [surf_rows[pl.ds(x, 8, stride=4), :] for x in range(4)]
    lines = [
        [pltpu.roll(item, 32 * d, axis=1) if d else item for d in range(4)] for item in lines
    ]
    strips = [pick(groups, [lines[x][(x - g) % 4] for x in range(4)]) for g in range(4)]
    for g in range(4):
        for v in range(8):
            sent[pl.ds((v * 4 + g) * SEND + 16, 1), :] = strips[g][v : v + 1, :]
    width = window.shape[0]
    start = jnp.min(cells[...] % width, axis=0, keepdims=True)
    place = lax.broadcasted_iota(jnp.int32, (width, 128), 0)
    window[...] = jnp.where((place >= start) & (place < start + 4), 1.0, 0.0).astype(jnp.bfloat16)

    solve_levels(cot, surf, scale, table, levels, hold_a, hold_c, low, halves)
    for v in range(8):
        store_turned(turned, v, levels[pl.ds(v * 128, 128), :].T)
    solve_rows(turned, faces, leak, rate_y, wind_y, hold_a, hold_b, hold_c, rows)
    for v in range(8):
        levels[pl.ds(v * 128, 128), :] = load_turned(turned, v).T

    for v in range(8):
        line = [surf_rows[pl.ds(v * 4 + x, 1), :] for x in range(4)]
        steps = [(line[x] + line[x + 1]) * 0.5 for x in range(3)]
        firsts, lasts = [], []
        for zp in range(4):
            j = v * 4 + zp
            rate = rate_x * scales[zp]
            e01, e12, e23 = (rate * step for step in steps)
            rhs = [levels[pl.ds(v * 128 + zp * 32 + x, 8, stride=4), :] for x in range(4)]
            one = rhs[1] * kept[j, pl.ds(0, 8), :]
            two = (rhs[2] + e12 * one) * kept[j, pl.ds(24, 8), :]
            one_upper = kept[j, pl.ds(16, 8), :]
            firsts.append(rhs[0] + (e01 + wind_x) * (one + one_upper * two))
            lasts.append(rhs[3] + e23 * two)
            kept[j, pl.ds(0, 8), :] = one
            kept[j, pl.ds(24, 8), :] = two
        for offset, items in ((0, firsts), (8, lasts)):
            for g, item in enumerate(to_strips(items, groups)):
                sent[pl.ds((v * 4 + g) * SEND + offset, 8), :] = item


def middle_kernel(vectors, got, ends, spread):
    groups = lane() // 32
    slabs = ends.shape[0]
    strip = lax.axis_index("tile") % 4
    for q in range(slabs // 8):
        shared = got[pl.ds(q * 8 * SEND + 16, 8, stride=SEND), :]
        turned = [pltpu.roll(shared, 32 * d, axis=1) if d else shared for d in range(4)]
        for x in range(4):
            spread[pl.ds(x * slabs + q * 8, 8), :] = pick(
                groups, [turned[(p - x) % 4] for p in range(4)]
            )
    rate = vectors[strip]
    wind = vectors[4]
    below, above, slack, rhs = [], [], [], []
    line = None
    outer = None
    for k in range(slabs):
        line = [spread[pl.ds(x * slabs + k, 1), :] for x in range(4)]
        if k == 0:
            outer = rate * (line[0] * 0.5)
        e01, e12, e23 = (rate * ((line[x] + line[x + 1]) * 0.5) for x in range(3))
        one_inv, one_fill, one_upper, two_inv, two_fill, two_slack, two_next = inner_coefs(
            e01, e12, e23, wind
        )
        two_slack = two_slack * two_inv
        q0 = e01 + wind
        own = 1.0 + q0 * (one_inv + one_upper * two_slack)
        if k == 0:
            own = own + outer
            below.append(None)
        else:
            below.append(outer)
        above.append(q0 * (one_upper * (two_next * two_inv)))
        slack.append(own)
        rhs.append(got[pl.ds(k * SEND, 8), :])
        if k < slabs - 1:
            outer = rate * ((line[3] + spread[pl.ds(k + 1, 1), :]) * 0.5)
        else:
            outer = rate * (line[3] * 0.5)
        own = 1.0 + e23 * two_slack
        below.append(e23 * (two_fill * two_inv))
        if k < slabs - 1:
            above.append(outer + wind)
        else:
            own = own + (outer + wind)
            above.append(None)
        slack.append(own)
        rhs.append(got[pl.ds(k * SEND + 8, 8), :])

    def total(i):
        out = slack[i]
        if below[i] is not None:
            out = out + below[i]
        if above[i] is not None:
            out = out + above[i]
        return out

    count = 2 * slabs
    alive = list(range(count))
    removed = []
    while len(alive) > 1:
        gone = alive[1::2]
        stay = alive[0::2]
        normal = {}
        for i in gone:
            inv = inverse(total(i))
            normal[i] = (
                below[i] * inv,
                None if above[i] is None else above[i] * inv,
                slack[i] * inv,
                rhs[i] * inv,
            )
        for n, i in enumerate(stay):
            new_below = new_above = None
            new_slack, new_rhs = slack[i], rhs[i]
            if n > 0:
                nb, na, ns, nr = normal[gone[n - 1]]
                new_slack = new_slack + below[i] * ns
                new_rhs = new_rhs + below[i] * nr
                new_below = below[i] * nb
            if n < len(gone):
                nb, na, ns, nr = normal[gone[n]]
                new_slack = new_slack + above[i] * ns
                new_rhs = new_rhs + above[i] * nr
                new_above = None if na is None else above[i] * na
            below[i], above[i], slack[i], rhs[i] = new_below, new_above, new_slack, new_rhs
        removed.append((alive, normal))
        alive = stay
    solved = {0: rhs[0] * inverse(slack[0])}
    for order, normal in reversed(removed):
        for n in range(1, len(order), 2):
            nb, na, ns, nr = normal[order[n]]
            item = nr + nb * solved[order[n - 1]]
            if na is not None:
                item = item + na * solved[order[n + 1]]
            solved[order[n]] = item
    for k in range(slabs):
        ends[k, pl.ds(0, 8), :] = solved[2 * k]
        ends[k, pl.ds(8, 8), :] = solved[2 * k + 1]


def inner_rows(ends, kept, j):
    first = ends[j, pl.ds(0, 8), :]
    last = ends[j, pl.ds(8, 8), :]
    a1, b1, c1, a2, b2, c2 = (kept[j, pl.ds(n * 8, 8), :] for n in range(6))
    two = a2 + b2 * first + c2 * last
    one = a1 + b1 * first + c1 * two
    return first, one, two, last


def sums_kernel(vectors, window, ends, kept, grad, sorted_ends):
    parts = []
    groups = lane() // 32
    for v in range(8):
        for row in (0, 8):
            items = from_strips([ends[v * 4 + g, pl.ds(row, 8), :] for g in range(4)], groups)
            for zp, item in enumerate(items):
                sorted_ends[v * 4 + zp, pl.ds(row, 8), :] = item
    for v in range(8):
        total = None
        for zp in range(4):
            first, one, two, last = inner_rows(sorted_ends, kept, v * 4 + zp)
            item = vectors[5 + (v // 4) * 4 + zp] * ((first + one) + (two + last))
            total = item if total is None else total + item
        parts.append(jnp.sum(total, axis=0, keepdims=True))
    sums = [jnp.concatenate(parts[f * 4 : f * 4 + 4], axis=1) for f in range(2)]
    pieces = []
    for _ in range(3):
        piece = [item.astype(jnp.bfloat16).astype(F32) for item in sums]
        sums = [item - cut for item, cut in zip(sums, piece)]
        pieces += piece
    pieces = jnp.concatenate(pieces + [jnp.zeros((2, sums[0].shape[1]), F32)], axis=0)
    picked = jnp.dot(pieces.astype(jnp.bfloat16), window[...], preferred_element_type=F32)
    grad[...] = (picked[0:2, :] + picked[2:4, :]) + picked[4:6, :]


def state_kernel(ends, kept, state, lines):
    low = sublane() < 4
    for f in range(2):
        for yb in range(4):
            v = f * 4 + yb
            for zp in range(4):
                for x, item in enumerate(inner_rows(ends, kept, v * 4 + zp)):
                    lines[pl.ds(v * 128 + zp * 32 + x, 8, stride=4), :] = item
        for z in range(8):
            for sp in range(2):
                for h in range(2):
                    base = (f * 4 + 2 * h) * 128 + z * 16 + sp * 8
                    even, odd = pair_halves(
                        lines[pl.ds(base, 8), :], lines[pl.ds(base + 128, 8), :], low
                    )
                    for s, item in ((2 * sp, even), (2 * sp + 1, odd)):
                        state[pl.ds(s * 256 + f * 128 + z * 16 + h * 8, 8), :] = item


def rows_of(block):
    s, f, z, x, y = block.shape
    return block.reshape(s, f, z, x, y // 128, 128).transpose(0, 1, 2, 4, 3, 5).reshape(-1, 128)


def on_device(
    cotangent, scenario_ids, weather, landuse, class_diff, level_scale, emit_profile, building_cells
):
    hbm = pl.BlockSpec(memory_space=pltpu.HBM)
    vmem = pl.BlockSpec(memory_space=pltpu.VMEM)
    params = pltpu.CompilerParams(vmem_limit_bytes=32 * 1024 * 1024)
    slabs = lax.axis_size("tile")
    groups = lax.axis_size("scen")
    width = cotangent.shape[4]
    cells = building_cells.T
    classes = landuse.reshape(4, 4, 128).transpose(1, 0, 2).reshape(16, 128)
    small = (scenario_ids, weather.T, class_diff, level_scale, emit_profile)
    operands = (*small, classes, cells, rows_of(cotangent))
    sent, kept, vectors, window = pl.pallas_call(
        first_kernel,
        out_shape=(
            jax.ShapeDtypeStruct((slabs * SEND, 128), F32),
            jax.ShapeDtypeStruct((slabs, 48, 128), F32),
            jax.ShapeDtypeStruct((13, 8, 128), F32),
            jax.ShapeDtypeStruct((width, cells.shape[1]), jnp.bfloat16),
        ),
        in_specs=[hbm] * 8,
        out_specs=(vmem,) * 4,
        scratch_shapes=[pltpu.SMEM(item.shape, item.dtype) for item in small]
        + [pltpu.VMEM(item.shape, item.dtype) for item in (classes, cells)]
        + [pltpu.VMEM((1024, 128), F32)] * 2
        + [pltpu.VMEM((64 * PITCH, 128), F32)] * 2
        + [pltpu.VMEM((1024, 128), F32)] * 3
        + [pltpu.VMEM((32, 128), F32), pltpu.SemaphoreType.DMA((9,))],
        compiler_params=params,
    )(*(pltpu.with_memory_space_constraint(item, pltpu.HBM) for item in operands))
    got = lax.all_to_all(sent.reshape(slabs, SEND, 1, 128), "tile", 0, 0).reshape(slabs * SEND, 128)
    ends = pl.pallas_call(
        middle_kernel,
        out_shape=jax.ShapeDtypeStruct((slabs, 16, 128), F32),
        in_specs=[vmem] * 2,
        out_specs=vmem,
        scratch_shapes=[pltpu.VMEM((4 * slabs, 128), F32)],
        compiler_params=params,
    )(vectors, got)
    ends = lax.all_to_all(ends, "tile", 0, 0)
    grad, ends = pl.pallas_call(
        sums_kernel,
        out_shape=(
            jax.ShapeDtypeStruct((2, cells.shape[1]), F32),
            jax.ShapeDtypeStruct((slabs, 16, 128), F32),
        ),
        in_specs=[vmem] * 4,
        out_specs=(vmem, vmem),
        compiler_params=params,
    )(vectors, window, ends, kept)
    state = pl.pallas_call(
        state_kernel,
        out_shape=jax.ShapeDtypeStruct((1024, 128), F32),
        in_specs=[vmem] * 2,
        out_specs=vmem,
        scratch_shapes=[pltpu.VMEM((1024, 128), F32)],
        compiler_params=params,
    )(ends, kept)
    grad = grad + lax.ppermute(grad, "scen", [(i, i ^ 1) for i in range(groups)])
    shifted = [
        lax.ppermute(grad, "scen", [(i, i ^ step) for i in range(groups)]) for step in (6, 2, 4)
    ]
    grad = (grad + shifted[0]) + (shifted[1] + shifted[2])
    state = state.reshape(4, 2, 8, 4, 4, 128).transpose(0, 1, 2, 4, 3, 5).reshape(cotangent.shape)
    return (state, grad)


def solution(mesh):
    placed = (
        P("scen", None, None, "tile", None),
        P("scen"),
        P(),
        P("tile", None),
        P(),
        P(),
        P(),
        P("tile", None),
    )
    return jax.shard_map(
        on_device,
        mesh=mesh,
        in_specs=placed,
        out_specs=(P("scen", None, None, "tile", None), P(None, "tile")),
        check_vma=False,
    )
```
